32 devices in a mesh: dp: 8 (over z, x), seq: 4 (over y, core).
Axes of the slice: x: 2, y: 2, z: 4, core: 2. Of those that a mesh axis runs over, the one named last changes fastest.
Arguments:
- points: bfloat16 [8, 1024, 20], P('dp', 'seq'), may hold values from -4 to 4
- counts: int32 [8], P('dp'), may hold values from 5 to 20
- cotangent: bfloat16 [8, 1024, 256], P('dp', 'seq'), may hold values from -6 to 6
- weights: float32 [1585152], P('dp'), may hold values from -2 to 2
- momenta: float32 [1585152], P('dp'), may hold values from -320 to 320
- averages: float32 [1585152], P('dp'), may hold values from -2 to 2
Outputs:
- states: bfloat16 [8, 1024, 256], P('dp', 'seq')
- point_grad: float32 [8, 1024, 20], P('dp', 'seq')
- gradients: float32 [1585152], P('dp')
- weights_new: float32 [1585152], P('dp')
- momenta_new: float32 [1585152], P('dp')
- averages_new: float32 [1585152], P('dp')
The draws below stay inside these ranges and needn't reach their ends.
All inputs are finite; a program needn't handle non-finite values.
Results may differ from the reference program's by a relative error of at most 0.014.
Values may be sent and summed in bfloat16 or wider, within the bound.
A program may use at most 192 MiB of HBM per device.

```python
import math
import jax
import jax.numpy as jnp
from jax import lax

D = 256
HEADS = 8
FF = 1024
DIN = 20
LAYERS = 2
LOOPS = 2
LENGTH = 1024
PROMPTS = 8
PARAMS = 1585152


def segment_plan():
    plan = [(DIN * D, 'normal', DIN ** (-0.5)), (D, 'normal', 0.2)]
    for layer_index in range(LAYERS):
        plan = plan + [(D, 'gain', 0.3), (D, 'normal', 0.2), (D, 'gain', 0.3), (D, 'normal', 0.2), (3 * D * D, 'normal', D ** (-0.5)), (D * D, 'normal', 3.0 * D ** (-0.5)), (D * FF, 'normal', D ** (-0.5)), (FF, 'normal', 0.2), (FF * D, 'normal', FF ** (-0.5))]
    return plan


def flat_draw(key):
    drawn = []
    used_total = 0
    for segment, (amount, draw_kind, spread) in enumerate(segment_plan()):
        sub_key = jax.random.fold_in(key, segment)
        if draw_kind == 'gain':
            drawn.append(1.0 + jax.random.uniform(sub_key, (amount,), jnp.float32, -spread, spread))
        else:
            drawn.append(spread * jax.random.truncated_normal(sub_key, -3.0, 3.0, (amount,), jnp.float32))
        used_total = used_total + amount
    padding_key = jax.random.fold_in(key, 1000)
    drawn.append(0.05 * jax.random.truncated_normal(padding_key, -3.0, 3.0, (PARAMS - used_total,), jnp.float32))
    return jnp.concatenate(drawn)


def draw_weights(key, part):
    return flat_draw(jax.random.fold_in(key, 11))


def draw_averages(key, part):
    return flat_draw(jax.random.fold_in(key, 23))


def draw_momenta(key, part):
    spread = 0.7 * math.sqrt(PROMPTS * LENGTH * LOOPS)
    sub_key = jax.random.fold_in(key, 37)
    return spread * jax.random.truncated_normal(sub_key, -3.0, 3.0, (PARAMS,), jnp.float32)


def touch_ends(values, stream_key, low, top_value):
    shape = values.shape
    place = [jax.random.randint(jax.random.fold_in(stream_key, axis), (), 0, shape[axis]) for axis in range(len(shape))]
    values = values.at[tuple(place)].set(low)
    longest = shape.index(max(shape))
    place[longest] = (place[longest] + 1) % shape[longest]
    return values.at[tuple(place)].set(top_value)


def steps_of(own_key, shape, split, least, top_value):
    factor_of = 1.0
    for dim, shards_of in split:
        steps = jax.random.uniform(jax.random.fold_in(jax.random.fold_in(own_key, 6), dim), (shards_of,), jnp.float32, least / len(split), top_value / len(split))
        factor_of = factor_of * jnp.repeat(jnp.exp(steps), shape[dim] // shards_of).reshape((-1,) + (1,) * (len(shape) - 1 - dim))
    return factor_of


def normal_values(own_key, dims, scale, limit, cuts=(), held_as=jnp.bfloat16):
    values = scale * jax.random.normal(own_key, dims, jnp.float32)
    if cuts:
        values = values * steps_of(own_key, dims, cuts, -0.22, 0.18)
    return jnp.clip(values, -limit, limit).astype(held_as)


def setup_inputs(seed: int = 0) -> dict:
    key_list = jax.random.split(jax.random.key(seed), 7)
    points = normal_values(key_list[0], (PROMPTS, LENGTH, DIN), 1.0, 4.0, ((0, 8), (1, 4)))
    counts = touch_ends(jax.random.randint(key_list[1], (PROMPTS,), DIN // 4, DIN + 1), jax.random.fold_in(key_list[1], 1), DIN // 4, DIN).astype(jnp.int32)
    cotangent = normal_values(key_list[2], (PROMPTS, LENGTH, D), 1.0, 6.0, ((0, 8), (1, 4)))
    weights = draw_weights(jax.random.fold_in(key_list[6], 71), 0)
    momenta = draw_momenta(jax.random.fold_in(key_list[6], 71), 0)
    averages = draw_averages(jax.random.fold_in(key_list[6], 71), 0)
    return {"points": points, "counts": counts, "cotangent": cotangent, "weights": weights, "momenta": momenta, "averages": averages}


PRECISE = lax.Precision.HIGHEST
EPSILON = 1e-05
RATE = 0.0003
MOMENTUM = 0.5
AVERAGE_DECAY = 0.9

@jax.custom_vjp
def low(v):
    return lax.optimization_barrier(v.astype(jnp.bfloat16)).astype(jnp.float32)

@jax.custom_vjp
def low_back(v):
    return v

def low_keep(v):
    return (low(v), None)

def low_pass(kept, grad):
    return (grad,)

def back_keep(v):
    return (v, None)

def back_low(kept, grad):
    return (low(grad),)
low.defvjp(low_keep, low_pass)
low_back.defvjp(back_keep, back_low)

def split_flat(vector, model_width, hidden_width, input_width, layer_count):
    layouts = [(input_width, model_width), (model_width,)]
    for layer_index in range(layer_count):
        layouts = layouts + [(4, model_width), (model_width, 3 * model_width), (model_width, model_width), (model_width, hidden_width), (hidden_width,), (hidden_width, model_width)]
    pieces = []
    offset = 0
    for dimensions in layouts:
        amount = math.prod(dimensions)
        pieces.append(vector[offset:offset + amount].reshape(dimensions))
        offset = offset + amount
    return pieces

def layer_norm(values, gain, bias):
    centred = values - lax.optimization_barrier(jnp.mean(values, axis=-1, keepdims=True))
    variance = lax.optimization_barrier(jnp.mean(centred * centred, axis=-1, keepdims=True))
    return centred * lax.rsqrt(variance + EPSILON) * gain + bias

def attend_core(queries, key_rows, value_rows):
    length_here = queries.shape[0]
    head_width = queries.shape[1] // HEADS
    query_heads = queries.reshape(length_here, HEADS, head_width)
    key_heads = key_rows.reshape(length_here, HEADS, head_width)
    value_heads = value_rows.reshape(length_here, HEADS, head_width)
    scores = jnp.einsum('qhd,khd->hqk', query_heads, key_heads, precision=PRECISE) * (1.0 / math.sqrt(head_width))
    scores = low_back(scores)
    positions = jnp.arange(length_here)
    causal = positions[None, :] <= positions[:, None]
    scores = jnp.where(causal[None], scores, -jnp.inf)
    probabilities = low(jax.nn.softmax(scores, axis=-1))
    mixed = jnp.einsum('hqk,khd->qhd', probabilities, value_heads, precision=PRECISE)
    return mixed.reshape(length_here, HEADS * head_width)

def layer_apply(hidden_state, layer_params):
    norm_params, w_qkv, w_out, w_up, b_up, w_down = layer_params
    model_width = hidden_state.shape[1]
    normed = low(layer_norm(hidden_state, norm_params[0], norm_params[1]))
    projected = low_back(low(jnp.dot(normed, w_qkv, precision=PRECISE)))
    queries = projected[:, :model_width]
    key_rows = projected[:, model_width:2 * model_width]
    value_rows = projected[:, 2 * model_width:]
    attended = low_back(low(jax.checkpoint(attend_core)(queries, key_rows, value_rows)))
    updated = hidden_state + low_back(jnp.dot(attended, w_out, precision=PRECISE))
    second = low(layer_norm(updated, norm_params[2], norm_params[3]))
    activated = low(jax.nn.gelu(low_back(jnp.dot(second, w_up, precision=PRECISE) + b_up)))
    return updated + low_back(jnp.dot(activated, w_down, precision=PRECISE))

def forward(flat, points_in, column_mask):
    pieces = split_flat(low(flat), D, FF, DIN, LAYERS)
    embedding = low_back(jnp.dot(points_in * column_mask, pieces[0], precision=PRECISE) + pieces[1])
    hidden_state = jnp.zeros_like(embedding)
    for loop_index in range(LOOPS):
        hidden_state = hidden_state + embedding
        for layer_index in range(LAYERS):
            hidden_state = layer_apply(hidden_state, pieces[2 + 6 * layer_index:8 + 6 * layer_index])
    return hidden_state

def reference(points, counts, cotangent, weights, momenta, averages):

    def one_prompt(running, inputs):
        prompt_points, prompt_count, prompt_cotangent = inputs
        column_mask = (jnp.arange(DIN).astype(jnp.int32) < prompt_count).astype(jnp.float32)
        final_state, pull = jax.vjp(lambda flat, points_in: forward(flat, points_in, column_mask), weights, prompt_points.astype(jnp.float32))
        grad_flat, grad_points = pull(prompt_cotangent.astype(jnp.float32))
        return (running + grad_flat, (final_state.astype(jnp.bfloat16), grad_points))
    gradients, outputs = lax.scan(one_prompt, jnp.zeros_like(weights), (points, counts, cotangent))
    states, point_grad = outputs
    momenta_new = MOMENTUM * momenta + gradients
    weights_new = weights - RATE * (gradients + MOMENTUM * momenta_new)
    averages_new = AVERAGE_DECAY * averages + (1.0 - AVERAGE_DECAY) * weights_new
    return (states, point_grad, gradients, weights_new, momenta_new, averages_new)
```

```python
import functools
import math

import jax
import jax.numpy as jnp
from jax import lax
from jax.experimental import pallas as pl
from jax.experimental.pallas import tpu as pltpu
from jax.sharding import PartitionSpec as P

MESH = pl.DeviceIdType.MESH
HEADS = 8
FF = 1024
LAYERS = 2
LOOPS = 2
APPS = LAYERS * LOOPS

EPSILON = 1e-05
RATE = 0.0003
MOMENTUM = 0.5
AVERAGE_DECAY = 0.9

F32 = jnp.float32
BF16 = jnp.bfloat16
DEPTH_PAD = 32
GELU_A = math.sqrt(2.0 / math.pi)
GELU_B = 0.044715


def mm(left, right):
    return jnp.dot(left, right, preferred_element_type=F32)


def mm_nt(left, right):
    return lax.dot_general(left, right, (((1,), (1,)), ((), ())), preferred_element_type=F32)


def twice(column):
    return jnp.concatenate([column, column], axis=1)


def halves(values):
    return values[:, :128] + values[:, 128:]


def normalise(values):
    centred = values - jnp.mean(values, axis=0, keepdims=True)
    variance = jnp.mean(centred * centred, axis=0, keepdims=True)
    scale = lax.rsqrt(variance + EPSILON)
    return centred * scale, scale


def normalise_back(grad, unit, scale, gain):
    scaled = grad * gain
    first = jnp.mean(scaled, axis=0, keepdims=True)
    second = jnp.mean(scaled * unit, axis=0, keepdims=True)
    return (scaled - first - unit * second) * scale


def block_kernel(
    seq_count,
    masked_t, rit, rin, rbias, norms, bup, wqkv_t, wqkv, wo_t, wo, wup_t, wup, wd_t, wd, cot,
    states, pg_t, gri, grb, gnorm, gwqkv, gwo, gwup, gbup, gwd,
    hid, nrm, qsave, kv, kvt, att, osave, lse, upd, nrm2, gp, act, emb,
    qmask, qtok, domask, dotok, ps, ds, peak, total, mixed, dq, gbuf, gemb, gin, gsend, grecv,
    send_n, recv_n, send_g, recv_g,
):
    me = lax.axis_index("seq")
    width = hid.shape[1]
    rows = hid.shape[2]
    head_width = width // HEADS
    exp_scale = math.log2(math.e) / math.sqrt(head_width)
    score_scale = 1.0 / math.sqrt(head_width)

    barrier = pltpu.get_barrier_semaphore()
    for step in range(1, seq_count):
        pl.semaphore_signal(
            barrier, inc=1, device_id={"seq": lax.rem(me + step, seq_count)}, device_id_type=MESH
        )

    qmask[...] = jnp.zeros_like(qmask)
    domask[...] = jnp.zeros_like(domask)
    for ref in (gnorm, gwqkv, gwo, gwup, gbup, gwd):
        ref[...] = jnp.zeros_like(ref)
    ones = jnp.ones((16, rows), BF16)
    column_head = lax.broadcasted_iota(jnp.int32, (rows, width), 1) // head_width

    embedded = mm(rit[...], masked_t[...]) + twice(rbias[...])
    emb[...] = embedded
    hid[0] = embedded
    pl.semaphore_wait(barrier, seq_count - 1)

    def normed_copy(app, source, target):
        return pltpu.make_async_remote_copy(
            src_ref=nrm.at[app, source],
            dst_ref=nrm.at[app, source],
            send_sem=send_n.at[app, target],
            recv_sem=recv_n.at[app, source],
            device_id={"seq": target},
            device_id_type=MESH,
        )

    def grad_copy(app, source, target):
        return pltpu.make_async_remote_copy(
            src_ref=gsend.at[app, target],
            dst_ref=grecv.at[app, source],
            send_sem=send_g.at[app, target],
            recv_sem=recv_g.at[app, source],
            device_id={"seq": target},
            device_id_type=MESH,
        )

    causal = lax.broadcasted_iota(jnp.int32, (rows, rows), 0) <= lax.broadcasted_iota(
        jnp.int32, (rows, rows), 1
    )

    def project_block(app, layer, block):
        block_t = nrm[app, block]
        kvt[app, block] = mm(wqkv_t[layer, width:], block_t).astype(BF16)
        kv[app, block] = mm(
            jnp.transpose(block_t.astype(F32)).astype(BF16), wqkv[layer, :, width:]
        ).astype(BF16)

    def attend_block(app, block, diagonal):
        for head in range(HEADS):
            lanes = slice(head * head_width, (head + 1) * head_width)
            scores = mm(kv[app, block, :, :width], qmask[head]) * exp_scale
            if diagonal:
                scores = jnp.where(causal, scores, -jnp.inf)
                top = jnp.max(scores, axis=0, keepdims=True)
                weight = jnp.exp2(scores - top)
                total[head : head + 1] = jnp.sum(weight, axis=0, keepdims=True)
                mixed[lanes] = mm(
                    kvt[app, block, width + head * head_width : width + (head + 1) * head_width],
                    weight.astype(BF16),
                )
            else:
                old = peak[head : head + 1]
                top = jnp.maximum(old, jnp.max(scores, axis=0, keepdims=True))
                fade = jnp.exp2(old - top)
                weight = jnp.exp2(scores - top)
                total[head : head + 1] = total[head : head + 1] * fade + jnp.sum(
                    weight, axis=0, keepdims=True
                )
                mixed[lanes] = mixed[lanes] * fade + mm(
                    kvt[app, block, width + head * head_width : width + (head + 1) * head_width],
                    weight.astype(BF16),
                )
            peak[head : head + 1] = top

    def forward(app, carry):
        layer = lax.rem(app, LAYERS)
        unit, _ = normalise(hid[app])
        normed = (unit * twice(norms[layer, 0]) + twice(norms[layer, 1])).astype(BF16)
        nrm[app, me] = normed
        for step in range(1, seq_count):

            @pl.when(me + step < seq_count)
            def _():
                normed_copy(app, me, me + step).start()

        queries = mm(wqkv_t[layer, :width], normed).astype(BF16)
        qsave[app] = queries
        for head in range(HEADS):
            lanes = slice(head * head_width, (head + 1) * head_width)
            qmask[head, lanes] = queries[lanes]
        project_block(app, layer, me)
        attend_block(app, me, True)

        def earlier(step, inner):
            block = me - 1 - step
            normed_copy(app, block, me).wait_recv()
            project_block(app, layer, block)
            attend_block(app, block, False)
            return inner

        lax.fori_loop(0, me, earlier, 0)
        for head in range(HEADS):
            lanes = slice(head * head_width, (head + 1) * head_width)
            out = mixed[lanes] * (1.0 / total[head : head + 1])
            osave[app, lanes] = out
            att[app, lanes] = out.astype(BF16)
        lse[app] = peak[...] + jnp.log2(total[...])
        updated = hid[app] + mm(wo_t[layer], att[app])
        upd[app] = updated
        unit, _ = normalise(updated)
        second = (unit * twice(norms[layer, 2]) + twice(norms[layer, 3])).astype(BF16)
        nrm2[app] = second
        before = mm(wup_t[layer], second) + twice(bup[layer])
        squared = before * before
        inner = GELU_A * before * (1.0 + GELU_B * squared)
        turned = jnp.tanh(inner)
        half = 0.5 * (1.0 + turned)
        activated = (before * half).astype(BF16)
        act[app] = activated
        gp[app] = half + (0.5 * GELU_A) * before * (1.0 - turned * turned) * (
            1.0 + (3.0 * GELU_B) * squared
        )
        result = upd[app] + mm(wd_t[layer], act[app])
        again = jnp.where((layer == LAYERS - 1) & (app < APPS - 1), 1.0, 0.0)
        hid[app + 1] = result + again * emb[...]
        return carry

    lax.fori_loop(0, APPS, forward, 0)
    states[...] = jnp.transpose(hid[APPS]).astype(BF16)

    gbuf[...] = jnp.transpose(cot[...].astype(F32))
    gemb[...] = jnp.zeros_like(gemb)

    def attend_back(app, layer, block, diagonal):
        keys = kv[app, block, :, :width]
        values = kv[app, block, :, width:]
        for head in range(HEADS):
            lanes = slice(head * head_width, (head + 1) * head_width)
            wide = slice(head * rows, (head + 1) * rows)
            scores = mm(keys, qmask[head]) * exp_scale
            weight = jnp.exp2(scores - lse[app, head : head + 1])
            if diagonal:
                weight = jnp.where(causal, weight, 0.0)
            ps[:, wide] = weight.astype(BF16)
            grad = mm(values, domask[head])
            back = (weight * (grad - total[head : head + 1])).astype(BF16)
            ds[:, wide] = back
            part = mm(kvt[app, block, lanes], back)
            dq[lanes] = dq[lanes] + part
        grad_keys = (mm(ds[...], qtok[...]) * score_scale).astype(BF16)
        grad_values = mm(ps[...], dotok[...]).astype(BF16)
        block_t = nrm[app, block]
        gwqkv[layer, :, width : 2 * width] += mm(block_t, grad_keys)
        gwqkv[layer, :, 2 * width :] += mm(block_t, grad_values)
        return mm_nt(wqkv[layer, :, width : 2 * width], grad_keys) + mm_nt(
            wqkv[layer, :, 2 * width :], grad_values
        )

    def backward(order, carry):
        app = APPS - 1 - order
        layer = lax.rem(app, LAYERS)
        grad_out = gbuf[...]
        out_low = grad_out.astype(BF16)
        gwd[layer] += mm_nt(act[app], out_low)
        pre_low = (mm(wd[layer], out_low) * gp[app]).astype(BF16)
        act[app] = pre_low
        gwup[layer] += mm_nt(nrm2[app], act[app])
        gbup[layer] += mm_nt(ones, act[app])[:8]
        grad_second = mm(wup[layer], act[app])
        unit, scale = normalise(upd[app])
        gnorm[layer, 2] += halves(grad_second * unit)
        gnorm[layer, 3] += halves(grad_second)
        grad_updated = gbuf[...] + normalise_back(grad_second, unit, scale, twice(norms[layer, 2]))
        gbuf[...] = grad_updated
        branch_low = grad_updated.astype(BF16)
        gwo[layer] += mm_nt(att[app], branch_low)
        grad_att = mm(wo[layer], branch_low).astype(BF16)
        for head in range(HEADS):
            lanes = slice(head * head_width, (head + 1) * head_width)
            domask[head, lanes] = grad_att[lanes]
            qmask[head, lanes] = qsave[app, lanes]
            total[head : head + 1] = jnp.sum(
                osave[app, lanes] * grad_att[lanes].astype(F32), axis=0, keepdims=True
            )
        grad_tok = jnp.transpose(grad_att.astype(F32))
        query_tok = jnp.transpose(qsave[app].astype(F32))
        for head in range(HEADS):
            wide = slice(head * rows, (head + 1) * rows)
            dotok[wide] = jnp.where(column_head == head, grad_tok, 0.0).astype(BF16)
            qtok[wide] = jnp.where(column_head == head, query_tok, 0.0).astype(BF16)
        dq[...] = jnp.zeros_like(dq)

        def earlier(block, inner):
            gsend[app, block] = attend_back(app, layer, block, False).astype(BF16)
            grad_copy(app, me, block).start()
            return inner

        lax.fori_loop(0, me, earlier, 0)
        gin[...] = attend_back(app, layer, me, True)
        grad_queries = (dq[...] * score_scale).astype(BF16)
        gwqkv[layer, :, :width] += mm_nt(nrm[app, me], grad_queries)
        gin[...] += mm(wqkv[layer, :, :width], grad_queries)

        def later(source, inner):
            grad_copy(app, source, me).wait_recv()
            gin[...] += grecv[app, source].astype(F32)
            return inner

        lax.fori_loop(me + 1, seq_count, later, 0)
        grad_normed = gin[...]
        unit, scale = normalise(hid[app])
        gnorm[layer, 0] += halves(grad_normed * unit)
        gnorm[layer, 1] += halves(grad_normed)
        grad_in = gbuf[...] + normalise_back(grad_normed, unit, scale, twice(norms[layer, 0]))
        gbuf[...] = grad_in
        first = jnp.where(layer == 0, 1.0, 0.0)
        gemb[...] += first * grad_in
        return carry

    lax.fori_loop(0, APPS, backward, 0)
    embed_low = gemb[...].astype(BF16)
    gri[...] = mm_nt(masked_t[...], embed_low)
    grb[...] = mm_nt(ones, embed_low)[:8]
    pg_t[...] = mm(rin[...], embed_low)

    def finish(app, carry):
        def sent_normed(target, inner):
            normed_copy(app, me, target).wait_send()
            return inner

        def sent_grad(target, inner):
            grad_copy(app, me, target).wait_send()
            return inner

        lax.fori_loop(me + 1, seq_count, sent_normed, 0)
        lax.fori_loop(0, me, sent_grad, 0)
        return carry

    lax.fori_loop(0, APPS, finish, 0)


def run_block(seq_count, rows, width, hidden, operands):
    vmem = pl.BlockSpec(memory_space=pltpu.VMEM)
    shape = jax.ShapeDtypeStruct
    outs = (
        shape((rows, width), BF16),
        shape((DEPTH_PAD, rows), F32),
        shape((DEPTH_PAD, width), F32),
        shape((8, width), F32),
        shape((LAYERS, 4, width, 128), F32),
        shape((LAYERS, width, 3 * width), F32),
        shape((LAYERS, width, width), F32),
        shape((LAYERS, width, hidden), F32),
        shape((LAYERS, 8, hidden), F32),
        shape((LAYERS, hidden, width), F32),
    )
    scratch = [
        pltpu.VMEM((APPS + 1, width, rows), F32),
        pltpu.VMEM((APPS, seq_count, width, rows), BF16),
        pltpu.VMEM((APPS, width, rows), BF16),
        pltpu.VMEM((APPS, seq_count, rows, 2 * width), BF16),
        pltpu.VMEM((APPS, seq_count, 2 * width, rows), BF16),
        pltpu.VMEM((APPS, width, rows), BF16),
        pltpu.VMEM((APPS, width, rows), F32),
        pltpu.VMEM((APPS, HEADS, rows), F32),
        pltpu.VMEM((APPS, width, rows), F32),
        pltpu.VMEM((APPS, width, rows), BF16),
        pltpu.VMEM((APPS, hidden, rows), F32),
        pltpu.VMEM((APPS, hidden, rows), BF16),
        pltpu.VMEM((width, rows), F32),
        pltpu.VMEM((HEADS, width, rows), BF16),
        pltpu.VMEM((HEADS * rows, width), BF16),
        pltpu.VMEM((HEADS, width, rows), BF16),
        pltpu.VMEM((HEADS * rows, width), BF16),
        pltpu.VMEM((rows, HEADS * rows), BF16),
        pltpu.VMEM((rows, HEADS * rows), BF16),
        pltpu.VMEM((HEADS, rows), F32),
        pltpu.VMEM((HEADS, rows), F32),
        pltpu.VMEM((width, rows), F32),
        pltpu.VMEM((width, rows), F32),
        pltpu.VMEM((width, rows), F32),
        pltpu.VMEM((width, rows), F32),
        pltpu.VMEM((width, rows), F32),
        pltpu.VMEM((APPS, seq_count, width, rows), BF16),
        pltpu.VMEM((APPS, seq_count, width, rows), BF16),
        pltpu.SemaphoreType.DMA((APPS, seq_count)),
        pltpu.SemaphoreType.DMA((APPS, seq_count)),
        pltpu.SemaphoreType.DMA((APPS, seq_count)),
        pltpu.SemaphoreType.DMA((APPS, seq_count)),
    ]
    return pl.pallas_call(
        functools.partial(block_kernel, seq_count),
        out_shape=outs,
        in_specs=[vmem] * len(operands),
        out_specs=(vmem,) * len(outs),
        scratch_shapes=scratch,
        compiler_params=pltpu.CompilerParams(
            collective_id=0, has_side_effects=True, vmem_limit_bytes=62 * 1024 * 1024
        ),
    )(*operands)


def split_flat(vector, model_width, hidden_width, input_width, layer_count):
    layouts = [(input_width, model_width), (model_width,)]
    for _ in range(layer_count):
        layouts = layouts + [
            (4, model_width),
            (model_width, 3 * model_width),
            (model_width, model_width),
            (model_width, hidden_width),
            (hidden_width,),
            (hidden_width, model_width),
        ]
    pieces = []
    offset = 0
    for dimensions in layouts:
        amount = math.prod(dimensions)
        pieces.append(vector[offset : offset + amount].reshape(dimensions))
        offset = offset + amount
    return pieces


def shards(points, counts, cotangent, weights, momenta, averages):
    rows = points.shape[1]
    depth = points.shape[2]
    width = cotangent.shape[2]
    seq_count = lax.axis_size("seq")
    column_mask = jnp.arange(depth, dtype=jnp.int32) < counts[0]
    masked_low = jnp.where(column_mask, points[0], 0).astype(BF16)
    masked_t = jnp.pad(masked_low.T, ((0, DEPTH_PAD - depth), (0, 0)))
    gathered = lax.all_gather(weights.astype(BF16), "dp", axis=0, tiled=True)
    pieces = split_flat(gathered, width, FF, depth, LAYERS)

    def layered(place):
        return jnp.stack([pieces[2 + 6 * layer + place] for layer in range(LAYERS)])

    def spread(values):
        return jnp.broadcast_to(values.astype(F32)[..., None], values.shape + (128,))

    def turned(values):
        return jnp.swapaxes(values, 1, 2)

    rin = jnp.pad(pieces[0], ((0, DEPTH_PAD - depth), (0, 0)))
    norms, wqkv, wo, wup, bup, wd = (layered(place) for place in range(6))
    operands = (
        masked_t, rin.T, rin, spread(pieces[1]), spread(norms), spread(bup),
        turned(wqkv), wqkv, turned(wo), wo, turned(wup), wup, turned(wd), wd, cotangent[0],
    )
    states, pg_t, gri, grb, gnorm, gwqkv, gwo, gwup, gbup, gwd = run_block(
        seq_count, rows, width, FF, operands
    )
    point_grad = jnp.where(column_mask, pg_t[:depth].T, 0.0)[None]
    gnorm = jnp.sum(gnorm, axis=-1)
    flat_parts = [gri[:depth].reshape(-1), grb[0]]
    for layer in range(LAYERS):
        flat_parts += [
            member.reshape(-1)
            for member in (
                gnorm[layer], gwqkv[layer], gwo[layer], gwup[layer], gbup[layer, 0], gwd[layer],
            )
        ]
    used_grads = jnp.concatenate(flat_parts)
    total_length = weights.shape[0] * lax.axis_size("dp")
    flat_grad = jnp.pad(used_grads, (0, total_length - used_grads.shape[0]))
    owner_share = lax.psum_scatter(flat_grad, "dp", scatter_dimension=0, tiled=True)
    gradients = lax.psum(owner_share.astype(BF16), "seq").astype(F32)
    momenta_new = MOMENTUM * momenta + gradients
    weights_new = weights - RATE * (gradients + MOMENTUM * momenta_new)
    averages_new = AVERAGE_DECAY * averages + (1.0 - AVERAGE_DECAY) * weights_new
    return (states[None], point_grad, gradients, weights_new, momenta_new, averages_new)


def solution(mesh):
    placed = (P("dp", "seq", None), P("dp"), P("dp", "seq", None), P("dp"), P("dp"), P("dp"))
    return jax.shard_map(
        shards,
        mesh=mesh,
        in_specs=placed,
        out_specs=(P("dp", "seq", None), P("dp", "seq", None), P("dp"), P("dp"), P("dp"), P("dp")),
        check_vma=False,
    )
```

```python
import functools
import math

import jax
import jax.numpy as jnp
from jax import lax
from jax.experimental import pallas as pl
from jax.experimental.pallas import tpu as pltpu
from jax.sharding import PartitionSpec as P

MESH = pl.DeviceIdType.MESH
HEADS = 8
FF = 1024
LAYERS = 2
LOOPS = 2
APPS = LAYERS * LOOPS

EPSILON = 1e-05
RATE = 0.0003
MOMENTUM = 0.5
AVERAGE_DECAY = 0.9

F32 = jnp.float32
BF16 = jnp.bfloat16
GELU_A = math.sqrt(2.0 / math.pi)
GELU_B = 0.044715


def mm(left, right):
    return jnp.dot(left, right, preferred_element_type=F32)


def mm_nt(left, right):
    return lax.dot_general(left, right, (((1,), (1,)), ((), ())), preferred_element_type=F32)


def twice(column):
    return jnp.concatenate([column, column], axis=1)


def halves(values):
    return values[:, :128] + values[:, 128:]


def normalise(values):
    centred = values - jnp.mean(values, axis=0, keepdims=True)
    variance = jnp.mean(centred * centred, axis=0, keepdims=True)
    scale = lax.rsqrt(variance + EPSILON)
    return centred * scale, scale


def normalise_back(grad, unit, scale, gain):
    scaled = grad * gain
    first = jnp.mean(scaled, axis=0, keepdims=True)
    second = jnp.mean(scaled * unit, axis=0, keepdims=True)
    return (scaled - first - unit * second) * scale


class Plan:
    def __init__(self, rows, depth, width, share, dp_count, seq_count):
        self.rows = rows
        self.depth = depth
        self.width = width
        self.hidden = FF
        self.dp = dp_count
        self.zs = dp_count // 2
        self.seq = seq_count
        self.flat = share // width
        self.half = -(-self.flat // 32) * 16
        self.block = 4 + 3 * width + width + FF + FF // width + FF
        self.total = self.flat * dp_count
        self.space = self.total + 32 + width

    def base(self, layer):
        return self.depth + 1 + layer * self.block


def whole_kernel(plan, names, *refs):
    ref = dict(zip(names, refs, strict=True))
    (
        points, counts, cot, weights, momenta, averages,
        states, point_grad, gradients, weights_new, momenta_new, averages_new,
    ) = (ref[name] for name in names[:12])
    rows, width, hidden = plan.rows, plan.width, plan.hidden
    seq_count, dp_count, zs, half = plan.seq, plan.dp, plan.zs, plan.half
    head_width = width // HEADS
    exp_scale = math.log2(math.e) / math.sqrt(head_width)
    score_scale = 1.0 / math.sqrt(head_width)
    low_half, high_half = half, plan.flat - half

    me = lax.axis_index("seq")
    owner = lax.axis_index("dp")
    my_z, my_x = owner // 2, lax.rem(owner, 2)
    my_y, my_c = me // 2, lax.rem(me, 2)
    sibling = {"seq": my_y * 2 + (1 - my_c)}
    across = {"seq": (1 - my_y) * 2 + my_c}
    beside = {"dp": my_z * 2 + (1 - my_x)}

    barrier = pltpu.get_barrier_semaphore()

    def greet(device):
        pl.semaphore_signal(barrier, inc=1, device_id=device, device_id_type=MESH)

    for step in range(1, seq_count):
        greet({"seq": lax.rem(me + step, seq_count)})
    greet(beside)

    def greet_z(step, carry):
        greet({"dp": lax.rem(my_z + step, zs) * 2 + my_x})
        return carry

    lax.fori_loop(1, zs, greet_z, 0)

    def remote(source, target, send, receive, device):
        return pltpu.make_async_remote_copy(
            src_ref=source, dst_ref=target, send_sem=send, recv_sem=receive,
            device_id=device, device_id_type=MESH,
        )

    gathered = ref["gathered"]
    tail_rows = high_half // 16 * 16
    for h in range(2):
        for r, count in ((0, low_half), (1, tail_rows)):
            gathered[owner, h, r, :count] = weights[
                pl.ds(2 * r * half + h, count, stride=2), :
            ].astype(BF16)
        if high_half < half:
            gathered[owner, h, 1, tail_rows:] = jnp.concatenate(
                [
                    weights[pl.ds(2 * (half + tail_rows) + h, high_half - tail_rows, stride=2), :],
                    jnp.zeros((half - high_half, 128), F32),
                ],
                axis=0,
            ).astype(BF16)

    pl.semaphore_wait(barrier, seq_count - 1 + zs)

    def along_z(source_z, target_z):
        piece = gathered.at[2 * source_z + my_x, my_c, my_y]
        return remote(
            piece, piece, ref["send_wz"].at[target_z], ref["recv_wz"].at[source_z],
            {"dp": 2 * target_z + my_x},
        )

    def along_y(z, part):
        piece = gathered.at[2 * z + my_x, my_c, part]
        return remote(piece, piece, ref["send_wy"].at[z], ref["recv_wy"].at[z], across)

    def along_x(z, x, part):
        piece = gathered.at[2 * z + x, my_c, part]
        return remote(
            piece, piece, ref["send_wx"].at[z, part], ref["recv_wx"].at[z, part], beside
        )

    def along_c(share, column):
        piece = gathered.at[share, column]
        return remote(piece, piece, ref["send_wc"].at[share], ref["recv_wc"].at[share], sibling)

    def each_z(body):
        def step(z, carry):
            body(z)
            return carry

        lax.fori_loop(0, zs, step, 0)

    def each_other_z(body):
        def step(z, carry):
            @pl.when(z != my_z)
            def _():
                body(z)

            return carry

        lax.fori_loop(0, zs, step, 0)

    each_other_z(lambda z: along_z(my_z, z).start())
    along_x(my_z, my_x, 0).start()
    along_x(my_z, my_x, 1).start()

    def second(z):
        along_z(z, my_z).wait_recv()
        along_y(z, my_y).start()
        along_x(z, my_x, my_y).start()

    def third(z):
        along_y(z, 1 - my_y).wait_recv()
        along_x(z, my_x, 1 - my_y).start()
        along_c(2 * z + my_x, my_c).start()

    def fourth(z):
        along_x(z, 1 - my_x, 0).wait_recv()
        along_x(z, 1 - my_x, 1).wait_recv()
        along_c(2 * z + 1 - my_x, my_c).start()

    def fifth(z):
        @pl.when(z != my_z)
        def _():
            along_c(2 * z + my_x, 1 - my_c).wait_recv()

        along_c(2 * z + 1 - my_x, 1 - my_c).wait_recv()

    each_other_z(second)
    each_other_z(third)
    each_z(fourth)
    each_z(fifth)

    flat = ref["flat"]
    for share in range(dp_count):
        for h in range(2):
            for r in range(2):
                flat[h, pl.ds(share * plan.flat + r * half, half), :] = gathered[
                    share, h, r
                ].astype(F32)

    rin, rit, rbias, norms, bup = (ref[n] for n in ("rin", "rit", "rbias", "norms", "bup"))
    wqkv, wqkv_t, wo, wo_t = (ref[n] for n in ("wqkv", "wqkv_t", "wo", "wo_t"))
    wup, wup_t, wd, wd_t = (ref[n] for n in ("wup", "wup_t", "wd", "wd_t"))
    depth_row = lax.broadcasted_iota(jnp.int32, (128, 128), 0)
    for h in range(2):
        lanes = slice(128 * h, 128 * (h + 1))
        block = flat[h, :128]
        turned = jnp.transpose(block)
        rbias[lanes] = jnp.broadcast_to(turned[:, plan.depth : plan.depth + 1], (128, 128))
        block = jnp.where(depth_row < plan.depth, block, 0.0)
        rin[:, lanes] = block.astype(BF16)
        rit[lanes] = jnp.transpose(block).astype(BF16)
        for layer in range(LAYERS):
            base = plan.base(layer)
            turned = jnp.transpose(flat[h, pl.ds(base, 128), :])
            for j in range(4):
                norms[layer, j, lanes] = jnp.broadcast_to(turned[:, j : j + 1], (128, 128))
            base += 4
            for j in range(3):
                value = flat[h, pl.ds(base + j, width, stride=3), :]
                place = slice(width * j + 128 * h, width * j + 128 * (h + 1))
                wqkv[layer, :, place] = value.astype(BF16)
                wqkv_t[layer, place] = jnp.transpose(value).astype(BF16)
            base += 3 * width
            value = flat[h, pl.ds(base, width), :]
            wo[layer, :, lanes] = value.astype(BF16)
            wo_t[layer, lanes] = jnp.transpose(value).astype(BF16)
            base += width
            parts = hidden // width
            for j in range(parts):
                value = flat[h, pl.ds(base + j, width, stride=parts), :]
                place = slice(width * j + 128 * h, width * j + 128 * (h + 1))
                wup[layer, :, place] = value.astype(BF16)
                wup_t[layer, place] = jnp.transpose(value).astype(BF16)
            base += hidden
            turned = jnp.transpose(flat[h, pl.ds(base, 128), :])
            for j in range(parts):
                bup[layer, width * j + 128 * h : width * j + 128 * (h + 1)] = jnp.broadcast_to(
                    turned[:, j : j + 1], (128, 128)
                )
            base += parts
            value = flat[h, pl.ds(base, hidden), :]
            wd[layer, :, lanes] = value.astype(BF16)
            wd_t[layer, lanes] = jnp.transpose(value).astype(BF16)

    column_mask = lax.broadcasted_iota(jnp.int32, (rows, 128), 1) < counts[0]
    wide_points = ref["wide_points"]
    wide_points[...] = jnp.zeros_like(wide_points)
    wide_points[:, : plan.depth] = points[...].astype(F32)
    masked_t = jnp.transpose(jnp.where(column_mask, wide_points[...], 0.0)).astype(BF16)
    ref["masked_t"][...] = masked_t

    (gnorm, hid, nrm, qsave, kv, kt, vt, att, osave, lse, upd, nrm2, gp, act, emb, qmask, qtok, domask, dotok, ps, ds, peak, total, mixed, dq, gbuf, gemb, gin, send_n, recv_n, send_g, recv_g) = (
        ref[n] for n in ("gnorm", "hid", "nrm", "qsave", "kv", "kt", "vt", "att", "osave", "lse", "upd", "nrm2", "gp", "act", "emb", "qmask", "qtok", "domask", "dotok", "ps", "ds", "peak", "total", "mixed", "dq", "gbuf", "gemb", "gin", "send_n", "recv_n", "send_g", "recv_g")
    )
    qmask[...] = jnp.zeros_like(qmask)
    domask[...] = jnp.zeros_like(domask)
    for sums in (gnorm, flat):
        sums[...] = jnp.zeros_like(sums)
    parts = hidden // width

    def accumulate(layer, offset, stride, value):
        start = plan.base(0) + layer * plan.block + offset
        count = value.shape[0]
        for h in range(2):
            lanes = slice(128 * h, 128 * (h + 1))
            flat[h, pl.ds(start, count, stride=stride), :] += value[:, lanes]

    ones = jnp.ones((16, rows), BF16)
    column_head = lax.broadcasted_iota(jnp.int32, (rows, width), 1) // head_width

    embedded = mm(rit[...], ref["masked_t"][...]) + twice(rbias[...])
    emb[...] = embedded
    hid[0] = embedded

    def normed_copy(app, source, target):
        return pltpu.make_async_remote_copy(
            src_ref=nrm.at[app, source],
            dst_ref=nrm.at[app, source],
            send_sem=send_n.at[app, target],
            recv_sem=recv_n.at[app, source],
            device_id={"seq": target},
            device_id_type=MESH,
        )

    def grad_copy(app, source, target):
        return pltpu.make_async_remote_copy(
            src_ref=nrm.at[app, target],
            dst_ref=nrm.at[app, source],
            send_sem=send_g.at[app, target],
            recv_sem=recv_g.at[app, source],
            device_id={"seq": target},
            device_id_type=MESH,
        )

    causal = lax.broadcasted_iota(jnp.int32, (rows, rows), 0) <= lax.broadcasted_iota(
        jnp.int32, (rows, rows), 1
    )

    def project_block(app, layer, block):
        block_t = nrm[app, block]
        kt[app, block] = mm(wqkv_t[layer, width : 2 * width], block_t).astype(BF16)
        vt[...] = mm(wqkv_t[layer, 2 * width :], block_t).astype(BF16)
        kv[app, block] = mm(
            jnp.transpose(block_t.astype(F32)).astype(BF16), wqkv[layer, :, width:]
        ).astype(BF16)

    def attend_block(app, block, diagonal):
        for head in range(HEADS):
            lanes = slice(head * head_width, (head + 1) * head_width)
            scores = mm(kv[app, block, :, :width], qmask[head]) * exp_scale
            if diagonal:
                scores = jnp.where(causal, scores, -jnp.inf)
                top = jnp.max(scores, axis=0, keepdims=True)
                weight = jnp.exp2(scores - top)
                total[head : head + 1] = jnp.sum(weight, axis=0, keepdims=True)
                mixed[lanes] = mm(
                    vt[lanes],
                    weight.astype(BF16),
                )
            else:
                old = peak[head : head + 1]
                top = jnp.maximum(old, jnp.max(scores, axis=0, keepdims=True))
                fade = jnp.exp2(old - top)
                weight = jnp.exp2(scores - top)
                total[head : head + 1] = total[head : head + 1] * fade + jnp.sum(
                    weight, axis=0, keepdims=True
                )
                mixed[lanes] = mixed[lanes] * fade + mm(
                    vt[lanes],
                    weight.astype(BF16),
                )
            peak[head : head + 1] = top

    def forward(app, carry):
        layer = lax.rem(app, LAYERS)
        unit, _ = normalise(hid[app])
        normed = (unit * twice(norms[layer, 0]) + twice(norms[layer, 1])).astype(BF16)
        nrm[app, me] = normed
        for step in range(1, seq_count):

            @pl.when(me + step < seq_count)
            def _():
                normed_copy(app, me, me + step).start()

        queries = mm(wqkv_t[layer, :width], normed).astype(BF16)
        qsave[app] = queries
        for head in range(HEADS):
            lanes = slice(head * head_width, (head + 1) * head_width)
            qmask[head, lanes] = queries[lanes]
        project_block(app, layer, me)
        attend_block(app, me, True)

        def earlier(step, inner):
            block = me - 1 - step
            normed_copy(app, block, me).wait_recv()
            project_block(app, layer, block)
            attend_block(app, block, False)
            return inner

        lax.fori_loop(0, me, earlier, 0)
        for head in range(HEADS):
            lanes = slice(head * head_width, (head + 1) * head_width)
            out = mixed[lanes] * (1.0 / total[head : head + 1])
            osave[app, lanes] = out
            att[app, lanes] = out.astype(BF16)
        lse[app] = peak[...] + jnp.log2(total[...])
        updated = hid[app] + mm(wo_t[layer], att[app])
        upd[app] = updated
        unit, _ = normalise(updated)
        second = (unit * twice(norms[layer, 2]) + twice(norms[layer, 3])).astype(BF16)
        nrm2[app] = second
        before = mm(wup_t[layer], second) + twice(bup[layer])
        squared = before * before
        inner = GELU_A * before * (1.0 + GELU_B * squared)
        turned = jnp.tanh(inner)
        half = 0.5 * (1.0 + turned)
        activated = (before * half).astype(BF16)
        act[app] = activated
        gp[app] = half + (0.5 * GELU_A) * before * (1.0 - turned * turned) * (
            1.0 + (3.0 * GELU_B) * squared
        )
        result = upd[app] + mm(wd_t[layer], act[app])
        again = jnp.where((layer == LAYERS - 1) & (app < APPS - 1), 1.0, 0.0)
        hid[app + 1] = result + again * emb[...]
        return carry

    lax.fori_loop(0, APPS, forward, 0)
    states[...] = jnp.transpose(hid[APPS]).astype(BF16)

    gbuf[...] = jnp.transpose(cot[...].astype(F32))
    gemb[...] = jnp.zeros_like(gemb)

    def attend_back(app, layer, block, diagonal):
        keys = kv[app, block, :, :width]
        values = kv[app, block, :, width:]
        for head in range(HEADS):
            lanes = slice(head * head_width, (head + 1) * head_width)
            wide = slice(head * rows, (head + 1) * rows)
            scores = mm(keys, qmask[head]) * exp_scale
            weight = jnp.exp2(scores - lse[app, head : head + 1])
            if diagonal:
                weight = jnp.where(causal, weight, 0.0)
            ps[:, wide] = weight.astype(BF16)
            grad = mm(values, domask[head])
            back = (weight * (grad - total[head : head + 1])).astype(BF16)
            ds[:, wide] = back
            part = mm(kt[app, block, lanes], back)
            dq[lanes] = dq[lanes] + part
        grad_keys = (mm(ds[...], qtok[...]) * score_scale).astype(BF16)
        grad_values = mm(ps[...], dotok[...]).astype(BF16)
        block_t = nrm[app, block]
        accumulate(layer, 5, 3, mm(block_t, grad_keys))
        accumulate(layer, 6, 3, mm(block_t, grad_values))
        return mm_nt(wqkv[layer, :, width : 2 * width], grad_keys) + mm_nt(
            wqkv[layer, :, 2 * width :], grad_values
        )

    def backward(order, carry):
        app = APPS - 1 - order
        layer = lax.rem(app, LAYERS)
        grad_out = gbuf[...]
        out_low = grad_out.astype(BF16)
        accumulate(layer, 4 + 4 * width + hidden + parts, 1, mm_nt(act[app], out_low))
        pre_low = (mm(wd[layer], out_low) * gp[app]).astype(BF16)
        act[app] = pre_low
        for j in range(parts):
            part = act[app, width * j : width * (j + 1)]
            accumulate(layer, 4 + 4 * width + j, parts, mm_nt(nrm2[app], part))
            accumulate(layer, 4 + 4 * width + hidden + j, 1, mm_nt(ones, part)[:1])
        grad_second = mm(wup[layer], act[app])
        unit, scale = normalise(upd[app])
        gnorm[layer, 2] += halves(grad_second * unit)
        gnorm[layer, 3] += halves(grad_second)
        grad_updated = gbuf[...] + normalise_back(grad_second, unit, scale, twice(norms[layer, 2]))
        gbuf[...] = grad_updated
        branch_low = grad_updated.astype(BF16)
        accumulate(layer, 4 + 3 * width, 1, mm_nt(att[app], branch_low))
        grad_att = mm(wo[layer], branch_low).astype(BF16)
        for head in range(HEADS):
            lanes = slice(head * head_width, (head + 1) * head_width)
            domask[head, lanes] = grad_att[lanes]
            qmask[head, lanes] = qsave[app, lanes]
            total[head : head + 1] = jnp.sum(
                osave[app, lanes] * grad_att[lanes].astype(F32), axis=0, keepdims=True
            )
        grad_tok = jnp.transpose(grad_att.astype(F32))
        query_tok = jnp.transpose(qsave[app].astype(F32))
        for head in range(HEADS):
            wide = slice(head * rows, (head + 1) * rows)
            dotok[wide] = jnp.where(column_head == head, grad_tok, 0.0).astype(BF16)
            qtok[wide] = jnp.where(column_head == head, query_tok, 0.0).astype(BF16)
        dq[...] = jnp.zeros_like(dq)

        def earlier(block, inner):
            nrm[app, block] = attend_back(app, layer, block, False).astype(BF16)
            grad_copy(app, me, block).start()
            return inner

        lax.fori_loop(0, me, earlier, 0)
        gin[...] = attend_back(app, layer, me, True)
        grad_queries = (dq[...] * score_scale).astype(BF16)
        accumulate(layer, 4, 3, mm_nt(nrm[app, me], grad_queries))
        gin[...] += mm(wqkv[layer, :, :width], grad_queries)

        def later(source, inner):
            grad_copy(app, source, me).wait_recv()
            gin[...] += nrm[app, source].astype(F32)
            return inner

        lax.fori_loop(me + 1, seq_count, later, 0)
        grad_normed = gin[...]
        unit, scale = normalise(hid[app])
        gnorm[layer, 0] += halves(grad_normed * unit)
        gnorm[layer, 1] += halves(grad_normed)
        grad_in = gbuf[...] + normalise_back(grad_normed, unit, scale, twice(norms[layer, 0]))
        gbuf[...] = grad_in
        first = jnp.where(layer == 0, 1.0, 0.0)
        gemb[...] += first * grad_in
        return carry

    lax.fori_loop(0, APPS, backward, 0)

    embed_low = gemb[...].astype(BF16)
    grad_in_rows = mm_nt(ref["masked_t"][...], embed_low)
    grad_bias_rows = mm_nt(ones, embed_low)
    point_rows = jnp.where(column_mask, jnp.transpose(mm(rin[...], embed_low)), 0.0)
    point_grad[...] = point_rows[:, : plan.depth]
    for h in range(2):
        lanes = slice(128 * h, 128 * (h + 1))
        flat[h, : plan.depth] = grad_in_rows[: plan.depth, lanes]
        flat[h, plan.depth : plan.depth + 1] = grad_bias_rows[:1, lanes]
        for layer in range(LAYERS):
            base = plan.base(layer)
            for j in range(4):
                flat[h, base + j : base + j + 1] = jnp.sum(
                    jnp.transpose(gnorm[layer, j, lanes]), axis=0, keepdims=True
                )

    each_other_z(lambda z: along_z(my_z, z).wait_send())
    each_other_z(lambda z: along_y(z, my_y).wait_send())
    for r in range(2):
        each_z(lambda z, r=r: along_x(z, my_x, r).wait_send())
    each_other_z(lambda z: along_c(2 * z + my_x, my_c).wait_send())
    each_z(lambda z: along_c(2 * z + 1 - my_x, my_c).wait_send())
    parts_low = ref["gathered"]
    for share in range(dp_count):
        for h in range(2):
            for r in range(2):
                parts_low[share, h, r] = flat[
                    h, pl.ds(share * plan.flat + r * half, half), :
                ].astype(BF16)

    from_core, from_x, from_y, from_z = (
        ref[n] for n in ("from_core", "from_x", "from_y", "from_z")
    )
    copy = remote(
        parts_low.at[:, 1 - my_c], from_core, ref["send_gc"].at[0], ref["recv_gc"].at[0], sibling
    )
    copy.start()
    copy.wait()

    def add(target, source):
        target[...] = (target[...].astype(F32) + source[...].astype(F32)).astype(BF16)

    def add_core(share, carry):
        for r in range(2):
            add(parts_low.at[share, my_c, r], from_core.at[share, r])
        return carry

    lax.fori_loop(0, dp_count, add_core, 0)

    def grad_x(z):
        return remote(
            parts_low.at[2 * z + 1 - my_x, my_c], from_x.at[z],
            ref["send_gx"].at[z], ref["recv_gx"].at[z], beside,
        )

    def grad_y(z):
        return remote(
            parts_low.at[2 * z + my_x, my_c, 1 - my_y], from_y.at[z],
            ref["send_gy"].at[z], ref["recv_gy"].at[z], across,
        )

    def grad_z(source_z, target_z):
        return remote(
            parts_low.at[2 * target_z + my_x, my_c, my_y], from_z.at[source_z],
            ref["send_gz"].at[target_z], ref["recv_gz"].at[source_z], {"dp": 2 * target_z + my_x},
        )

    each_z(lambda z: grad_x(z).start())

    def after_x(z):
        grad_x(z).wait()
        for r in range(2):
            add(parts_low.at[2 * z + my_x, my_c, r], from_x.at[z, r])
        grad_y(z).start()

    each_z(after_x)

    def after_y(z):
        grad_y(z).wait()
        add(parts_low.at[2 * z + my_x, my_c, my_y], from_y.at[z])

        @pl.when(z != my_z)
        def _():
            grad_z(my_z, z).start()

    each_z(after_y)
    last = ref["last"]
    last[...] = parts_low[owner, my_c, my_y].astype(F32)

    def after_z(z):
        grad_z(z, my_z).wait_recv()
        last[...] += from_z[z].astype(F32)

    each_other_z(after_z)
    summed = ref["summed"]
    summed[my_c, my_y] = last[...].astype(BF16)

    def share_seq(source, target):
        piece = summed.at[lax.rem(source, 2), source // 2]
        return remote(
            piece, piece, ref["send_gs"].at[target], ref["recv_gs"].at[source], {"seq": target}
        )

    for step in range(1, seq_count):
        share_seq(me, lax.rem(me + step, seq_count)).start()
    for step in range(1, seq_count):
        share_seq(lax.rem(me + step, seq_count), me).wait_recv()
    for h in range(2):
        for r, count in ((0, low_half), (1, high_half)):
            gradients[pl.ds(2 * r * half + h, count, stride=2), :] = summed[h, r].astype(F32)[
                :count
            ]
    grad = gradients[...]
    momentum = MOMENTUM * momenta[...] + grad
    momenta_new[...] = momentum
    fresh = weights[...] - RATE * (grad + MOMENTUM * momentum)
    weights_new[...] = fresh
    averages_new[...] = AVERAGE_DECAY * averages[...] + (1.0 - AVERAGE_DECAY) * fresh

    each_other_z(lambda z: grad_z(my_z, z).wait_send())
    for step in range(1, seq_count):
        share_seq(me, lax.rem(me + step, seq_count)).wait_send()

    def finish(app, carry):
        def sent_normed(target, inner):
            normed_copy(app, me, target).wait_send()
            return inner

        def sent_grad(target, inner):
            grad_copy(app, me, target).wait_send()
            return inner

        lax.fori_loop(me + 1, seq_count, sent_normed, 0)
        lax.fori_loop(0, me, sent_grad, 0)
        return carry

    lax.fori_loop(0, APPS, finish, 0)


def shards(points, counts, cotangent, weights, momenta, averages):
    rows, depth = points.shape[1:]
    width = cotangent.shape[2]
    share = weights.shape[0]
    plan = Plan(rows, depth, width, share, lax.axis_size("dp"), lax.axis_size("seq"))
    hidden, seq_count, dp_count, zs, half = plan.hidden, plan.seq, plan.dp, plan.zs, plan.half
    vmem = pl.BlockSpec(memory_space=pltpu.VMEM)
    smem = pl.BlockSpec(memory_space=pltpu.SMEM)
    shape = jax.ShapeDtypeStruct
    lines = (share // 128, 128)
    outs = (
        shape((rows, width), BF16),
        shape((rows, depth), F32),
        shape(lines, F32),
        shape(lines, F32),
        shape(lines, F32),
        shape(lines, F32),
    )
    low = lambda *dims: pltpu.VMEM(dims, BF16)
    full = lambda *dims: pltpu.VMEM(dims, F32)
    flags = lambda *dims: pltpu.SemaphoreType.DMA(dims)
    scratch = {
        "gathered": low(dp_count, 2, 2, half, 128),
        "flat": full(2, plan.space, 128),
        "rin": low(128, width),
        "rit": low(width, 128),
        "rbias": full(width, 128),
        "norms": full(LAYERS, 4, width, 128),
        "bup": full(LAYERS, hidden, 128),
        "wqkv": low(LAYERS, width, 3 * width),
        "wqkv_t": low(LAYERS, 3 * width, width),
        "wo": low(LAYERS, width, width),
        "wo_t": low(LAYERS, width, width),
        "wup": low(LAYERS, width, hidden),
        "wup_t": low(LAYERS, hidden, width),
        "wd": low(LAYERS, hidden, width),
        "wd_t": low(LAYERS, width, hidden),
        "wide_points": full(rows, 128),
        "masked_t": low(128, rows),
        "gnorm": full(LAYERS, 4, width, 128),
        "from_core": low(dp_count, 2, half, 128),
        "from_x": low(zs, 2, half, 128),
        "from_y": low(zs, half, 128),
        "from_z": low(zs, half, 128),
        "last": full(half, 128),
        "summed": low(2, 2, half, 128),
        "hid": full(APPS + 1, width, rows),
        "nrm": low(APPS, seq_count, width, rows),
        "qsave": low(APPS, width, rows),
        "kv": low(APPS, seq_count, rows, 2 * width),
        "kt": low(APPS, seq_count, width, rows),
        "vt": low(width, rows),
        "att": low(APPS, width, rows),
        "osave": full(APPS, width, rows),
        "lse": full(APPS, HEADS, rows),
        "upd": full(APPS, width, rows),
        "nrm2": low(APPS, width, rows),
        "gp": full(APPS, hidden, rows),
        "act": low(APPS, hidden, rows),
        "emb": full(width, rows),
        "qmask": low(HEADS, width, rows),
        "qtok": low(HEADS * rows, width),
        "domask": low(HEADS, width, rows),
        "dotok": low(HEADS * rows, width),
        "ps": low(rows, HEADS * rows),
        "ds": low(rows, HEADS * rows),
        "peak": full(HEADS, rows),
        "total": full(HEADS, rows),
        "mixed": full(width, rows),
        "dq": full(width, rows),
        "gbuf": full(width, rows),
        "gemb": full(width, rows),
        "gin": full(width, rows),
        "send_n": flags(APPS, seq_count),
        "recv_n": flags(APPS, seq_count),
        "send_g": flags(APPS, seq_count),
        "recv_g": flags(APPS, seq_count),
        "send_wz": flags(zs),
        "recv_wz": flags(zs),
        "send_wy": flags(zs),
        "recv_wy": flags(zs),
        "send_wx": flags(zs, 2),
        "recv_wx": flags(zs, 2),
        "send_wc": flags(dp_count),
        "recv_wc": flags(dp_count),
        "send_gc": flags(1),
        "recv_gc": flags(1),
        "send_gx": flags(zs),
        "recv_gx": flags(zs),
        "send_gy": flags(zs),
        "recv_gy": flags(zs),
        "send_gz": flags(zs),
        "recv_gz": flags(zs),
        "send_gs": flags(seq_count),
        "recv_gs": flags(seq_count),
    }
    names = (
        "points", "counts", "cot", "weights", "momenta", "averages",
        "states", "point_grad", "gradients", "weights_new", "momenta_new", "averages_new",
        *scratch,
    )
    states, point_grad, *vectors = pl.pallas_call(
        functools.partial(whole_kernel, plan, names),
        out_shape=outs,
        in_specs=[vmem, smem, vmem, vmem, vmem, vmem],
        out_specs=(vmem,) * len(outs),
        scratch_shapes=list(scratch.values()),
        compiler_params=pltpu.CompilerParams(
            collective_id=0, has_side_effects=True, vmem_limit_bytes=63 * 1024 * 1024
        ),
    )(
        points[0], counts, cotangent[0],
        weights.reshape(lines), momenta.reshape(lines), averages.reshape(lines),
    )
    return (states[None], point_grad[None], *(v.reshape(-1) for v in vectors))


def solution(mesh):
    placed = (P("dp", "seq", None), P("dp"), P("dp", "seq", None), P("dp"), P("dp"), P("dp"))
    return jax.shard_map(
        shards,
        mesh=mesh,
        in_specs=placed,
        out_specs=(P("dp", "seq", None), P("dp", "seq", None), P("dp"), P("dp"), P("dp"), P("dp")),
        check_vma=False,
    )
```

```python
import functools
import math

import jax
import jax.numpy as jnp
from jax import lax
from jax.experimental import pallas as pl
from jax.experimental.pallas import tpu as pltpu
from jax.sharding import PartitionSpec as P

MESH = pl.DeviceIdType.MESH
HEADS = 8
FF = 1024
LAYERS = 2
LOOPS = 2
APPS = LAYERS * LOOPS

EPSILON = 1e-05
RATE = 0.0003
MOMENTUM = 0.5
AVERAGE_DECAY = 0.9

F32 = jnp.float32
BF16 = jnp.bfloat16
GELU_A = math.sqrt(2.0 / math.pi)
GELU_B = 0.044715
LOCAL = (
    "gnorm", "hid", "nrm", "qsave", "kv", "kt", "vt", "att", "osave", "lse", "upd", "nrm2", "gp", "act", "emb", "qmask", "domask", "ps", "ds", "dqkv", "grad_low", "peak", "total", "gbuf", "gemb", "gin", "send_n", "recv_n", "send_g", "recv_g",
)


def mm(left, right):
    return jnp.dot(left, right, preferred_element_type=F32)


def mm_nt(left, right):
    return lax.dot_general(left, right, (((1,), (1,)), ((), ())), preferred_element_type=F32)


def twice(column):
    column = column.astype(F32)
    return jnp.concatenate([column, column], axis=1)


def halves(values):
    return values[:, :128] + values[:, 128:]


def normalise(values):
    centred = values - jnp.mean(values, axis=0, keepdims=True)
    variance = jnp.mean(centred * centred, axis=0, keepdims=True)
    scale = lax.rsqrt(variance + EPSILON)
    return centred * scale, scale


def normalise_back(grad, unit, scale, gain):
    scaled = grad * gain
    first = jnp.mean(scaled, axis=0, keepdims=True)
    second = jnp.mean(scaled * unit, axis=0, keepdims=True)
    return (scaled - first - unit * second) * scale


class Plan:
    def __init__(self, rows, depth, width, share, dp_count, seq_count):
        self.rows = rows
        self.depth = depth
        self.width = width
        self.hidden = FF
        self.dp = dp_count
        self.zs = dp_count // 2
        self.seq = seq_count
        self.flat = share // width
        self.half = -(-self.flat // 32) * 16
        self.block = 4 + 3 * width + width + FF + FF // width + FF
        self.total = self.flat * dp_count
        self.space = self.total + 32 + width

    def base(self, layer):
        return self.depth + 1 + layer * self.block


def whole_kernel(plan, names, *refs):
    ref = dict(zip(names, refs, strict=True))
    (
        points, counts, cot, weights, states, point_grad, gradients,
    ) = (ref[name] for name in names[:7])
    rows, width, hidden = plan.rows, plan.width, plan.hidden
    seq_count, dp_count, zs, half = plan.seq, plan.dp, plan.zs, plan.half
    head_width = width // HEADS
    exp_scale = math.log2(math.e) / math.sqrt(head_width)
    score_scale = 1.0 / math.sqrt(head_width)
    low_half, high_half = half, plan.flat - half

    me = lax.axis_index("seq")
    owner = lax.axis_index("dp")
    my_z, my_x = owner // 2, lax.rem(owner, 2)
    my_y, my_c = me // 2, lax.rem(me, 2)
    sibling = {"seq": my_y * 2 + (1 - my_c)}
    across = {"seq": (1 - my_y) * 2 + my_c}
    beside = {"dp": my_z * 2 + (1 - my_x)}

    barrier = pltpu.get_barrier_semaphore()

    def greet(device):
        pl.semaphore_signal(barrier, inc=1, device_id=device, device_id_type=MESH)

    for step in range(1, seq_count):
        greet({"seq": lax.rem(me + step, seq_count)})
    greet(beside)

    def greet_z(step, carry):
        greet({"dp": lax.rem(my_z + step, zs) * 2 + my_x})
        return carry

    lax.fori_loop(1, zs, greet_z, 0)

    def remote(source, target, send, receive, device):
        return pltpu.make_async_remote_copy(
            src_ref=source, dst_ref=target, send_sem=send, recv_sem=receive,
            device_id=device, device_id_type=MESH,
        )

    gathered = ref["gathered"]
    tail_rows = high_half // 16 * 16
    for h in range(2):
        for r, count in ((0, low_half), (1, tail_rows)):
            gathered[owner, h, r, :count] = weights[
                pl.ds(2 * r * half + h, count, stride=2), :
            ].astype(BF16)
        if high_half < half:
            gathered[owner, h, 1, tail_rows:] = jnp.concatenate(
                [
                    weights[pl.ds(2 * (half + tail_rows) + h, high_half - tail_rows, stride=2), :],
                    jnp.zeros((half - high_half, 128), F32),
                ],
                axis=0,
            ).astype(BF16)

    pl.semaphore_wait(barrier, seq_count - 1 + zs)

    def along_z(source_z, target_z):
        piece = gathered.at[2 * source_z + my_x, my_c, my_y]
        return remote(
            piece, piece, ref["send_wz"].at[target_z], ref["recv_wz"].at[source_z],
            {"dp": 2 * target_z + my_x},
        )

    def along_y(z, part):
        piece = gathered.at[2 * z + my_x, my_c, part]
        return remote(piece, piece, ref["send_wy"].at[z], ref["recv_wy"].at[z], across)

    def along_x(z, x, part):
        piece = gathered.at[2 * z + x, my_c, part]
        return remote(
            piece, piece, ref["send_wx"].at[z, part], ref["recv_wx"].at[z, part], beside
        )

    def along_c(share, column):
        piece = gathered.at[share, column]
        return remote(piece, piece, ref["send_wc"].at[share], ref["recv_wc"].at[share], sibling)

    def each_z(body):
        def step(z, carry):
            body(z)
            return carry

        lax.fori_loop(0, zs, step, 0)

    def each_other_z(body):
        def step(z, carry):
            @pl.when(z != my_z)
            def _():
                body(z)

            return carry

        lax.fori_loop(0, zs, step, 0)

    each_other_z(lambda z: along_z(my_z, z).start())
    along_x(my_z, my_x, 0).start()
    along_x(my_z, my_x, 1).start()

    def second(z):
        along_z(z, my_z).wait_recv()
        along_y(z, my_y).start()
        along_x(z, my_x, my_y).start()

    def third(z):
        along_y(z, 1 - my_y).wait_recv()
        along_x(z, my_x, 1 - my_y).start()
        along_c(2 * z + my_x, my_c).start()

    def fourth(z):
        along_x(z, 1 - my_x, 0).wait_recv()
        along_x(z, 1 - my_x, 1).wait_recv()
        along_c(2 * z + 1 - my_x, my_c).start()

    def fifth(z):
        @pl.when(z != my_z)
        def _():
            along_c(2 * z + my_x, 1 - my_c).wait_recv()

        along_c(2 * z + 1 - my_x, 1 - my_c).wait_recv()

    each_other_z(second)
    each_other_z(third)
    each_z(fourth)
    each_z(fifth)

    flat = ref["flat"]
    for share in range(dp_count):
        for h in range(2):
            for r in range(2):
                flat[h, pl.ds(share * plan.flat + r * half, half), :] = gathered[
                    share, h, r
                ].astype(F32)

    rin, rit, rbias, norms, bup = (ref[n] for n in ("rin", "rit", "rbias", "norms", "bup"))
    wqkv, wqkv_t, wo, wo_t = (ref[n] for n in ("wqkv", "wqkv_t", "wo", "wo_t"))
    wup, wup_t, wd, wd_t = (ref[n] for n in ("wup", "wup_t", "wd", "wd_t"))
    depth_row = lax.broadcasted_iota(jnp.int32, (128, 128), 0)
    for h in range(2):
        lanes = slice(128 * h, 128 * (h + 1))
        block = flat[h, :128]
        turned = jnp.transpose(block)
        rbias[lanes] = jnp.broadcast_to(turned[:, plan.depth : plan.depth + 1], (128, 128))
        block = jnp.where(depth_row < plan.depth, block, 0.0)
        rin[:, lanes] = block.astype(BF16)
        rit[lanes] = jnp.transpose(block).astype(BF16)
        for layer in range(LAYERS):
            base = plan.base(layer)
            turned = jnp.transpose(flat[h, pl.ds(base, 128), :])
            for j in range(4):
                norms[layer, j, lanes] = jnp.broadcast_to(
                    turned[:, j : j + 1], (128, 128)
                ).astype(BF16)
            base += 4
            for j in range(3):
                value = flat[h, pl.ds(base + j, width, stride=3), :]
                place = slice(width * j + 128 * h, width * j + 128 * (h + 1))
                wqkv[layer, :, place] = value.astype(BF16)
                wqkv_t[layer, place] = jnp.transpose(value).astype(BF16)
            base += 3 * width
            value = flat[h, pl.ds(base, width), :]
            wo[layer, :, lanes] = value.astype(BF16)
            wo_t[layer, lanes] = jnp.transpose(value).astype(BF16)
            base += width
            parts = hidden // width
            for j in range(parts):
                value = flat[h, pl.ds(base + j, width, stride=parts), :]
                place = slice(width * j + 128 * h, width * j + 128 * (h + 1))
                wup[layer, :, place] = value.astype(BF16)
                wup_t[layer, place] = jnp.transpose(value).astype(BF16)
            base += hidden
            turned = jnp.transpose(flat[h, pl.ds(base, 128), :])
            for j in range(parts):
                bup[layer, width * j + 128 * h : width * j + 128 * (h + 1)] = jnp.broadcast_to(
                    turned[:, j : j + 1], (128, 128)
                ).astype(BF16)
            base += parts
            value = flat[h, pl.ds(base, hidden), :]
            wd[layer, :, lanes] = value.astype(BF16)
            wd_t[layer, lanes] = jnp.transpose(value).astype(BF16)

    depth_mask = lax.broadcasted_iota(jnp.int32, (plan.depth, rows), 0) < counts[0]
    wide_points = ref["wide_points"]
    wide_points[...] = jnp.zeros_like(wide_points)
    wide_points[: plan.depth] = jnp.where(depth_mask, points[...].astype(F32), 0.0)
    masked_t = wide_points[...].astype(BF16)
    ref["masked_t"][...] = masked_t

    (
        gnorm, hid, nrm, qsave, kv, kt, vt, att, osave, lse, upd, nrm2, gp, act, emb, qmask, domask, ps, ds, dqkv, grad_low, peak, total, gbuf, gemb, gin, send_n, recv_n, send_g, recv_g,
    ) = (ref[n] for n in LOCAL)
    qmask[...] = jnp.zeros_like(qmask)
    domask[...] = jnp.zeros_like(domask)
    for sums in (gnorm, flat):
        sums[...] = jnp.zeros_like(sums)
    parts = hidden // width

    def accumulate(layer, offset, stride, value):
        start = plan.base(0) + layer * plan.block + offset
        count = value.shape[0]
        for h in range(2):
            lanes = slice(128 * h, 128 * (h + 1))
            flat[h, pl.ds(start, count, stride=stride), :] += value[:, lanes]

    ones = jnp.ones((16, rows), BF16)

    embedded = mm(rit[...], ref["masked_t"][...]) + twice(rbias[...])
    emb[...] = embedded
    hid[0] = embedded

    def normed_copy(app, source, target):
        return pltpu.make_async_remote_copy(
            src_ref=nrm.at[app, source],
            dst_ref=nrm.at[app, source],
            send_sem=send_n.at[app, target],
            recv_sem=recv_n.at[app, source],
            device_id={"seq": target},
            device_id_type=MESH,
        )

    def grad_copy(app, source, target):
        return pltpu.make_async_remote_copy(
            src_ref=nrm.at[app, target],
            dst_ref=nrm.at[app, source],
            send_sem=send_g.at[app, target],
            recv_sem=recv_g.at[app, source],
            device_id={"seq": target},
            device_id_type=MESH,
        )

    causal = lax.broadcasted_iota(jnp.int32, (rows, rows), 0) <= lax.broadcasted_iota(
        jnp.int32, (rows, rows), 1
    )

    def mask_last(values, fill):
        before = values.shape[0] - rows
        last_block = jnp.where(causal, values[before:], fill)
        return jnp.concatenate([values[:before], last_block], axis=0) if before else last_block

    def project_block(app, layer, block):
        block_t = nrm[app, block]
        places = slice(block * rows, (block + 1) * rows)
        both = mm(wqkv_t[layer, width:], block_t).astype(BF16)
        kt[app, :, places] = both[:width]
        vt[:, places] = both[width:]
        kv[app, places] = mm(
            jnp.transpose(block_t.astype(F32)).astype(BF16), wqkv[layer, :, width:]
        ).astype(BF16)

    def attend(app, blocks):
        keys = blocks * rows
        for head in range(HEADS):
            lanes = slice(head * head_width, (head + 1) * head_width)
            scores = mm(kv[app, :keys, :width], qmask[head]) * exp_scale
            scores = mask_last(scores, -jnp.inf)
            top = jnp.max(scores, axis=0, keepdims=True)
            weight = jnp.exp2(scores - top)
            peak[head : head + 1] = top
            total[head : head + 1] = jnp.sum(weight, axis=0, keepdims=True)
            ps[head, :keys] = weight.astype(BF16)
        for head in range(HEADS):
            lanes = slice(head * head_width, (head + 1) * head_width)
            out = mm(vt[lanes, :keys], ps[head, :keys]) * (1.0 / total[head : head + 1])
            osave[app, lanes] = out
            att[app, lanes] = out.astype(BF16)
        lse[app] = peak[...] + jnp.log2(total[...])

    def forward(app, carry):
        layer = lax.rem(app, LAYERS)
        unit, _ = normalise(hid[app])
        normed = (unit * twice(norms[layer, 0]) + twice(norms[layer, 1])).astype(BF16)
        nrm[app, me] = normed
        for step in range(1, seq_count):

            @pl.when(me + step < seq_count)
            def _():
                normed_copy(app, me, me + step).start()

        queries = mm(wqkv_t[layer, :width], normed).astype(BF16)
        qsave[app] = queries
        for head in range(HEADS):
            lanes = slice(head * head_width, (head + 1) * head_width)
            qmask[head, lanes] = queries[lanes]
        for place in range(seq_count):

            @pl.when(me == place)
            def _(place=place):
                project_block(app, layer, place)
                for block in range(place):
                    normed_copy(app, block, me).wait_recv()
                    project_block(app, layer, block)
                attend(app, place + 1)

        updated = hid[app] + mm(wo_t[layer], att[app])
        upd[app] = updated
        unit, _ = normalise(updated)
        second = (unit * twice(norms[layer, 2]) + twice(norms[layer, 3])).astype(BF16)
        nrm2[app] = second
        before = mm(wup_t[layer], second) + twice(bup[layer])
        squared = before * before
        inner = GELU_A * before * (1.0 + GELU_B * squared)
        turned = jnp.tanh(inner)
        half = 0.5 * (1.0 + turned)
        activated = (before * half).astype(BF16)
        act[app] = activated
        gp[app] = half + (0.5 * GELU_A) * before * (1.0 - turned * turned) * (
            1.0 + (3.0 * GELU_B) * squared
        )
        result = upd[app] + mm(wd_t[layer], act[app])
        again = jnp.where((layer == LAYERS - 1) & (app < APPS - 1), 1.0, 0.0)
        hid[app + 1] = result + again * emb[...]
        return carry

    lax.fori_loop(0, APPS, forward, 0)
    states[...] = jnp.transpose(hid[APPS]).astype(BF16)

    gbuf[...] = jnp.transpose(cot[...].astype(F32))
    gemb[...] = jnp.zeros_like(gemb)

    def attend_back(app, layer, blocks):
        keys = blocks * rows
        own = slice(keys - rows, keys)
        for head in range(HEADS):
            scores = mm(kv[app, :keys, :width], qmask[head]) * exp_scale
            weight = jnp.exp2(scores - lse[app, head : head + 1])
            weight = mask_last(weight, 0.0)
            ps[head, :keys] = weight.astype(BF16)
            grad = mm(kv[app, :keys, width:], domask[head])
            ds[head, :keys] = (weight * (grad - total[head : head + 1])).astype(BF16)
        for head in range(HEADS):
            lanes = slice(head * head_width, (head + 1) * head_width)
            below = slice(width + head * head_width, width + (head + 1) * head_width)
            last_rows = slice(2 * width + head * head_width, 2 * width + (head + 1) * head_width)
            dqkv[lanes, own] = (mm(kt[app, lanes, :keys], ds[head, :keys]) * score_scale).astype(BF16)
            dqkv[below, :keys] = (
                mm_nt(qsave[app, lanes], ds[head, :keys]) * score_scale
            ).astype(BF16)
            dqkv[last_rows, :keys] = mm_nt(grad_low[lanes], ps[head, :keys]).astype(BF16)
        for block in range(blocks):
            places = slice(block * rows, (block + 1) * rows)
            first = 0 if block == blocks - 1 else width
            grads = mm_nt(nrm[app, block], dqkv[first:, places])
            for j in range(first // width, 3):
                accumulate(layer, 4 + j, 3, grads[:, width * j - first : width * (j + 1) - first])
            back = mm(wqkv[layer, :, first:], dqkv[first:, places])
            if block == blocks - 1:
                gin[...] = back
            else:
                nrm[app, block] = back.astype(BF16)
                grad_copy(app, me, block).start()

    def backward(order, carry):
        app = APPS - 1 - order
        layer = lax.rem(app, LAYERS)
        grad_out = gbuf[...]
        out_low = grad_out.astype(BF16)
        accumulate(layer, 4 + 4 * width + hidden + parts, 1, mm_nt(act[app], out_low))
        pre_low = (mm(wd[layer], out_low) * gp[app]).astype(BF16)
        act[app] = pre_low
        for j in range(parts):
            part = act[app, width * j : width * (j + 1)]
            accumulate(layer, 4 + 4 * width + j, parts, mm_nt(nrm2[app], part))
            accumulate(layer, 4 + 4 * width + hidden + j, 1, mm_nt(ones, part)[:1])
        grad_second = mm(wup[layer], act[app])
        unit, scale = normalise(upd[app])
        gnorm[layer, 2] += halves(grad_second * unit)
        gnorm[layer, 3] += halves(grad_second)
        grad_updated = gbuf[...] + normalise_back(grad_second, unit, scale, twice(norms[layer, 2]))
        gbuf[...] = grad_updated
        branch_low = grad_updated.astype(BF16)
        accumulate(layer, 4 + 3 * width, 1, mm_nt(att[app], branch_low))
        grad_att = mm(wo[layer], branch_low).astype(BF16)
        grad_low[...] = grad_att
        for head in range(HEADS):
            lanes = slice(head * head_width, (head + 1) * head_width)
            domask[head, lanes] = grad_att[lanes]
            qmask[head, lanes] = qsave[app, lanes]
            total[head : head + 1] = jnp.sum(
                osave[app, lanes] * grad_att[lanes].astype(F32), axis=0, keepdims=True
            )
        for place in range(seq_count):

            @pl.when(me == place)
            def _(place=place):
                attend_back(app, layer, place + 1)

        def later(source, inner):
            grad_copy(app, source, me).wait_recv()
            gin[...] += nrm[app, source].astype(F32)
            return inner

        lax.fori_loop(me + 1, seq_count, later, 0)
        grad_normed = gin[...]
        unit, scale = normalise(hid[app])
        gnorm[layer, 0] += halves(grad_normed * unit)
        gnorm[layer, 1] += halves(grad_normed)
        grad_in = gbuf[...] + normalise_back(grad_normed, unit, scale, twice(norms[layer, 0]))
        gbuf[...] = grad_in
        first = jnp.where(layer == 0, 1.0, 0.0)
        gemb[...] += first * grad_in
        return carry

    lax.fori_loop(0, APPS, backward, 0)

    embed_low = gemb[...].astype(BF16)
    grad_in_rows = mm_nt(ref["masked_t"][...], embed_low)
    grad_bias_rows = mm_nt(ones, embed_low)
    point_grad[...] = jnp.where(depth_mask, mm(rin[...], embed_low)[: plan.depth], 0.0)
    for h in range(2):
        lanes = slice(128 * h, 128 * (h + 1))
        flat[h, : plan.depth] = grad_in_rows[: plan.depth, lanes]
        flat[h, plan.depth : plan.depth + 1] = grad_bias_rows[:1, lanes]
        for layer in range(LAYERS):
            base = plan.base(layer)
            for j in range(4):
                flat[h, base + j : base + j + 1] = jnp.sum(
                    jnp.transpose(gnorm[layer, j, lanes]), axis=0, keepdims=True
                )

    each_other_z(lambda z: along_z(my_z, z).wait_send())
    each_other_z(lambda z: along_y(z, my_y).wait_send())
    for r in range(2):
        each_z(lambda z, r=r: along_x(z, my_x, r).wait_send())
    each_other_z(lambda z: along_c(2 * z + my_x, my_c).wait_send())
    each_z(lambda z: along_c(2 * z + 1 - my_x, my_c).wait_send())
    parts_low = ref["gathered"]
    for share in range(dp_count):
        for h in range(2):
            for r in range(2):
                parts_low[share, h, r] = flat[
                    h, pl.ds(share * plan.flat + r * half, half), :
                ].astype(BF16)

    from_core, from_x, from_y, from_z = (
        ref[n] for n in ("from_core", "from_x", "from_y", "from_z")
    )
    copy = remote(
        parts_low.at[:, 1 - my_c], from_core, ref["send_gc"].at[0], ref["recv_gc"].at[0], sibling
    )
    copy.start()
    copy.wait()

    def add(target, source):
        target[...] = (target[...].astype(F32) + source[...].astype(F32)).astype(BF16)

    def add_core(share, carry):
        for r in range(2):
            add(parts_low.at[share, my_c, r], from_core.at[share, r])
        return carry

    lax.fori_loop(0, dp_count, add_core, 0)

    def grad_x(z):
        return remote(
            parts_low.at[2 * z + 1 - my_x, my_c], from_x.at[z],
            ref["send_gx"].at[z], ref["recv_gx"].at[z], beside,
        )

    def grad_y(z):
        return remote(
            parts_low.at[2 * z + my_x, my_c, 1 - my_y], from_y.at[z],
            ref["send_gy"].at[z], ref["recv_gy"].at[z], across,
        )

    def grad_z(source_z, target_z):
        return remote(
            parts_low.at[2 * target_z + my_x, my_c, my_y], from_z.at[source_z],
            ref["send_gz"].at[target_z], ref["recv_gz"].at[source_z], {"dp": 2 * target_z + my_x},
        )

    each_z(lambda z: grad_x(z).start())

    def after_x(z):
        grad_x(z).wait()
        for r in range(2):
            add(parts_low.at[2 * z + my_x, my_c, r], from_x.at[z, r])
        grad_y(z).start()

    each_z(after_x)

    def after_y(z):
        grad_y(z).wait()
        add(parts_low.at[2 * z + my_x, my_c, my_y], from_y.at[z])

        @pl.when(z != my_z)
        def _():
            grad_z(my_z, z).start()

    each_z(after_y)
    last = ref["last"]
    last[...] = parts_low[owner, my_c, my_y].astype(F32)

    def after_z(z):
        grad_z(z, my_z).wait_recv()
        last[...] += from_z[z].astype(F32)

    each_other_z(after_z)
    summed = ref["summed"]
    summed[my_c, my_y] = last[...].astype(BF16)

    def share_seq(source, target):
        piece = summed.at[lax.rem(source, 2), source // 2]
        return remote(
            piece, piece, ref["send_gs"].at[target], ref["recv_gs"].at[source], {"seq": target}
        )

    for step in range(1, seq_count):
        share_seq(me, lax.rem(me + step, seq_count)).start()
    for step in range(1, seq_count):
        share_seq(lax.rem(me + step, seq_count), me).wait_recv()
    for h in range(2):
        for r, count in ((0, low_half), (1, high_half)):
            ref["shared"][pl.ds(2 * r * half + h, count, stride=2), :] = summed[h, r].astype(F32)[
                :count
            ]
    gradients[...] = ref["shared"][...].astype(BF16)

    each_other_z(lambda z: grad_z(my_z, z).wait_send())
    for step in range(1, seq_count):
        share_seq(me, lax.rem(me + step, seq_count)).wait_send()

    def finish(app, carry):
        def sent_normed(target, inner):
            normed_copy(app, me, target).wait_send()
            return inner

        def sent_grad(target, inner):
            grad_copy(app, me, target).wait_send()
            return inner

        lax.fori_loop(me + 1, seq_count, sent_normed, 0)
        lax.fori_loop(0, me, sent_grad, 0)
        return carry

    lax.fori_loop(0, APPS, finish, 0)


def shards(points, counts, cotangent, weights, momenta, averages):
    rows, depth = points.shape[1:]
    width = cotangent.shape[2]
    share = weights.shape[0]
    plan = Plan(rows, depth, width, share, lax.axis_size("dp"), lax.axis_size("seq"))
    hidden, seq_count, dp_count, zs, half = plan.hidden, plan.seq, plan.dp, plan.zs, plan.half
    vmem = pl.BlockSpec(memory_space=pltpu.VMEM)
    smem = pl.BlockSpec(memory_space=pltpu.SMEM)
    shape = jax.ShapeDtypeStruct
    lines = (share // 128, 128)
    outs = (shape((rows, width), BF16), shape((depth, rows), F32), shape(lines, BF16))
    low = lambda *dims: pltpu.VMEM(dims, BF16)
    full = lambda *dims: pltpu.VMEM(dims, F32)
    flags = lambda *dims: pltpu.SemaphoreType.DMA(dims)
    scratch = {
        "gathered": low(dp_count, 2, 2, half, 128),
        "flat": full(2, plan.space, 128),
        "rin": low(128, width),
        "rit": low(width, 128),
        "rbias": full(width, 128),
        "norms": low(LAYERS, 4, width, 128),
        "bup": low(LAYERS, hidden, 128),
        "wqkv": low(LAYERS, width, 3 * width),
        "wqkv_t": low(LAYERS, 3 * width, width),
        "wo": low(LAYERS, width, width),
        "wo_t": low(LAYERS, width, width),
        "wup": low(LAYERS, width, hidden),
        "wup_t": low(LAYERS, hidden, width),
        "wd": low(LAYERS, hidden, width),
        "wd_t": low(LAYERS, width, hidden),
        "wide_points": full(128, rows),
        "masked_t": low(128, rows),
        "gnorm": full(LAYERS, 4, width, 128),
        "from_core": low(dp_count, 2, half, 128),
        "from_x": low(zs, 2, half, 128),
        "from_y": low(zs, half, 128),
        "from_z": low(zs, half, 128),
        "last": full(half, 128),
        "summed": low(2, 2, half, 128),
        "shared": full(share // 128, 128),
        "hid": full(APPS + 1, width, rows),
        "nrm": low(APPS, seq_count, width, rows),
        "qsave": low(APPS, width, rows),
        "kv": low(APPS, seq_count * rows, 2 * width),
        "kt": low(APPS, width, seq_count * rows),
        "vt": low(width, seq_count * rows),
        "att": low(APPS, width, rows),
        "osave": full(APPS, width, rows),
        "lse": full(APPS, HEADS, rows),
        "upd": full(APPS, width, rows),
        "nrm2": low(APPS, width, rows),
        "gp": full(APPS, hidden, rows),
        "act": low(APPS, hidden, rows),
        "emb": full(width, rows),
        "qmask": low(HEADS, width, rows),
        "domask": low(HEADS, width, rows),
        "ps": low(HEADS, seq_count * rows, rows),
        "ds": low(HEADS, seq_count * rows, rows),
        "dqkv": low(3 * width, seq_count * rows),
        "grad_low": low(width, rows),
        "peak": full(HEADS, rows),
        "total": full(HEADS, rows),
        "gbuf": full(width, rows),
        "gemb": full(width, rows),
        "gin": full(width, rows),
        "send_n": flags(APPS, seq_count),
        "recv_n": flags(APPS, seq_count),
        "send_g": flags(APPS, seq_count),
        "recv_g": flags(APPS, seq_count),
        "send_wz": flags(zs),
        "recv_wz": flags(zs),
        "send_wy": flags(zs),
        "recv_wy": flags(zs),
        "send_wx": flags(zs, 2),
        "recv_wx": flags(zs, 2),
        "send_wc": flags(dp_count),
        "recv_wc": flags(dp_count),
        "send_gc": flags(1),
        "recv_gc": flags(1),
        "send_gx": flags(zs),
        "recv_gx": flags(zs),
        "send_gy": flags(zs),
        "recv_gy": flags(zs),
        "send_gz": flags(zs),
        "recv_gz": flags(zs),
        "send_gs": flags(seq_count),
        "recv_gs": flags(seq_count),
    }
    names = (
        "points", "counts", "cot", "weights", "states", "point_grad", "gradients",
        *scratch,
    )
    states, point_grad, summed = pl.pallas_call(
        functools.partial(whole_kernel, plan, names),
        out_shape=outs,
        in_specs=[vmem, smem, vmem, vmem],
        out_specs=(vmem,) * len(outs),
        scratch_shapes=list(scratch.values()),
        compiler_params=pltpu.CompilerParams(
            collective_id=0, has_side_effects=True, vmem_limit_bytes=63 * 1024 * 1024
        ),
    )(points[0].T, counts, cotangent[0], weights.reshape(lines))
    grad = summed.astype(F32)
    momentum = MOMENTUM * momenta.reshape(lines) + grad
    fresh = weights.reshape(lines) - RATE * (grad + MOMENTUM * momentum)
    mean = AVERAGE_DECAY * averages.reshape(lines) + (1.0 - AVERAGE_DECAY) * fresh
    return (states[None], point_grad.T[None], *(v.reshape(-1) for v in (grad, fresh, momentum, mean)))


def solution(mesh):
    placed = (P("dp", "seq", None), P("dp"), P("dp", "seq", None), P("dp"), P("dp"), P("dp"))
    return jax.shard_map(
        shards,
        mesh=mesh,
        in_specs=placed,
        out_specs=(P("dp", "seq", None), P("dp", "seq", None), P("dp"), P("dp"), P("dp"), P("dp")),
        check_vma=False,
    )
```

```python
import functools
import math

import jax
import jax.numpy as jnp
from jax import lax
from jax.experimental import pallas as pl
from jax.experimental.pallas import tpu as pltpu
from jax.sharding import PartitionSpec as P

MESH = pl.DeviceIdType.MESH
HEADS = 8
FF = 1024
LAYERS = 2
LOOPS = 2
APPS = LAYERS * LOOPS

EPSILON = 1e-05
RATE = 0.0003
MOMENTUM = 0.5
AVERAGE_DECAY = 0.9

F32 = jnp.float32
BF16 = jnp.bfloat16
GELU_A = math.sqrt(2.0 / math.pi)
GELU_B = 0.044715
SEQ = 4
LOCAL = (
    "gnorm", "hid", "nrm", "qsave", "kv", "kt", "vt", "att", "osave", "lse", "upd", "nrm2", "gp",
    "act", "emb", "qmask", "domask", "ps", "ds", "dqkv", "grad_low", "peak", "total", "gbuf",
    "gemb", "gin", "held", "merge", "send_n", "recv_n", "send_g", "recv_g", "recv_m", "gathered",
    "flat",
)


def mm(left, right):
    return jnp.dot(left, right, preferred_element_type=F32)


def mm_nt(left, right):
    return lax.dot_general(left, right, (((1,), (1,)), ((), ())), preferred_element_type=F32)


def twice(column):
    column = column.astype(F32)
    return jnp.concatenate([column, column], axis=1)


def halves(values):
    return values[:, :128] + values[:, 128:]


def normalise(values):
    centred = values - jnp.mean(values, axis=0, keepdims=True)
    variance = jnp.mean(centred * centred, axis=0, keepdims=True)
    scale = lax.rsqrt(variance + EPSILON)
    return centred * scale, scale


def normalise_back(grad, unit, scale, gain):
    scaled = grad * gain
    first = jnp.mean(scaled, axis=0, keepdims=True)
    second = jnp.mean(scaled * unit, axis=0, keepdims=True)
    return (scaled - first - unit * second) * scale


class Plan:
    def __init__(self, rows, depth, width, share, dp_count, seq_count):
        self.rows = rows
        self.depth = depth
        self.width = width
        self.hidden = FF
        self.dp = dp_count
        self.zs = dp_count // 2
        self.seq = seq_count
        self.flat = share // width
        self.half = -(-self.flat // 32) * 16
        self.mixer = 4 + 3 * width + width
        self.block = self.mixer + FF + FF // width + FF
        self.total = self.flat * dp_count
        self.space = self.total + 32 + width
        self.used = self.base(LAYERS)
        self.reach = {
            (layer, part): min(self.zs, -(-(self.base(layer) + rows_here) // (2 * self.flat)))
            for layer in range(LAYERS)
            for part, rows_here in (("mixer", self.mixer), ("hidden", self.block))
        }
        self.reach[LAYERS - 1, "hidden"] = self.zs

    def base(self, layer):
        return self.depth + 1 + layer * self.block


def whole_kernel(plan, names, *refs):
    ref = dict(zip(names, refs, strict=True))
    (
        points, counts, cot, weights, states, point_grad, gradients,
    ) = (ref[name] for name in names[:7])
    rows, width, hidden = plan.rows, plan.width, plan.hidden
    dp_count, zs, half = plan.dp, plan.zs, plan.half
    head_width = width // HEADS
    exp_scale = math.log2(math.e) / math.sqrt(head_width)
    score_scale = 1.0 / math.sqrt(head_width)
    low_half, high_half = half, plan.flat - half
    (
        gnorm, hid, nrm, qsave, kv, kt, vt, att, osave, lse, upd, nrm2, gp, act, emb, qmask,
        domask, ps, ds, dqkv, grad_low, peak, total, gbuf, gemb, gin, held, merge,
        send_n, recv_n, send_g, recv_g, recv_m, gathered, flat,
    ) = (ref[n] for n in LOCAL)
    rin, rit, rbias, norms, bup = (ref[n] for n in ("rin", "rit", "rbias", "norms", "bup"))
    wqkv, wqkv_t, wo, wo_t = (ref[n] for n in ("wqkv", "wqkv_t", "wo", "wo_t"))
    wup, wup_t, wd, wd_t = (ref[n] for n in ("wup", "wup_t", "wd", "wd_t"))

    me = lax.axis_index("seq")
    owner = lax.axis_index("dp")
    my_z, my_x = owner // 2, lax.rem(owner, 2)
    my_y, my_c = me // 2, lax.rem(me, 2)
    sibling = {"seq": my_y * 2 + (1 - my_c)}
    across = {"seq": (1 - my_y) * 2 + my_c}
    here = my_x * 2 + my_y

    def in_plane(step):
        x = lax.rem(my_x + step // 2, 2)
        y = lax.rem(my_y + step % 2, 2)
        return x, y, {"dp": my_z * 2 + x, "seq": y * 2 + my_c}

    barrier = pltpu.get_barrier_semaphore()

    def greet(device):
        pl.semaphore_signal(barrier, inc=1, device_id=device, device_id_type=MESH)

    def greet_z(step, carry):
        greet({"dp": lax.rem(my_z + step, zs) * 2 + my_x})
        return carry

    for step in range(1, plan.seq):
        greet({"seq": lax.rem(me + step, plan.seq)})
    for step in (2, 3):
        greet(in_plane(step)[2])
    lax.fori_loop(1, zs, greet_z, 0)

    def remote(source, target, send, receive, device):
        return pltpu.make_async_remote_copy(
            src_ref=source, dst_ref=target, send_sem=send, recv_sem=receive,
            device_id=device, device_id_type=MESH,
        )

    def each(low, high, body):
        def step(z, carry):
            body(z)
            return carry

        lax.fori_loop(low, high, step, 0)

    def each_other_z(low, high, body):
        def step(z):
            @pl.when(z != my_z)
            def _():
                body(z)

        each(low, high, step)

    tail_rows = high_half // 16 * 16
    for h in range(2):
        for r, count in ((0, low_half), (1, tail_rows)):
            gathered[owner, h, r, :count] = weights[
                pl.ds(2 * r * half + h, count, stride=2), :
            ].astype(BF16)
        if high_half < half:
            gathered[owner, h, 1, tail_rows:] = jnp.concatenate(
                [
                    weights[pl.ds(2 * (half + tail_rows) + h, high_half - tail_rows, stride=2), :],
                    jnp.zeros((half - high_half, 128), F32),
                ],
                axis=0,
            ).astype(BF16)

    pl.semaphore_wait(barrier, plan.seq + zs)

    def weights_z(source_z, target_z):
        piece = gathered.at[2 * source_z + my_x, my_c, my_y]
        return remote(
            piece, piece, ref["send_wz"].at[target_z], ref["recv_wz"].at[source_z],
            {"dp": 2 * target_z + my_x},
        )

    def weights_plane_out(group, step):
        piece = gathered.at[2 * group + my_x, my_c, my_y]
        _, _, device = in_plane(step)
        return remote(
            piece, piece, ref["send_wp"].at[group, step], ref["recv_wp"].at[group, here], device
        )

    def weights_plane_in(group, step):
        x, y, device = in_plane(step)
        piece = gathered.at[2 * group + x, my_c, y]
        return remote(
            piece, piece, ref["send_wp"].at[group, step], ref["recv_wp"].at[group, x * 2 + y],
            device,
        )

    def weights_core(share, column):
        piece = gathered.at[share, column]
        return remote(piece, piece, ref["send_wc"].at[share], ref["recv_wc"].at[share], sibling)

    def own_group(group):
        @pl.when(group == my_z)
        def _():
            each_other_z(0, zs, lambda z: weights_z(group, z).start())
            for step in (2, 3):
                weights_plane_out(group, step).start()

    def forward_group(group):
        weights_z(group, my_z).wait_recv()
        for step in (1, 2, 3):
            weights_plane_out(group, step).start()

    def spread_group(group):
        own_group(group)

        @pl.when(group != my_z)
        def _():
            forward_group(group)

    def pass_group(group):
        @pl.when(group != my_z)
        def _():
            weights_plane_in(group, 1).wait_recv()
            weights_core(2 * group + my_x, my_c).start()

        for step in (2, 3):
            weights_plane_in(group, step).wait_recv()
        weights_core(2 * group + 1 - my_x, my_c).start()

    def take_group(group):
        @pl.when(group != my_z)
        def _():
            weights_core(2 * group + my_x, 1 - my_c).wait_recv()

        weights_core(2 * group + 1 - my_x, 1 - my_c).wait_recv()

    def unpack(low, high):
        for share in range(2 * low, 2 * high):
            for h in range(2):
                for r in range(2):
                    flat[h, pl.ds(share * plan.flat + r * half, half), :] = gathered[
                        share, h, r
                    ].astype(F32)

    def column_of(turned, j):
        return jnp.broadcast_to(turned[:, j : j + 1], (128, 128)).astype(BF16)

    def mixer_weights(layer):
        for h in range(2):
            lanes = slice(128 * h, 128 * (h + 1))
            base = plan.base(layer)
            turned = jnp.transpose(flat[h, pl.ds(base, 128), :])
            for j in range(4):
                norms[layer, j, lanes] = column_of(turned, j)
            base += 4
            for j in range(3):
                value = flat[h, pl.ds(base + j, width, stride=3), :]
                place = slice(width * j + 128 * h, width * j + 128 * (h + 1))
                wqkv[layer, :, place] = value.astype(BF16)
                wqkv_t[layer, place] = jnp.transpose(value).astype(BF16)
            base += 3 * width
            value = flat[h, pl.ds(base, width), :]
            wo[layer, :, lanes] = value.astype(BF16)
            wo_t[layer, lanes] = jnp.transpose(value).astype(BF16)

    parts = hidden // width

    def hidden_weights(layer):
        for h in range(2):
            lanes = slice(128 * h, 128 * (h + 1))
            base = plan.base(layer) + plan.mixer
            for j in range(parts):
                value = flat[h, pl.ds(base + j, width, stride=parts), :]
                place = slice(width * j + 128 * h, width * j + 128 * (h + 1))
                wup[layer, :, place] = value.astype(BF16)
                wup_t[layer, place] = jnp.transpose(value).astype(BF16)
            base += hidden
            turned = jnp.transpose(flat[h, pl.ds(base, 128), :])
            for j in range(parts):
                place = slice(width * j + 128 * h, width * j + 128 * (h + 1))
                bup[layer, place] = column_of(turned, j)
            base += parts
            value = flat[h, pl.ds(base, hidden), :]
            wd[layer, :, lanes] = value.astype(BF16)
            wd_t[layer, lanes] = jnp.transpose(value).astype(BF16)

    reach_a, reach_b = plan.reach[0, "mixer"], plan.reach[0, "hidden"]
    reach_c, reach_d = plan.reach[1, "mixer"], plan.reach[1, "hidden"]

    each(0, reach_a, spread_group)
    each(reach_a, reach_b, own_group)
    qmask[...] = jnp.zeros_like(qmask)
    domask[...] = jnp.zeros_like(domask)
    gnorm[...] = jnp.zeros_like(gnorm)
    gemb[...] = jnp.zeros_like(gemb)
    ones = jnp.ones((16, rows), BF16)
    depth_mask = lax.broadcasted_iota(jnp.int32, (plan.depth, rows), 0) < counts[0]
    wide_points = ref["wide_points"]
    wide_points[...] = jnp.zeros_like(wide_points)
    wide_points[: plan.depth] = jnp.where(depth_mask, points[...].astype(F32), 0.0)
    ref["masked_t"][...] = wide_points[...].astype(BF16)
    gbuf[...] = jnp.transpose(cot[...].astype(F32))
    each(0, reach_a, pass_group)
    each(0, reach_a, take_group)
    unpack(0, reach_a)

    depth_row = lax.broadcasted_iota(jnp.int32, (128, 128), 0)
    for h in range(2):
        lanes = slice(128 * h, 128 * (h + 1))
        block = flat[h, :128]
        turned = jnp.transpose(block)
        rbias[lanes] = jnp.broadcast_to(turned[:, plan.depth : plan.depth + 1], (128, 128))
        block = jnp.where(depth_row < plan.depth, block, 0.0)
        rin[:, lanes] = block.astype(BF16)
        rit[lanes] = jnp.transpose(block).astype(BF16)
    mixer_weights(0)

    embedded = mm(rit[...], ref["masked_t"][...]) + twice(rbias[...])
    emb[...] = embedded
    hid[0] = embedded

    def normed_copy(app, block, target, slot):
        return remote(
            nrm.at[app, block], nrm.at[app, block], send_n.at[app, slot], recv_n.at[app, block],
            {"seq": target},
        )

    def grad_copy(app, block, target, slot):
        return remote(
            nrm.at[app, block], nrm.at[app, me], send_g.at[app, slot], recv_g.at[app, me],
            {"seq": target},
        )

    def grad_arrival(app, source):
        return remote(
            nrm.at[app, source], nrm.at[app, source], send_g.at[app, 0], recv_g.at[app, source],
            {"seq": source},
        )

    def merge_copy(app, block):
        return remote(nrm.at[app, block], merge.at[app], send_g.at[app, 1], recv_m.at[app], sibling)

    causal = lax.broadcasted_iota(jnp.int32, (rows, rows), 0) <= lax.broadcasted_iota(
        jnp.int32, (rows, rows), 1
    )

    def mask_last(values, fill):
        before = values.shape[0] - rows
        last_block = jnp.where(causal, values[before:], fill)
        return jnp.concatenate([values[:before], last_block], axis=0) if before else last_block

    def project_block(app, layer, block):
        block_t = nrm[app, block]
        places = slice(block * rows, (block + 1) * rows)
        both = mm(wqkv_t[layer, width:], block_t).astype(BF16)
        kt[app, :, places] = both[:width]
        vt[:, places] = both[width:]
        kv[app, places] = mm(
            jnp.transpose(block_t.astype(F32)).astype(BF16), wqkv[layer, :, width:]
        ).astype(BF16)

    def attend(app, blocks):
        keys = blocks * rows
        for head in range(HEADS):
            scores = mm(kv[app, :keys, :width], qmask[head]) * exp_scale
            scores = mask_last(scores, -jnp.inf)
            top = jnp.max(scores, axis=0, keepdims=True)
            weight = jnp.exp2(scores - top)
            peak[head : head + 1] = top
            total[head : head + 1] = jnp.sum(weight, axis=0, keepdims=True)
            ps[head, :keys] = weight.astype(BF16)
        for head in range(HEADS):
            lanes = slice(head * head_width, (head + 1) * head_width)
            out = mm(vt[lanes, :keys], ps[head, :keys]) * (1.0 / total[head : head + 1])
            osave[app, lanes] = out
            att[app, lanes] = out.astype(BF16)
        lse[app] = peak[...] + jnp.log2(total[...])

    def gather_blocks(app, layer, place):
        project_block(app, layer, place)
        if place % 2 == 1:
            normed_copy(app, place - 1, me, 0).wait_recv()
            project_block(app, layer, place - 1)
        if place >= 2:
            near = place - 2
            far = 1 - near
            normed_copy(app, near, me, 0).wait_recv()
            normed_copy(app, near, place + 1 - 2 * (place % 2), 2).start()
            project_block(app, layer, near)
            normed_copy(app, far, me, 0).wait_recv()
            project_block(app, layer, far)

    def forward(app, carry):
        layer = lax.rem(app, LAYERS)

        @pl.when(app == 1)
        def _():
            each(reach_c, reach_d, pass_group)
            each(reach_b, reach_c, take_group)
            unpack(reach_b, reach_c)
            mixer_weights(1)

        unit, _ = normalise(hid[app])
        normed = (unit * twice(norms[layer, 0]) + twice(norms[layer, 1])).astype(BF16)
        nrm[app, me] = normed

        @pl.when(my_y == 0)
        def _():
            normed_copy(app, me, me + 2, 1).start()

        @pl.when(my_c == 0)
        def _():
            normed_copy(app, me, me + 1, 0).start()

        queries = mm(wqkv_t[layer, :width], normed).astype(BF16)
        qsave[app] = queries
        for head in range(HEADS):
            lanes = slice(head * head_width, (head + 1) * head_width)
            qmask[head, lanes] = queries[lanes]

        @pl.when(app == 0)
        def _():
            each_other_z(reach_a, reach_b, forward_group)
            each(reach_b, reach_d, own_group)

        for place in range(SEQ):

            @pl.when(me == place)
            def _(place=place):
                gather_blocks(app, layer, place)
                attend(app, place + 1)

        updated = hid[app] + mm(wo_t[layer], att[app])
        upd[app] = updated
        unit, _ = normalise(updated)
        second = (unit * twice(norms[layer, 2]) + twice(norms[layer, 3])).astype(BF16)
        nrm2[app] = second

        @pl.when(app == 0)
        def _():
            each(reach_a, reach_c, pass_group)
            each_other_z(reach_b, reach_d, forward_group)
            each(reach_a, reach_b, take_group)
            unpack(reach_a, reach_b)
            hidden_weights(0)

        @pl.when(app == 1)
        def _():
            each(reach_c, reach_d, take_group)
            unpack(reach_c, reach_d)
            hidden_weights(1)

        before = mm(wup_t[layer], nrm2[app]) + twice(bup[layer])
        squared = before * before
        inner = GELU_A * before * (1.0 + GELU_B * squared)
        turned = jnp.tanh(inner)
        risen = 0.5 * (1.0 + turned)
        act[app] = (before * risen).astype(BF16)
        gp[app] = risen + (0.5 * GELU_A) * before * (1.0 - turned * turned) * (
            1.0 + (3.0 * GELU_B) * squared
        )
        result = upd[app] + mm(wd_t[layer], act[app])
        again = jnp.where((layer == LAYERS - 1) & (app < APPS - 1), 1.0, 0.0)
        hid[app + 1] = result + again * emb[...]
        return carry

    lax.fori_loop(0, APPS, forward, 0)
    states[...] = jnp.transpose(hid[APPS]).astype(BF16)

    each_other_z(0, zs, lambda z: weights_z(my_z, z).wait_send())
    each_other_z(0, zs, lambda z: weights_plane_out(z, 1).wait_send())
    for step in (2, 3):
        each(0, zs, lambda z, step=step: weights_plane_out(z, step).wait_send())
    each_other_z(0, zs, lambda z: weights_core(2 * z + my_x, my_c).wait_send())
    each(0, zs, lambda z: weights_core(2 * z + 1 - my_x, my_c).wait_send())

    def normed_sent(app):
        @pl.when(my_c == 0)
        def _():
            normed_copy(app, me, me + 1, 0).wait_send()

        @pl.when(my_y == 0)
        def _():
            normed_copy(app, me, me + 2, 1).wait_send()

        @pl.when(my_y == 1)
        def _():
            normed_copy(app, my_c, my_y * 2 + 1 - my_c, 2).wait_send()

    each(0, APPS, normed_sent)
    flat[:, pl.ds(plan.used, plan.total - plan.used), :] = jnp.zeros(
        (2, plan.total - plan.used, 128), F32
    )

    from_core, from_plane, from_z = (ref[n] for n in ("from_core", "from_plane", "from_z"))
    last, summed = ref["last"], ref["summed"]

    def grads_core(group):
        pair = pl.ds(2 * group, 2)
        return remote(
            gathered.at[pair, 1 - my_c], from_core.at[pair],
            ref["send_gc"].at[group], ref["recv_gc"].at[group], sibling,
        )

    def grads_plane(group, step):
        x, y, device = in_plane(step)
        return remote(
            gathered.at[2 * group + x, my_c, y], from_plane.at[group, here],
            ref["send_gp"].at[group, step], ref["recv_gp"].at[group, here], device,
        )

    def grads_plane_in(group, step):
        x, y, device = in_plane(step)
        place = x * 2 + y
        return place, remote(
            gathered.at[2 * group + my_x, my_c, my_y], from_plane.at[group, place],
            ref["send_gp"].at[group, step], ref["recv_gp"].at[group, place], device,
        )

    def grads_z(source_z, target_z):
        return remote(
            gathered.at[2 * target_z + my_x, my_c, my_y], from_z.at[source_z],
            ref["send_gz"].at[target_z], ref["recv_gz"].at[source_z], {"dp": 2 * target_z + my_x},
        )

    def round_group(low, high):
        def body(group):
            for x in range(2):
                for h in range(2):
                    for r in range(2):
                        start = (2 * group + x) * plan.flat + r * half
                        gathered[2 * group + x, h, r] = flat[h, pl.ds(start, half), :].astype(BF16)
            grads_core(group).start()

        each(low, high, body)

    def plane_group(low, high):
        def body(group):
            grads_core(group).wait()
            for step in (3, 2, 1, 0):
                x, y, _ = in_plane(step)
                share = 2 * group + x
                gathered[share, my_c, y] = (
                    gathered[share, my_c, y].astype(F32) + from_core[share, y].astype(F32)
                ).astype(BF16)
                if step:
                    grads_plane(group, step).start()

        each(low, high, body)

    def rise_group(low, high):
        def body(group):
            value = gathered[2 * group + my_x, my_c, my_y].astype(F32)
            for step in (1, 2, 3):
                place, arrival = grads_plane_in(group, step)
                arrival.wait_recv()
                value = value + from_plane[group, place].astype(F32)
            gathered[2 * group + my_x, my_c, my_y] = value.astype(BF16)

            @pl.when(group != my_z)
            def _():
                grads_z(my_z, group).start()

            @pl.when(group == my_z)
            def _():
                last[...] = value

        each(low, high, body)

    def share_seq(source, target):
        piece = summed.at[lax.rem(source, 2), source // 2]
        return remote(
            piece, piece, ref["send_gs"].at[target], ref["recv_gs"].at[source], {"seq": target}
        )

    def collect(low, high):
        def body(z):
            grads_z(z, my_z).wait_recv()
            last[...] += from_z[z].astype(F32)

        def when_mine(group):
            @pl.when(group == my_z)
            def _():
                each_other_z(0, zs, body)
                summed[my_c, my_y] = last[...].astype(BF16)
                for step in range(1, SEQ):
                    share_seq(me, lax.rem(me + step, SEQ)).start()

        each(low, high, when_mine)

    def first_group(row):
        return min(zs, -(-row // (2 * plan.flat)))

    group_a = first_group(plan.base(1) + plan.mixer)
    group_b = first_group(plan.base(0) + plan.mixer)

    def accumulate(app, layer, offset, stride, value, again=False):
        start = plan.base(0) + layer * plan.block + offset
        count = value.shape[0]
        for h in range(2):
            place = (h, pl.ds(start, count, stride=stride), slice(None))
            part = value[:, 128 * h : 128 * (h + 1)]
            kept = flat[place]
            flat[place] = part + (kept if again else jnp.where(app < LAYERS, kept, 0.0))

    def attend_back(app, layer, blocks):
        keys = blocks * rows
        own = slice(keys - rows, keys)
        for head in range(HEADS):
            scores = mm(kv[app, :keys, :width], qmask[head]) * exp_scale
            weight = jnp.exp2(scores - lse[app, head : head + 1])
            weight = mask_last(weight, 0.0)
            ps[head, :keys] = weight.astype(BF16)
            grad = mm(kv[app, :keys, width:], domask[head])
            ds[head, :keys] = (weight * (grad - total[head : head + 1])).astype(BF16)
        for head in range(HEADS):
            lanes = slice(head * head_width, (head + 1) * head_width)
            key_lanes = slice(width + head * head_width, width + (head + 1) * head_width)
            value_lanes = slice(2 * width + head * head_width, 2 * width + (head + 1) * head_width)
            dqkv[lanes, own] = (mm(kt[app, lanes, :keys], ds[head, :keys]) * score_scale).astype(BF16)
            dqkv[key_lanes, :keys] = (
                mm_nt(qsave[app, lanes], ds[head, :keys]) * score_scale
            ).astype(BF16)
            dqkv[value_lanes, :keys] = mm_nt(grad_low[lanes], ps[head, :keys]).astype(BF16)
        place = blocks - 1
        order = [b for b in (1 - place % 2, place - 2, place - 1) if 0 <= b < place]
        order = [*dict.fromkeys(order), place]
        for block in order:
            places = slice(block * rows, (block + 1) * rows)
            first = 0 if block == place else width
            grads = mm_nt(nrm[app, block], dqkv[first:, places])
            for j in range(first // width, 3):
                accumulate(
                    app, layer, 4 + j, 3, grads[:, width * j - first : width * (j + 1) - first],
                    again=j > 0 and block != order[0],
                )
            back = mm(wqkv[layer, :, first:], dqkv[first:, places])
            if block == place:
                gin[...] = back
            elif block == place - 2:
                held[...] = back
            else:
                nrm[app, block] = back.astype(BF16)
                if place >= 2 and block == 1 - place % 2:
                    merge_copy(app, block).start()
                else:
                    grad_copy(app, block, block, 0).start()

    def flush_norms(layer):
        start = plan.base(0) + layer * plan.block
        for h in range(2):
            for j in range(4):
                flat[h, pl.ds(start + j, 1), :] = jnp.sum(
                    jnp.transpose(gnorm[layer, j, 128 * h : 128 * (h + 1)]), axis=0, keepdims=True
                )

    def backward(order, carry):
        app = APPS - 1 - order
        layer = lax.rem(app, LAYERS)
        out_low = gbuf[...].astype(BF16)
        accumulate(app, layer, plan.mixer + hidden + parts, 1, mm_nt(act[app], out_low))
        pre_low = (mm(wd[layer], out_low) * gp[app]).astype(BF16)
        act[app] = pre_low
        for j in range(parts):
            part = act[app, width * j : width * (j + 1)]
            accumulate(app, layer, plan.mixer + j, parts, mm_nt(nrm2[app], part))
            accumulate(app, layer, plan.mixer + hidden + j, 1, mm_nt(ones, part)[:1])

        @pl.when(app == 1)
        def _():
            round_group(group_a, zs)

        @pl.when(app == 0)
        def _():
            rise_group(group_a, zs)
            round_group(group_b, group_a)

        grad_second = mm(wup[layer], act[app])
        unit, scale = normalise(upd[app])
        gnorm[layer, 2] += halves(grad_second * unit)
        gnorm[layer, 3] += halves(grad_second)
        grad_updated = gbuf[...] + normalise_back(grad_second, unit, scale, twice(norms[layer, 2]))
        gbuf[...] = grad_updated
        branch_low = grad_updated.astype(BF16)
        accumulate(app, layer, 4 + 3 * width, 1, mm_nt(att[app], branch_low))
        grad_att = mm(wo[layer], branch_low).astype(BF16)
        grad_low[...] = grad_att
        for head in range(HEADS):
            lanes = slice(head * head_width, (head + 1) * head_width)
            domask[head, lanes] = grad_att[lanes]
            qmask[head, lanes] = qsave[app, lanes]
            total[head : head + 1] = jnp.sum(
                osave[app, lanes] * grad_att[lanes].astype(F32), axis=0, keepdims=True
            )

        @pl.when(app == 1)
        def _():
            plane_group(group_a, zs)

        @pl.when(app == 0)
        def _():
            plane_group(group_b, group_a)

        for place in range(SEQ):

            @pl.when(me == place)
            def _(place=place):
                attend_back(app, layer, place + 1)

        def arrive(source):
            grad_arrival(app, source).wait_recv()
            gin[...] += nrm[app, source].astype(F32)

        @pl.when(my_c == 0)
        def _():
            arrive(me + 1)

        @pl.when(my_y == 0)
        def _():
            arrive(me + 2)

        grad_normed = gin[...]
        unit, scale = normalise(hid[app])
        gnorm[layer, 0] += halves(grad_normed * unit)
        gnorm[layer, 1] += halves(grad_normed)
        grad_in = gbuf[...] + normalise_back(grad_normed, unit, scale, twice(norms[layer, 0]))
        gbuf[...] = grad_in
        first = jnp.where(layer == 0, 1.0, 0.0)
        gemb[...] += first * grad_in

        @pl.when(my_y == 1)
        def _():
            merge_copy(app, my_c).wait_recv()
            nrm[app, my_c] = (held[...] + merge[app].astype(F32)).astype(BF16)
            grad_copy(app, my_c, my_c, 2).start()

        @pl.when(app < LAYERS)
        def _():
            flush_norms(layer)

        return carry

    lax.fori_loop(0, APPS, backward, 0)
    embed_low = gemb[...].astype(BF16)
    grad_in_rows = mm_nt(ref["masked_t"][...], embed_low)
    grad_bias_rows = mm_nt(ones, embed_low)
    for h in range(2):
        lanes = slice(128 * h, 128 * (h + 1))
        flat[h, : plan.depth] = grad_in_rows[: plan.depth, lanes]
        flat[h, plan.depth : plan.depth + 1] = grad_bias_rows[:1, lanes]
    round_group(0, group_b)
    point_grad[...] = jnp.where(depth_mask, mm(rin[...], embed_low)[: plan.depth], 0.0)
    rise_group(group_b, group_a)
    plane_group(0, group_b)
    collect(group_b, zs)
    rise_group(0, group_b)
    collect(0, group_b)
    for step in range(1, SEQ):
        share_seq(lax.rem(me + step, SEQ), me).wait_recv()
    for h in range(2):
        for r, count in ((0, low_half), (1, high_half)):
            ref["shared"][pl.ds(2 * r * half + h, count, stride=2), :] = summed[h, r].astype(F32)[
                :count
            ]
    gradients[...] = ref["shared"][...].astype(BF16)

    for step in (1, 2, 3):
        each(0, zs, lambda z, step=step: grads_plane(z, step).wait_send())
    each_other_z(0, zs, lambda z: grads_z(my_z, z).wait_send())
    for step in range(1, SEQ):
        share_seq(me, lax.rem(me + step, SEQ)).wait_send()

    def finish(app):
        @pl.when(my_c == 1)
        def _():
            grad_copy(app, me - 1, me - 1, 0).wait_send()

        @pl.when(my_y == 1)
        def _():
            merge_copy(app, 1 - my_c).wait_send()
            grad_copy(app, my_c, my_c, 2).wait_send()

    each(0, APPS, finish)


def update_kernel(
    summed, weights, momenta, averages, states, point_grad,
    grad_out, fresh_out, momentum_out, mean_out, states_out, point_out,
):
    grad = summed[...].astype(F32)
    momentum = MOMENTUM * momenta[...] + grad
    fresh = weights[...] - RATE * (grad + MOMENTUM * momentum)
    grad_out[...] = grad
    momentum_out[...] = momentum
    fresh_out[...] = fresh
    mean_out[...] = AVERAGE_DECAY * averages[...] + (1.0 - AVERAGE_DECAY) * fresh

    @pl.when(pl.program_id(0) == 0)
    def _():
        states_out[...] = states[...]
        for row in range(point_grad.shape[0]):
            point_out[row] = point_grad[row : row + 1]


def shards(points, counts, cotangent, weights, momenta, averages):
    rows, depth = points.shape[1:]
    width = cotangent.shape[2]
    share = weights.shape[0]
    plan = Plan(rows, depth, width, share, lax.axis_size("dp"), lax.axis_size("seq"))
    hidden, dp_count, zs, half = plan.hidden, plan.dp, plan.zs, plan.half
    vmem = pl.BlockSpec(memory_space=pltpu.VMEM)
    smem = pl.BlockSpec(memory_space=pltpu.SMEM)
    shape = jax.ShapeDtypeStruct
    lines = (share // 128, 128)
    outs = (shape((rows, width), BF16), shape((depth, rows), F32), shape(lines, BF16))
    low = lambda *dims: pltpu.VMEM(dims, BF16)
    full = lambda *dims: pltpu.VMEM(dims, F32)
    flags = lambda *dims: pltpu.SemaphoreType.DMA(dims)
    scratch = {
        "gathered": low(dp_count, 2, 2, half, 128),
        "flat": full(2, plan.space, 128),
        "rin": low(128, width),
        "rit": low(width, 128),
        "rbias": full(width, 128),
        "norms": low(LAYERS, 4, width, 128),
        "bup": low(LAYERS, hidden, 128),
        "wqkv": low(LAYERS, width, 3 * width),
        "wqkv_t": low(LAYERS, 3 * width, width),
        "wo": low(LAYERS, width, width),
        "wo_t": low(LAYERS, width, width),
        "wup": low(LAYERS, width, hidden),
        "wup_t": low(LAYERS, hidden, width),
        "wd": low(LAYERS, hidden, width),
        "wd_t": low(LAYERS, width, hidden),
        "wide_points": full(128, rows),
        "masked_t": low(128, rows),
        "gnorm": full(LAYERS, 4, width, 128),
        "from_core": low(dp_count, 2, half, 128),
        "from_plane": low(zs, 4, half, 128),
        "from_z": low(zs, half, 128),
        "last": full(half, 128),
        "summed": low(2, 2, half, 128),
        "shared": full(share // 128, 128),
        "hid": full(APPS + 1, width, rows),
        "nrm": low(APPS, SEQ, width, rows),
        "qsave": low(APPS, width, rows),
        "kv": low(APPS, SEQ * rows, 2 * width),
        "kt": low(APPS, width, SEQ * rows),
        "vt": low(width, SEQ * rows),
        "att": low(APPS, width, rows),
        "osave": full(APPS, width, rows),
        "lse": full(APPS, HEADS, rows),
        "upd": full(APPS, width, rows),
        "nrm2": low(APPS, width, rows),
        "gp": full(APPS, hidden, rows),
        "act": low(APPS, hidden, rows),
        "emb": full(width, rows),
        "qmask": low(HEADS, width, rows),
        "domask": low(HEADS, width, rows),
        "ps": low(HEADS, SEQ * rows, rows),
        "ds": low(HEADS, SEQ * rows, rows),
        "dqkv": low(3 * width, SEQ * rows),
        "grad_low": low(width, rows),
        "peak": full(HEADS, rows),
        "total": full(HEADS, rows),
        "gbuf": full(width, rows),
        "gemb": full(width, rows),
        "gin": full(width, rows),
        "held": full(width, rows),
        "merge": low(APPS, width, rows),
        "send_n": flags(APPS, 3),
        "recv_n": flags(APPS, SEQ),
        "send_g": flags(APPS, 3),
        "recv_g": flags(APPS, SEQ),
        "recv_m": flags(APPS),
        "send_wz": flags(zs),
        "recv_wz": flags(zs),
        "send_wp": flags(zs, 4),
        "recv_wp": flags(zs, 4),
        "send_wc": flags(dp_count),
        "recv_wc": flags(dp_count),
        "send_gc": flags(zs),
        "recv_gc": flags(zs),
        "send_gp": flags(zs, 4),
        "recv_gp": flags(zs, 4),
        "send_gz": flags(zs),
        "recv_gz": flags(zs),
        "send_gs": flags(SEQ),
        "recv_gs": flags(SEQ),
    }
    names = (
        "points", "counts", "cot", "weights", "states", "point_grad", "gradients", *scratch,
    )
    mine = weights.reshape(lines)
    states, point_grad, summed = pl.pallas_call(
        functools.partial(whole_kernel, plan, names),
        out_shape=outs,
        in_specs=[vmem, smem, vmem, vmem],
        out_specs=(vmem,) * len(outs),
        scratch_shapes=list(scratch.values()),
        compiler_params=pltpu.CompilerParams(
            collective_id=0, has_side_effects=True, vmem_limit_bytes=63 * 1024 * 1024
        ),
    )(points[0].T, counts, cotangent[0], mine)
    vector = shape(lines, F32)
    step_rows = min(512, lines[0])
    line_block = pl.BlockSpec((step_rows, 128), lambda i: (i, 0))
    states_block = pl.BlockSpec((rows, width), lambda i: (0, 0))
    point_block = pl.BlockSpec((depth, rows), lambda i: (0, 0))
    grad, fresh, momentum, mean, states, point_grad = pl.pallas_call(
        update_kernel,
        grid=(-(-lines[0] // step_rows),),
        out_shape=(
            vector, vector, vector, vector, shape((rows, width), BF16), shape((depth, 1, rows), F32),
        ),
        in_specs=[line_block] * 4 + [states_block, point_block],
        out_specs=(
            line_block, line_block, line_block, line_block, states_block,
            pl.BlockSpec((depth, 1, rows), lambda i: (0, 0, 0)),
        ),
        compiler_params=pltpu.CompilerParams(vmem_limit_bytes=63 * 1024 * 1024),
    )(summed, mine, momenta.reshape(lines), averages.reshape(lines), states, point_grad)
    return (
        states[None], jnp.transpose(point_grad, (1, 2, 0)),
        *(v.reshape(-1) for v in (grad, fresh, momentum, mean)),
    )


def solution(mesh):
    placed = (P("dp", "seq", None), P("dp"), P("dp", "seq", None), P("dp"), P("dp"), P("dp"))
    return jax.shard_map(
        shards,
        mesh=mesh,
        in_specs=placed,
        out_specs=(P("dp", "seq", None), P("dp", "seq", None), P("dp"), P("dp"), P("dp"), P("dp")),
        check_vma=False,
    )
```

```python
import functools
import math

import jax
import jax.numpy as jnp
from jax import lax
from jax.experimental import pallas as pl
from jax.experimental.pallas import tpu as pltpu
from jax.sharding import PartitionSpec as P

MESH = pl.DeviceIdType.MESH
HEADS = 8
FF = 1024
LAYERS = 2
LOOPS = 2
APPS = LAYERS * LOOPS

EPSILON = 1e-05
RATE = 0.0003
MOMENTUM = 0.5
AVERAGE_DECAY = 0.9

F32 = jnp.float32
BF16 = jnp.bfloat16
GELU_A = math.sqrt(2.0 / math.pi)
GELU_B = 0.044715
SEQ = 4
LOCAL = (
    "gnorm", "hid", "nrm", "qsave", "kv", "kt", "vt", "att", "osave", "lse", "upd", "nrm2", "gp",
    "act", "emb", "qmask", "domask", "ps", "ds", "dqkv", "grad_low", "peak", "total", "gbuf",
    "gemb", "gin", "merge", "send_n", "recv_n", "send_g", "recv_g", "recv_m", "gathered",
    "flat",
)


def mm(left, right):
    return jnp.dot(left, right, preferred_element_type=F32)


def mm_nt(left, right):
    return lax.dot_general(left, right, (((1,), (1,)), ((), ())), preferred_element_type=F32)


def twice(column):
    column = column.astype(F32)
    return jnp.concatenate([column, column], axis=1)


def halves(values):
    return values[:, :128] + values[:, 128:]


def normalise(values):
    centred = values - jnp.mean(values, axis=0, keepdims=True)
    variance = jnp.mean(centred * centred, axis=0, keepdims=True)
    scale = lax.rsqrt(variance + EPSILON)
    return centred * scale, scale


def normalise_back(grad, unit, scale, gain):
    scaled = grad * gain
    first = jnp.mean(scaled, axis=0, keepdims=True)
    second = jnp.mean(scaled * unit, axis=0, keepdims=True)
    return (scaled - first - unit * second) * scale


class Plan:
    def __init__(self, rows, depth, width, share, dp_count, seq_count):
        self.rows = rows
        self.depth = depth
        self.width = width
        self.hidden = FF
        self.dp = dp_count
        self.zs = dp_count // 2
        self.seq = seq_count
        self.flat = share // width
        self.quarter = -(-self.flat // 64) * 16
        self.mixer = 4 + 3 * width + width
        self.block = self.mixer + FF + FF // width + FF
        self.total = self.flat * dp_count
        self.space = self.total + 64 + width
        self.used = self.base(LAYERS)
        self.reach = {
            (layer, part): min(self.zs, -(-(self.base(layer) + rows_here) // (2 * self.flat)))
            for layer in range(LAYERS)
            for part, rows_here in (("mixer", self.mixer), ("hidden", self.block))
        }
        self.reach[LAYERS - 1, "hidden"] = self.zs

    def base(self, layer):
        return self.depth + 1 + layer * self.block


def whole_kernel(plan, names, *refs):
    ref = dict(zip(names, refs, strict=True))
    (
        points, counts, cot, weights, states, point_grad, gradients,
    ) = (ref[name] for name in names[:7])
    rows, width, hidden = plan.rows, plan.width, plan.hidden
    dp_count, zs, quarter = plan.dp, plan.zs, plan.quarter
    head_width = width // HEADS
    exp_scale = math.log2(math.e) / math.sqrt(head_width)
    score_scale = 1.0 / math.sqrt(head_width)
    quarters = [(r, w, (2 * r + w) * quarter) for r in range(2) for w in range(2)]
    waves = range(2)
    (
        gnorm, hid, nrm, qsave, kv, kt, vt, att, osave, lse, upd, nrm2, gp, act, emb, qmask,
        domask, ps, ds, dqkv, grad_low, peak, total, gbuf, gemb, gin, merge,
        send_n, recv_n, send_g, recv_g, recv_m, gathered, flat,
    ) = (ref[n] for n in LOCAL)
    rin, rit, rbias, norms, bup = (ref[n] for n in ("rin", "rit", "rbias", "norms", "bup"))
    wqkv, wqkv_t, wo, wo_t = (ref[n] for n in ("wqkv", "wqkv_t", "wo", "wo_t"))
    wup, wup_t, wd, wd_t = (ref[n] for n in ("wup", "wup_t", "wd", "wd_t"))

    me = lax.axis_index("seq")
    owner = lax.axis_index("dp")
    my_z, my_x = owner // 2, lax.rem(owner, 2)
    my_y, my_c = me // 2, lax.rem(me, 2)
    sibling = {"seq": my_y * 2 + (1 - my_c)}
    across = {"seq": (1 - my_y) * 2 + my_c}
    here = my_x * 2 + my_y

    def in_plane(step):
        x = lax.rem(my_x + step // 2, 2)
        y = lax.rem(my_y + step % 2, 2)
        return x, y, {"dp": my_z * 2 + x, "seq": y * 2 + my_c}

    barrier = pltpu.get_barrier_semaphore()

    def greet(device):
        pl.semaphore_signal(barrier, inc=1, device_id=device, device_id_type=MESH)

    def greet_z(step, carry):
        greet({"dp": lax.rem(my_z + step, zs) * 2 + my_x})
        return carry

    for step in range(1, plan.seq):
        greet({"seq": lax.rem(me + step, plan.seq)})
    for step in (2, 3):
        greet(in_plane(step)[2])
    lax.fori_loop(1, zs, greet_z, 0)

    def remote(source, target, send, receive, device):
        return pltpu.make_async_remote_copy(
            src_ref=source, dst_ref=target, send_sem=send, recv_sem=receive,
            device_id=device, device_id_type=MESH,
        )

    def each(low, high, body):
        def step(z, carry):
            body(z)
            return carry

        lax.fori_loop(low, high, step, 0)

    def each_other_z(low, high, body):
        def step(z):
            @pl.when(z != my_z)
            def _():
                body(z)

        each(low, high, step)

    for h in range(2):
        for r, w, start in quarters:
            count = min(quarter, plan.flat - start)
            whole_rows = count // 16 * 16
            if whole_rows:
                gathered[owner, h, r, w, :whole_rows] = weights[
                    pl.ds(2 * start + h, whole_rows, stride=2), :
                ].astype(BF16)
            if whole_rows < quarter:
                rest = [jnp.zeros((quarter - count, 128), F32)]
                if whole_rows < count:
                    begin = 2 * (start + whole_rows) + h
                    rest = [weights[pl.ds(begin, count - whole_rows, stride=2), :], *rest]
                gathered[owner, h, r, w, whole_rows:] = jnp.concatenate(rest, axis=0).astype(BF16)

    depth_mask = lax.broadcasted_iota(jnp.int32, (plan.depth, rows), 0) < counts[0]
    gin[...] = jnp.zeros_like(gin)
    gin[: plan.depth] = jnp.where(depth_mask, points[...].astype(F32), 0.0)
    masked_all = ref["masked_all"]
    masked_all[me] = gin[:128].astype(BF16)

    pl.semaphore_wait(barrier, plan.seq + zs)

    def points_copy(source, target):
        piece = masked_all.at[source]
        return remote(
            piece, piece, ref["send_p"].at[target], ref["recv_p"].at[source], {"seq": target}
        )

    for step in range(1, SEQ):

        @pl.when(me + step < SEQ)
        def _(step=step):
            points_copy(me, me + step).start()

    def weights_z(source_z, target_z, w):
        piece = gathered.at[2 * source_z + my_x, my_c, my_y, w]
        return remote(
            piece, piece, ref["send_wz"].at[target_z, w], ref["recv_wz"].at[source_z, w],
            {"dp": 2 * target_z + my_x},
        )

    def weights_plane_out(group, step, w):
        piece = gathered.at[2 * group + my_x, my_c, my_y, w]
        _, _, device = in_plane(step)
        return remote(
            piece, piece, ref["send_wp"].at[group, step, w], ref["recv_wp"].at[group, here, w],
            device,
        )

    def weights_plane_in(group, step, w):
        x, y, device = in_plane(step)
        piece = gathered.at[2 * group + x, my_c, y, w]
        return remote(
            piece, piece, ref["send_wp"].at[group, step, w],
            ref["recv_wp"].at[group, x * 2 + y, w], device,
        )

    def weights_core(share, column, w):
        piece = gathered.at[share, column, :, w]
        return remote(
            piece, piece, ref["send_wc"].at[share, w], ref["recv_wc"].at[share, w], sibling
        )

    def send_near():
        for w in waves:
            for step in (2, 3):
                weights_plane_out(my_z, step, w).start()
        for w in waves:
            each(0, my_z, lambda z, w=w: weights_z(my_z, z, w).start())

    def send_up():
        for w in waves:
            each(0, zs - 1 - my_z, lambda i, w=w: weights_z(my_z, zs - 1 - i, w).start())

    def forward_group(group):
        for w in waves:
            weights_z(group, my_z, w).wait_recv()
            for step in (1, 2, 3):
                weights_plane_out(group, step, w).start()

    def pass_group(group):
        for w in waves:

            @pl.when(group != my_z)
            def _(w=w):
                weights_plane_in(group, 1, w).wait_recv()
                weights_core(2 * group + my_x, my_c, w).start()

            for step in (2, 3):
                weights_plane_in(group, step, w).wait_recv()
            weights_core(2 * group + 1 - my_x, my_c, w).start()

    def take_group(group):
        for w in waves:

            @pl.when(group != my_z)
            def _(w=w):
                weights_core(2 * group + my_x, 1 - my_c, w).wait_recv()

            weights_core(2 * group + 1 - my_x, 1 - my_c, w).wait_recv()

    def unpack(low, high):
        for share in range(2 * low, 2 * high):
            for h in range(2):
                for r, w, start in quarters:
                    flat[h, pl.ds(share * plan.flat + start, quarter), :] = gathered[
                        share, h, r, w
                    ].astype(F32)

    def column_of(turned, j):
        return jnp.broadcast_to(turned[:, j : j + 1], (128, 128)).astype(BF16)

    def mixer_weights(layer):
        for h in range(2):
            lanes = slice(128 * h, 128 * (h + 1))
            base = plan.base(layer)
            turned = jnp.transpose(flat[h, pl.ds(base, 128), :])
            for j in range(4):
                norms[layer, j, lanes] = column_of(turned, j)
            base += 4
            for j in range(3):
                value = flat[h, pl.ds(base + j, width, stride=3), :]
                place = slice(width * j + 128 * h, width * j + 128 * (h + 1))
                wqkv[layer, :, place] = value.astype(BF16)
                wqkv_t[layer, place] = jnp.transpose(value).astype(BF16)
            base += 3 * width
            value = flat[h, pl.ds(base, width), :]
            wo[layer, :, lanes] = value.astype(BF16)
            wo_t[layer, lanes] = jnp.transpose(value).astype(BF16)

    parts = hidden // width

    def hidden_weights(layer):
        for h in range(2):
            lanes = slice(128 * h, 128 * (h + 1))
            base = plan.base(layer) + plan.mixer
            for j in range(parts):
                value = flat[h, pl.ds(base + j, width, stride=parts), :]
                place = slice(width * j + 128 * h, width * j + 128 * (h + 1))
                wup[layer, :, place] = value.astype(BF16)
                wup_t[layer, place] = jnp.transpose(value).astype(BF16)
            base += hidden
            turned = jnp.transpose(flat[h, pl.ds(base, 128), :])
            for j in range(parts):
                place = slice(width * j + 128 * h, width * j + 128 * (h + 1))
                bup[layer, place] = column_of(turned, j)
            base += parts
            value = flat[h, pl.ds(base, hidden), :]
            wd[layer, :, lanes] = value.astype(BF16)
            wd_t[layer, lanes] = jnp.transpose(value).astype(BF16)

    reach_a, reach_b = plan.reach[0, "mixer"], plan.reach[0, "hidden"]
    reach_c, reach_d = plan.reach[1, "mixer"], plan.reach[1, "hidden"]

    def first_groups(group):
        @pl.when(group == my_z)
        def _():
            send_up()

        @pl.when(group != my_z)
        def _():
            forward_group(group)

    send_near()
    each(0, reach_a, first_groups)

    @pl.when(my_z >= reach_a)
    def _():
        send_up()

    @pl.when(my_z < reach_a)
    def _():
        each(reach_a, reach_b, forward_group)

    qmask[...] = jnp.zeros_like(qmask)
    domask[...] = jnp.zeros_like(domask)
    gnorm[...] = jnp.zeros_like(gnorm)
    gemb[...] = jnp.zeros_like(gemb)
    ones = jnp.ones((16, rows), BF16)
    gbuf[...] = jnp.transpose(cot[...].astype(F32))
    each(0, reach_a, pass_group)

    @pl.when(my_z >= reach_a)
    def _():
        each_other_z(reach_a, reach_b, forward_group)

    each(0, reach_a, take_group)
    unpack(0, reach_a)

    depth_row = lax.broadcasted_iota(jnp.int32, (128, 128), 0)
    for h in range(2):
        lanes = slice(128 * h, 128 * (h + 1))
        block = flat[h, :128]
        turned = jnp.transpose(block)
        rbias[lanes] = jnp.broadcast_to(turned[:, plan.depth : plan.depth + 1], (128, 128))
        block = jnp.where(depth_row < plan.depth, block, 0.0)
        rin[:, lanes] = block.astype(BF16)
        rit[lanes] = jnp.transpose(block).astype(BF16)
    mixer_weights(0)

    embedded = mm(rit[...], masked_all[me]) + twice(rbias[...])
    emb[...] = embedded
    hid[0] = embedded

    def normed_copy(app, block, target, slot):
        return remote(
            nrm.at[app, block], nrm.at[app, block], send_n.at[app, slot], recv_n.at[app, block],
            {"seq": target},
        )

    def grad_copy(app, block, target, slot):
        return remote(
            nrm.at[app, block], nrm.at[app, me], send_g.at[app, slot], recv_g.at[app, me],
            {"seq": target},
        )

    def grad_arrival(app, source):
        return remote(
            nrm.at[app, source], nrm.at[app, source], send_g.at[app, 0], recv_g.at[app, source],
            {"seq": source},
        )

    def turn_of(app):
        return pl.ds(pl.multiple_of(app * rows, rows), rows)

    def merge_copy(app):
        return remote(
            vt.at[:, turn_of(app)], merge.at[app], send_g.at[app, 1], recv_m.at[app], sibling
        )

    causal = lax.broadcasted_iota(jnp.int32, (rows, rows), 0) <= lax.broadcasted_iota(
        jnp.int32, (rows, rows), 1
    )

    def mask_last(values, fill):
        before = values.shape[0] - rows
        last_block = jnp.where(causal, values[before:], fill)
        return jnp.concatenate([values[:before], last_block], axis=0) if before else last_block

    def project_block(app, layer, block):
        block_t = nrm[app, block]
        places = slice(block * rows, (block + 1) * rows)
        both = mm(wqkv_t[layer, width:], block_t).astype(BF16)
        kt[app, :, places] = both[:width]
        vt[:, places] = both[width:]
        kv[app, places] = mm(
            jnp.transpose(block_t.astype(F32)).astype(BF16), wqkv[layer, :, width:]
        ).astype(BF16)

    def attend(app, blocks):
        keys = blocks * rows
        for head in range(HEADS):
            scores = mm(kv[app, :keys, :width], qmask[head]) * exp_scale
            scores = mask_last(scores, -jnp.inf)
            top = jnp.max(scores, axis=0, keepdims=True)
            weight = jnp.exp2(scores - top)
            peak[head : head + 1] = top
            total[head : head + 1] = jnp.sum(weight, axis=0, keepdims=True)
            ps[head, :keys] = weight.astype(BF16)
        for head in range(HEADS):
            lanes = slice(head * head_width, (head + 1) * head_width)
            out = mm(vt[lanes, :keys], ps[head, :keys]) * (1.0 / total[head : head + 1])
            osave[app, lanes] = out
            att[app, lanes] = out.astype(BF16)
        lse[app] = peak[...] + jnp.log2(total[...])

    def first_normed(block):
        points_copy(block, me).wait_recv()
        unit, _ = normalise(mm(rit[...], masked_all[block]) + twice(rbias[...]))
        nrm[0, block] = (unit * twice(norms[0, 0]) + twice(norms[0, 1])).astype(BF16)

    def gather_blocks(app, layer, place):
        project_block(app, layer, place)
        near, far = place - 2, 1 - (place - 2)

        @pl.when(app == 0)
        def _():
            each(0, place, first_normed)

        if place % 2 == 1:

            @pl.when(app > 0)
            def _():
                normed_copy(app, place - 1, me, 0).wait_recv()

            project_block(app, layer, place - 1)
        if place >= 2:

            @pl.when(app > 0)
            def _():
                normed_copy(app, near, me, 0).wait_recv()
                normed_copy(app, near, place + 1 - 2 * (place % 2), 2).start()

            project_block(app, layer, near)

            @pl.when(app > 0)
            def _():
                normed_copy(app, far, me, 0).wait_recv()

            project_block(app, layer, far)

    def forward(app, carry):
        layer = lax.rem(app, LAYERS)

        @pl.when(app == 1)
        def _():
            each(reach_c, reach_d, pass_group)
            each(reach_b, reach_c, take_group)
            unpack(reach_b, reach_c)
            mixer_weights(1)

        unit, _ = normalise(hid[app])
        normed = (unit * twice(norms[layer, 0]) + twice(norms[layer, 1])).astype(BF16)
        nrm[app, me] = normed

        @pl.when((my_y == 0) & (app > 0))
        def _():
            normed_copy(app, me, me + 2, 1).start()

        @pl.when((my_c == 0) & (app > 0))
        def _():
            normed_copy(app, me, me + 1, 0).start()

        queries = mm(wqkv_t[layer, :width], normed).astype(BF16)
        qsave[app] = queries
        for head in range(HEADS):
            lanes = slice(head * head_width, (head + 1) * head_width)
            qmask[head, lanes] = queries[lanes]

        for place in range(SEQ):

            @pl.when(me == place)
            def _(place=place):
                gather_blocks(app, layer, place)
                attend(app, place + 1)

        updated = hid[app] + mm(wo_t[layer], att[app])
        upd[app] = updated
        unit, _ = normalise(updated)
        second = (unit * twice(norms[layer, 2]) + twice(norms[layer, 3])).astype(BF16)
        nrm2[app] = second

        @pl.when(app == 0)
        def _():
            each(reach_a, reach_c, pass_group)
            each_other_z(reach_b, reach_d, forward_group)
            each(reach_a, reach_b, take_group)
            unpack(reach_a, reach_b)
            hidden_weights(0)

        @pl.when(app == 1)
        def _():
            each(reach_c, reach_d, take_group)
            unpack(reach_c, reach_d)
            hidden_weights(1)

        before = mm(wup_t[layer], nrm2[app]) + twice(bup[layer])
        squared = before * before
        inner = GELU_A * before * (1.0 + GELU_B * squared)
        turned = jnp.tanh(inner)
        risen = 0.5 * (1.0 + turned)
        act[app] = (before * risen).astype(BF16)
        gp[app] = risen + (0.5 * GELU_A) * before * (1.0 - turned * turned) * (
            1.0 + (3.0 * GELU_B) * squared
        )
        result = upd[app] + mm(wd_t[layer], act[app])
        again = jnp.where((layer == LAYERS - 1) & (app < APPS - 1), 1.0, 0.0)
        hid[app + 1] = result + again * emb[...]
        return carry

    lax.fori_loop(0, APPS, forward, 0)
    states[...] = jnp.transpose(hid[APPS]).astype(BF16)

    for w in waves:
        each_other_z(0, zs, lambda z, w=w: weights_z(my_z, z, w).wait_send())
        each_other_z(0, zs, lambda z, w=w: weights_plane_out(z, 1, w).wait_send())
        for step in (2, 3):
            each(0, zs, lambda z, step=step, w=w: weights_plane_out(z, step, w).wait_send())
        each_other_z(0, zs, lambda z, w=w: weights_core(2 * z + my_x, my_c, w).wait_send())
        each(0, zs, lambda z, w=w: weights_core(2 * z + 1 - my_x, my_c, w).wait_send())
    for step in range(1, SEQ):

        @pl.when(me + step < SEQ)
        def _(step=step):
            points_copy(me, me + step).wait_send()


    def normed_sent(app):
        @pl.when(my_c == 0)
        def _():
            normed_copy(app, me, me + 1, 0).wait_send()

        @pl.when(my_y == 0)
        def _():
            normed_copy(app, me, me + 2, 1).wait_send()

        @pl.when(my_y == 1)
        def _():
            normed_copy(app, my_c, my_y * 2 + 1 - my_c, 2).wait_send()

    each(1, APPS, normed_sent)
    flat[:, pl.ds(plan.used, plan.total - plan.used), :] = jnp.zeros(
        (2, plan.total - plan.used, 128), F32
    )

    from_core, from_plane, from_z = (ref[n] for n in ("from_core", "from_plane", "from_z"))
    last, summed = ref["last"], ref["summed"]

    def grads_core(group, w):
        pair = pl.ds(2 * group, 2)
        return remote(
            gathered.at[pair, 1 - my_c, :, w], from_core.at[pair, :, w],
            ref["send_gc"].at[group, w], ref["recv_gc"].at[group, w], sibling,
        )

    def grads_plane(group, step, w):
        x, y, device = in_plane(step)
        return remote(
            gathered.at[2 * group + x, my_c, y, w], from_plane.at[group, here, w],
            ref["send_gp"].at[group, step, w], ref["recv_gp"].at[group, here, w], device,
        )

    def grads_plane_in(group, step, w):
        x, y, device = in_plane(step)
        place = x * 2 + y
        return place, remote(
            gathered.at[2 * group + my_x, my_c, my_y, w], from_plane.at[group, place, w],
            ref["send_gp"].at[group, step, w], ref["recv_gp"].at[group, place, w], device,
        )

    def grads_z(source_z, target_z, w):
        return remote(
            gathered.at[2 * target_z + my_x, my_c, my_y, w], from_z.at[source_z, w],
            ref["send_gz"].at[target_z, w], ref["recv_gz"].at[source_z, w],
            {"dp": 2 * target_z + my_x},
        )

    def round_group(low, high):
        def body(group):
            for w in waves:
                for h in range(2):
                    for x in range(2):
                        for r in range(2):
                            start = (2 * group + x) * plan.flat + (2 * r + w) * quarter
                            gathered[2 * group + x, h, r, w] = flat[
                                h, pl.ds(start, quarter), :
                            ].astype(BF16)
                grads_core(group, w).start()

        each(low, high, body)

    def plane_group(low, high):
        def body(group):
            for w in waves:
                grads_core(group, w).wait()
                for step in (3, 2, 1, 0):
                    x, y, _ = in_plane(step)
                    share = 2 * group + x
                    gathered[share, my_c, y, w] = (
                        gathered[share, my_c, y, w].astype(F32) + from_core[share, y, w].astype(F32)
                    ).astype(BF16)
                    if step:
                        grads_plane(group, step, w).start()

        each(low, high, body)

    def rise_group(low, high):
        def body(group):
            for w in waves:
                value = gathered[2 * group + my_x, my_c, my_y, w].astype(F32)
                for step in (1, 2, 3):
                    place, arrival = grads_plane_in(group, step, w)
                    arrival.wait_recv()
                    value = value + from_plane[group, place, w].astype(F32)
                gathered[2 * group + my_x, my_c, my_y, w] = value.astype(BF16)

                @pl.when(group != my_z)
                def _(w=w):
                    grads_z(my_z, group, w).start()

                @pl.when(group == my_z)
                def _(w=w, value=value):
                    last[w] = value

        each(low, high, body)

    def share_sum(kind, w, column, half, device):
        piece = summed.at[column, half, w]
        return remote(
            piece, piece, ref["send_gs"].at[kind, w], ref["recv_gs"].at[kind, w], device
        )

    def collect(low, high):
        def when_mine(group):
            @pl.when(group == my_z)
            def _():
                for w in waves:

                    def body(z, w=w):
                        grads_z(z, my_z, w).wait_recv()
                        last[w] += from_z[z, w].astype(F32)

                    each_other_z(0, zs, body)
                    summed[my_c, my_y, w] = last[w].astype(BF16)
                    share_sum(1, w, my_c, my_y, across).start()
                    share_sum(0, w, my_c, my_y, sibling).start()

        each(low, high, when_mine)

    def first_group(row):
        return min(zs, -(-row // (2 * plan.flat)))

    group_a = first_group(plan.base(1) + plan.mixer)
    group_b = first_group(plan.base(0) + plan.mixer)
    group_m = (group_a + group_b + 1) // 2

    def accumulate(app, layer, offset, stride, value, again=False):
        start = plan.base(0) + layer * plan.block + offset
        count = value.shape[0]
        for h in range(2):
            place = (h, pl.ds(start, count, stride=stride), slice(None))
            part = value[:, 128 * h : 128 * (h + 1)]
            kept = flat[place]
            flat[place] = part + (kept if again else jnp.where(app < LAYERS, kept, 0.0))

    part_q, held = emb, hid.at[APPS]

    def soften_back(app, keys, diagonal):
        for head in range(HEADS):
            scores = mm(kv[app, keys, :width], qmask[head]) * exp_scale
            weight = jnp.exp2(scores - lse[app, head : head + 1])
            if diagonal:
                weight = mask_last(weight, 0.0)
            ps[head, keys] = weight.astype(BF16)
            grad = mm(kv[app, keys, width:], domask[head])
            ds[head, keys] = (weight * (grad - total[head : head + 1])).astype(BF16)

    def heads_back(app, keys, own, added):
        for head in range(HEADS):
            lanes = slice(head * head_width, (head + 1) * head_width)
            key_lanes = slice(width + head * head_width, width + (head + 1) * head_width)
            value_lanes = slice(2 * width + head * head_width, 2 * width + (head + 1) * head_width)
            dqkv[key_lanes, keys] = (
                mm_nt(qsave[app, lanes], ds[head, keys]) * score_scale
            ).astype(BF16)
            dqkv[value_lanes, keys] = mm_nt(grad_low[lanes], ps[head, keys]).astype(BF16)
            part = mm(kt[app, lanes, keys], ds[head, keys])
            if own is None:
                part_q[lanes] = part
            else:
                part = part + part_q[lanes] if added else part
                dqkv[lanes, own] = (part * score_scale).astype(BF16)

    def span_of(low, high):
        return slice(low * rows, high * rows)

    def normed_back(layer, first, block):
        return mm(wqkv[layer, :, first:], dqkv[first:, span_of(block, block + 1)])

    def weights_back(app, layer, first, block, again):
        grads = mm_nt(nrm[app, block], dqkv[first:, span_of(block, block + 1)])
        for j in range(first // width, 3):
            accumulate(
                app, layer, 4 + j, 3, grads[:, width * j - first : width * (j + 1) - first],
                again=j > 0 and again,
            )

    def attend_back(app, layer, place):
        start = place // 2 * 2
        if start:
            kept, passed = place % 2, 1 - place % 2
            soften_back(app, span_of(0, start), False)
            heads_back(app, span_of(0, start), None, False)
            vt[:, turn_of(app)] = normed_back(layer, width, passed).astype(BF16)
            merge_copy(app).start()
            held[...] = normed_back(layer, width, kept)
            weights_back(app, layer, width, passed, False)
            weights_back(app, layer, width, kept, True)
        soften_back(app, span_of(start, place + 1), True)
        if start:
            merge_copy(app).wait_recv()
            nrm[app, kept] = (held[...] + merge[app].astype(F32)).astype(BF16)
            grad_copy(app, kept, kept, 2).start()
        heads_back(app, span_of(start, place + 1), span_of(place, place + 1), bool(start))
        if place % 2:
            back = normed_back(layer, width, place - 1).astype(BF16)
            weights_back(app, layer, width, place - 1, bool(start))
            nrm[app, place - 1] = back
            grad_copy(app, place - 1, place - 1, 0).start()
        gin[...] = normed_back(layer, 0, place)
        weights_back(app, layer, 0, place, bool(start) or place % 2 == 1)

    def flush_norms(layer):
        start = plan.base(0) + layer * plan.block
        for h in range(2):
            for j in range(4):
                flat[h, pl.ds(start + j, 1), :] = jnp.sum(
                    jnp.transpose(gnorm[layer, j, 128 * h : 128 * (h + 1)]), axis=0, keepdims=True
                )

    def backward(order, carry):
        app = APPS - 1 - order
        layer = lax.rem(app, LAYERS)
        out_low = gbuf[...].astype(BF16)
        accumulate(app, layer, plan.mixer + hidden + parts, 1, mm_nt(act[app], out_low))
        pre_low = (mm(wd[layer], out_low) * gp[app]).astype(BF16)
        act[app] = pre_low
        for j in range(parts):
            part = act[app, width * j : width * (j + 1)]
            accumulate(app, layer, plan.mixer + j, parts, mm_nt(nrm2[app], part))
            accumulate(app, layer, plan.mixer + hidden + j, 1, mm_nt(ones, part)[:1])

        @pl.when(app == 1)
        def _():
            round_group(group_a, zs)

        @pl.when(app == 0)
        def _():
            rise_group(group_a, zs)
            round_group(group_b, group_a)

        grad_second = mm(wup[layer], act[app])
        unit, scale = normalise(upd[app])
        gnorm[layer, 2] += halves(grad_second * unit)
        gnorm[layer, 3] += halves(grad_second)
        grad_updated = gbuf[...] + normalise_back(grad_second, unit, scale, twice(norms[layer, 2]))
        gbuf[...] = grad_updated
        branch_low = grad_updated.astype(BF16)
        accumulate(app, layer, 4 + 3 * width, 1, mm_nt(att[app], branch_low))
        grad_att = mm(wo[layer], branch_low).astype(BF16)
        grad_low[...] = grad_att
        for head in range(HEADS):
            lanes = slice(head * head_width, (head + 1) * head_width)
            domask[head, lanes] = grad_att[lanes]
            qmask[head, lanes] = qsave[app, lanes]
            total[head : head + 1] = jnp.sum(
                osave[app, lanes] * grad_att[lanes].astype(F32), axis=0, keepdims=True
            )

        @pl.when(app == 1)
        def _():
            plane_group(group_a, zs)

        @pl.when(app == 0)
        def _():
            plane_group(group_m, group_a)

        for place in range(SEQ):

            @pl.when(me == place)
            def _(place=place):
                attend_back(app, layer, place)

        @pl.when(app == 0)
        def _():
            plane_group(group_b, group_m)

        def arrive(source):
            grad_arrival(app, source).wait_recv()
            gin[...] += nrm[app, source].astype(F32)

        @pl.when(my_c == 0)
        def _():
            arrive(me + 1)

        @pl.when(my_y == 0)
        def _():
            arrive(me + 2)

        grad_normed = gin[...]
        unit, scale = normalise(hid[app])
        gnorm[layer, 0] += halves(grad_normed * unit)
        gnorm[layer, 1] += halves(grad_normed)
        grad_in = gbuf[...] + normalise_back(grad_normed, unit, scale, twice(norms[layer, 0]))
        gbuf[...] = grad_in
        first = jnp.where(layer == 0, 1.0, 0.0)
        gemb[...] += first * grad_in

        @pl.when(app < LAYERS)
        def _():
            flush_norms(layer)

        return carry

    lax.fori_loop(0, APPS, backward, 0)
    embed_low = gemb[...].astype(BF16)
    grad_in_rows = mm_nt(masked_all[me], embed_low)
    grad_bias_rows = mm_nt(ones, embed_low)
    for h in range(2):
        lanes = slice(128 * h, 128 * (h + 1))
        flat[h, : plan.depth] = grad_in_rows[: plan.depth, lanes]
        flat[h, plan.depth : plan.depth + 1] = grad_bias_rows[:1, lanes]
    round_group(0, group_b)
    point_grad[...] = jnp.where(depth_mask, mm(rin[...], embed_low)[: plan.depth], 0.0)
    rise_group(group_m, group_a)
    plane_group(0, group_b)
    rise_group(group_b, group_m)
    rise_group(0, group_b)
    collect(0, zs)
    for w in waves:
        share_sum(1, w, my_c, 1 - my_y, across).wait_recv()
        share_sum(2, w, my_c, 1 - my_y, sibling).start()
    for w in waves:
        share_sum(0, w, 1 - my_c, my_y, sibling).wait_recv()
    for w in waves:
        share_sum(2, w, 1 - my_c, 1 - my_y, sibling).wait_recv()
    for h in range(2):
        for r, w, start in quarters:
            count = min(quarter, plan.flat - start)
            if count > 0:
                flat[0, pl.ds(2 * start + h, count, stride=2), :] = summed[h, r, w].astype(F32)[
                    :count
                ]
    gradients[...] = flat[0, : gradients.shape[0]].astype(BF16)

    for w in waves:
        for step in (1, 2, 3):
            each(0, zs, lambda z, step=step, w=w: grads_plane(z, step, w).wait_send())
        each_other_z(0, zs, lambda z, w=w: grads_z(my_z, z, w).wait_send())
        share_sum(0, w, my_c, my_y, sibling).wait_send()
        share_sum(1, w, my_c, my_y, across).wait_send()
        share_sum(2, w, my_c, 1 - my_y, sibling).wait_send()

    def finish(app):
        @pl.when(my_c == 1)
        def _():
            grad_copy(app, me - 1, me - 1, 0).wait_send()

        @pl.when(my_y == 1)
        def _():
            merge_copy(app).wait_send()
            grad_copy(app, my_c, my_c, 2).wait_send()

    each(0, APPS, finish)


def update_kernel(
    summed, weights, momenta, averages, states, point_grad,
    grad_out, fresh_out, momentum_out, mean_out, states_out, point_out,
):
    grad = summed[...].astype(F32)
    momentum = MOMENTUM * momenta[...] + grad
    fresh = weights[...] - RATE * (grad + MOMENTUM * momentum)
    grad_out[...] = grad
    momentum_out[...] = momentum
    fresh_out[...] = fresh
    mean_out[...] = AVERAGE_DECAY * averages[...] + (1.0 - AVERAGE_DECAY) * fresh

    @pl.when(pl.program_id(0) == 0)
    def _():
        states_out[...] = states[...]
        for row in range(point_grad.shape[0]):
            point_out[row] = point_grad[row : row + 1]


def shards(points, counts, cotangent, weights, momenta, averages):
    rows, depth = points.shape[1:]
    width = cotangent.shape[2]
    share = weights.shape[0]
    plan = Plan(rows, depth, width, share, lax.axis_size("dp"), lax.axis_size("seq"))
    hidden, dp_count, zs, quarter = plan.hidden, plan.dp, plan.zs, plan.quarter
    vmem = pl.BlockSpec(memory_space=pltpu.VMEM)
    smem = pl.BlockSpec(memory_space=pltpu.SMEM)
    shape = jax.ShapeDtypeStruct
    lines = (share // 128, 128)
    outs = (shape((rows, width), BF16), shape((depth, rows), F32), shape(lines, BF16))
    low = lambda *dims: pltpu.VMEM(dims, BF16)
    full = lambda *dims: pltpu.VMEM(dims, F32)
    flags = lambda *dims: pltpu.SemaphoreType.DMA(dims)
    scratch = {
        "gathered": low(dp_count, 2, 2, 2, quarter, 128),
        "flat": full(2, plan.space, 128),
        "rin": low(128, width),
        "rit": low(width, 128),
        "rbias": full(width, 128),
        "norms": low(LAYERS, 4, width, 128),
        "bup": low(LAYERS, hidden, 128),
        "wqkv": low(LAYERS, width, 3 * width),
        "wqkv_t": low(LAYERS, 3 * width, width),
        "wo": low(LAYERS, width, width),
        "wo_t": low(LAYERS, width, width),
        "wup": low(LAYERS, width, hidden),
        "wup_t": low(LAYERS, hidden, width),
        "wd": low(LAYERS, hidden, width),
        "wd_t": low(LAYERS, width, hidden),
        "masked_all": low(SEQ, 128, rows),
        "gnorm": full(LAYERS, 4, width, 128),
        "from_core": low(dp_count, 2, 2, quarter, 128),
        "from_plane": low(zs, 4, 2, quarter, 128),
        "from_z": low(zs, 2, quarter, 128),
        "last": full(2, quarter, 128),
        "summed": low(2, 2, 2, quarter, 128),
        "hid": full(APPS + 1, width, rows),
        "nrm": low(APPS, SEQ, width, rows),
        "qsave": low(APPS, width, rows),
        "kv": low(APPS, SEQ * rows, 2 * width),
        "kt": low(APPS, width, SEQ * rows),
        "vt": low(width, SEQ * rows),
        "att": low(APPS, width, rows),
        "osave": full(APPS, width, rows),
        "lse": full(APPS, HEADS, rows),
        "upd": full(APPS, width, rows),
        "nrm2": low(APPS, width, rows),
        "gp": full(APPS, hidden, rows),
        "act": low(APPS, hidden, rows),
        "emb": full(width, rows),
        "qmask": low(HEADS, width, rows),
        "domask": low(HEADS, width, rows),
        "ps": low(HEADS, SEQ * rows, rows),
        "ds": low(HEADS, SEQ * rows, rows),
        "dqkv": low(3 * width, SEQ * rows),
        "grad_low": low(width, rows),
        "peak": full(HEADS, rows),
        "total": full(HEADS, rows),
        "gbuf": full(width, rows),
        "gemb": full(width, rows),
        "gin": full(width, rows),
        "merge": low(APPS, width, rows),
        "send_n": flags(APPS, 3),
        "recv_n": flags(APPS, SEQ),
        "send_g": flags(APPS, 3),
        "recv_g": flags(APPS, SEQ),
        "recv_m": flags(APPS),
        "send_p": flags(SEQ),
        "recv_p": flags(SEQ),
        "send_wz": flags(zs, 2),
        "recv_wz": flags(zs, 2),
        "send_wp": flags(zs, 4, 2),
        "recv_wp": flags(zs, 4, 2),
        "send_wc": flags(dp_count, 2),
        "recv_wc": flags(dp_count, 2),
        "send_gc": flags(zs, 2),
        "recv_gc": flags(zs, 2),
        "send_gp": flags(zs, 4, 2),
        "recv_gp": flags(zs, 4, 2),
        "send_gz": flags(zs, 2),
        "recv_gz": flags(zs, 2),
        "send_gs": flags(3, 2),
        "recv_gs": flags(3, 2),
    }
    names = (
        "points", "counts", "cot", "weights", "states", "point_grad", "gradients", *scratch,
    )
    mine = weights.reshape(lines)
    states, point_grad, summed = pl.pallas_call(
        functools.partial(whole_kernel, plan, names),
        out_shape=outs,
        in_specs=[vmem, smem, vmem, vmem],
        out_specs=(vmem,) * len(outs),
        scratch_shapes=list(scratch.values()),
        compiler_params=pltpu.CompilerParams(
            collective_id=0, has_side_effects=True, vmem_limit_bytes=63 * 1024 * 1024
        ),
    )(points[0].T, counts, cotangent[0], mine)
    vector = shape(lines, F32)
    step_rows = min(512, lines[0])
    line_block = pl.BlockSpec((step_rows, 128), lambda i: (i, 0))
    states_block = pl.BlockSpec((rows, width), lambda i: (0, 0))
    point_block = pl.BlockSpec((depth, rows), lambda i: (0, 0))
    grad, fresh, momentum, mean, states, point_grad = pl.pallas_call(
        update_kernel,
        grid=(-(-lines[0] // step_rows),),
        out_shape=(
            vector, vector, vector, vector, shape((rows, width), BF16), shape((depth, 1, rows), F32),
        ),
        in_specs=[line_block] * 4 + [states_block, point_block],
        out_specs=(
            line_block, line_block, line_block, line_block, states_block,
            pl.BlockSpec((depth, 1, rows), lambda i: (0, 0, 0)),
        ),
        compiler_params=pltpu.CompilerParams(vmem_limit_bytes=63 * 1024 * 1024),
    )(summed, mine, momenta.reshape(lines), averages.reshape(lines), states, point_grad)
    return (
        states[None], jnp.transpose(point_grad, (1, 2, 0)),
        *(v.reshape(-1) for v in (grad, fresh, momentum, mean)),
    )


def solution(mesh):
    placed = (P("dp", "seq", None), P("dp"), P("dp", "seq", None), P("dp"), P("dp"), P("dp"))
    return jax.shard_map(
        shards,
        mesh=mesh,
        in_specs=placed,
        out_specs=(P("dp", "seq", None), P("dp", "seq", None), P("dp"), P("dp"), P("dp"), P("dp")),
        check_vma=False,
    )
```

```python
import functools
import math
import types

import jax
import jax.numpy as jnp
from jax import lax
from jax.experimental import pallas as pl
from jax.experimental.pallas import tpu as pltpu
from jax.sharding import PartitionSpec as P

MESH = pl.DeviceIdType.MESH
HEADS = 8
FF = 1024
LAYERS = 2
LOOPS = 2
APPS = LAYERS * LOOPS

EPSILON = 1e-05
RATE = 0.0003
MOMENTUM = 0.5
AVERAGE_DECAY = 0.9

F32 = jnp.float32
BF16 = jnp.bfloat16
GELU_A = math.sqrt(2.0 / math.pi)
GELU_B = 0.044715
SEQ = 4
FIRST = 32


def mm(left, right):
    return jnp.dot(left, right, preferred_element_type=F32)


def mm_nt(left, right):
    return lax.dot_general(left, right, (((1,), (1,)), ((), ())), preferred_element_type=F32)


def twice(column):
    column = column.astype(F32)
    return jnp.concatenate([column, column], axis=1)


def halves(values):
    return values[:, :128] + values[:, 128:]


def normalise(values):
    centred = values - jnp.mean(values, axis=0, keepdims=True)
    variance = jnp.mean(centred * centred, axis=0, keepdims=True)
    scale = lax.rsqrt(variance + EPSILON)
    return centred * scale, scale


def normalise_back(grad, unit, scale, gain):
    scaled = grad * gain
    first = jnp.mean(scaled, axis=0, keepdims=True)
    second = jnp.mean(scaled * unit, axis=0, keepdims=True)
    return (scaled - first - unit * second) * scale


class Plan:
    def __init__(self, rows, depth, width, share, dp_count, seq_count):
        self.rows = rows
        self.depth = depth
        self.width = width
        self.hidden = FF
        self.dp = dp_count
        self.zs = dp_count // 2
        self.seq = seq_count
        self.flat = share // width
        self.quarter = -(-self.flat // 64) * 16
        self.mixer = 4 + 3 * width + width
        self.block = self.mixer + FF + FF // width + FF
        self.total = self.flat * dp_count
        self.space = self.total + 64 + width
        self.used = self.base(LAYERS)
        self.reach = {
            (layer, part): min(self.zs, -(-(self.base(layer) + rows_here) // (2 * self.flat)))
            for layer in range(LAYERS)
            for part, rows_here in (("mixer", self.mixer), ("hidden", self.block))
        }
        self.reach[LAYERS - 1, "hidden"] = self.zs
        self.late = [(0, self.base(0) + 4)]
        group, spill = divmod(self.base(1), 2 * self.flat)
        if group and 0 < spill <= FIRST:
            self.late.append((group, spill))
            self.settled = group
        else:
            self.settled = min(self.zs, -(-self.base(1) // (2 * self.flat)))

    def base(self, layer):
        return self.depth + 1 + layer * self.block


def whole_kernel(plan, names, *refs):
    points, counts, cot, weights, states, point_grad, gradients, *scratch = refs
    ref = types.SimpleNamespace(**dict(zip(names, scratch, strict=True)))
    rows, width, hidden = plan.rows, plan.width, plan.hidden
    dp_count, zs, quarter = plan.dp, plan.zs, plan.quarter
    head_width = width // HEADS
    exp_scale = math.log2(math.e) / math.sqrt(head_width)
    score_scale = 1.0 / math.sqrt(head_width)
    quarters = [(r, w, (2 * r + w) * quarter) for r in range(2) for w in range(2)]
    waves = range(2)
    gnorm, hid, nrm, qsave, kv, kt, vt, att = (
        ref.gnorm, ref.hid, ref.nrm, ref.qsave, ref.kv, ref.kt, ref.vt, ref.att,
    )
    osave, lse, upd, nrm2, gp, act, emb, qmask = (
        ref.osave, ref.lse, ref.upd, ref.nrm2, ref.gp, ref.act, ref.emb, ref.qmask,
    )
    domask, ps, ds, dqkv, grad_low, peak, total, gbuf = (
        ref.domask, ref.ps, ref.ds, ref.dqkv, ref.grad_low, ref.peak, ref.total, ref.gbuf,
    )
    gemb, gin, merge, send_n, recv_n, send_g, recv_g, recv_m = (
        ref.gemb, ref.gin, ref.merge, ref.send_n, ref.recv_n, ref.send_g, ref.recv_g, ref.recv_m,
    )
    gathered, flat = (
        ref.gathered, ref.flat,
    )
    rin, rit, rbias, norms, bup = ref.rin, ref.rit, ref.rbias, ref.norms, ref.bup
    wqkv, wqkv_t, wo, wo_t = ref.wqkv, ref.wqkv_t, ref.wo, ref.wo_t
    wup, wup_t, wd, wd_t = ref.wup, ref.wup_t, ref.wd, ref.wd_t

    me = lax.axis_index("seq")
    owner = lax.axis_index("dp")
    my_z, my_x = owner // 2, lax.rem(owner, 2)
    my_y, my_c = me // 2, lax.rem(me, 2)
    sibling = {"seq": my_y * 2 + (1 - my_c)}
    across = {"seq": (1 - my_y) * 2 + my_c}
    here = my_x * 2 + my_y

    def in_plane(step):
        x = lax.rem(my_x + step // 2, 2)
        y = lax.rem(my_y + step % 2, 2)
        return x, y, {"dp": my_z * 2 + x, "seq": y * 2 + my_c}

    barrier = pltpu.get_barrier_semaphore()

    def greet(device):
        pl.semaphore_signal(barrier, inc=1, device_id=device, device_id_type=MESH)

    def greet_z(step, carry):
        greet({"dp": lax.rem(my_z + step, zs) * 2 + my_x})
        return carry

    for step in range(1, plan.seq):
        greet({"seq": lax.rem(me + step, plan.seq)})
    for step in (2, 3):
        greet(in_plane(step)[2])
    lax.fori_loop(1, zs, greet_z, 0)

    def remote(source, target, send, receive, device):
        return pltpu.make_async_remote_copy(
            src_ref=source, dst_ref=target, send_sem=send, recv_sem=receive,
            device_id=device, device_id_type=MESH,
        )

    def each(low, high, body):
        def step(z, carry):
            body(z)
            return carry

        lax.fori_loop(low, high, step, 0)

    def each_other_z(low, high, body):
        def step(z):
            @pl.when(z != my_z)
            def _():
                body(z)

        each(low, high, step)

    for h in range(2):
        for r, w, start in quarters:
            count = min(quarter, plan.flat - start)
            whole_rows = count // 16 * 16
            if whole_rows:
                gathered[owner, h, r, w, :whole_rows] = weights[
                    pl.ds(2 * start + h, whole_rows, stride=2), :
                ].astype(BF16)
            if whole_rows < quarter:
                rest = [jnp.zeros((quarter - count, 128), F32)]
                if whole_rows < count:
                    begin = 2 * (start + whole_rows) + h
                    rest = [weights[pl.ds(begin, count - whole_rows, stride=2), :], *rest]
                gathered[owner, h, r, w, whole_rows:] = jnp.concatenate(rest, axis=0).astype(BF16)

    depth_mask = lax.broadcasted_iota(jnp.int32, (plan.depth, rows), 0) < counts[0]
    gin[...] = jnp.zeros_like(gin)
    gin[: plan.depth] = jnp.where(depth_mask, points[...].astype(F32), 0.0)
    masked_all = ref.masked_all
    masked_all[me] = gin[:128].astype(BF16)

    pl.semaphore_wait(barrier, plan.seq + zs)

    def points_copy(source, target):
        piece = masked_all.at[source]
        return remote(
            piece, piece, ref.send_p.at[target], ref.recv_p.at[source], {"seq": target}
        )

    for step in range(1, SEQ):

        @pl.when(me + step < SEQ)
        def _(step=step):
            points_copy(me, me + step).start()

    def weights_z(source_z, target_z, w):
        piece = gathered.at[2 * source_z + my_x, my_c, my_y, w]
        return remote(
            piece, piece, ref.send_wz.at[target_z, w], ref.recv_wz.at[source_z, w],
            {"dp": 2 * target_z + my_x},
        )

    def weights_plane_out(group, step, w):
        piece = gathered.at[2 * group + my_x, my_c, my_y, w]
        _, _, device = in_plane(step)
        return remote(
            piece, piece, ref.send_wp.at[group, step, w], ref.recv_wp.at[group, here, w],
            device,
        )

    def weights_plane_in(group, step, w):
        x, y, device = in_plane(step)
        piece = gathered.at[2 * group + x, my_c, y, w]
        return remote(
            piece, piece, ref.send_wp.at[group, step, w],
            ref.recv_wp.at[group, x * 2 + y, w], device,
        )

    def weights_core(share, column, w):
        piece = gathered.at[share, column, :, w]
        return remote(
            piece, piece, ref.send_wc.at[share, w], ref.recv_wc.at[share, w], sibling
        )

    def send_near():
        for w in waves:
            for step in (2, 3):
                weights_plane_out(my_z, step, w).start()
        for w in waves:
            each(0, my_z, lambda z, w=w: weights_z(my_z, z, w).start())

    def send_up():
        for w in waves:
            each(0, zs - 1 - my_z, lambda i, w=w: weights_z(my_z, zs - 1 - i, w).start())

    def forward_group(group):
        for w in waves:
            weights_z(group, my_z, w).wait_recv()
            for step in (1, 2, 3):
                weights_plane_out(group, step, w).start()

    def pass_group(group):
        for w in waves:

            @pl.when(group != my_z)
            def _(w=w):
                weights_plane_in(group, 1, w).wait_recv()
                weights_core(2 * group + my_x, my_c, w).start()

            for step in (2, 3):
                weights_plane_in(group, step, w).wait_recv()
            weights_core(2 * group + 1 - my_x, my_c, w).start()

    def take_group(group):
        for w in waves:

            @pl.when(group != my_z)
            def _(w=w):
                weights_core(2 * group + my_x, 1 - my_c, w).wait_recv()

            weights_core(2 * group + 1 - my_x, 1 - my_c, w).wait_recv()

    def unpack(low, high):
        for share in range(2 * low, 2 * high):
            for h in range(2):
                for r, w, start in quarters:
                    flat[h, pl.ds(share * plan.flat + start, quarter), :] = gathered[
                        share, h, r, w
                    ].astype(F32)

    def column_of(turned, j):
        return jnp.broadcast_to(turned[:, j : j + 1], (128, 128)).astype(BF16)

    def mixer_weights(layer):
        for h in range(2):
            lanes = slice(128 * h, 128 * (h + 1))
            base = plan.base(layer)
            turned = jnp.transpose(flat[h, pl.ds(base, 128), :])
            for j in range(4):
                norms[layer, j, lanes] = column_of(turned, j)
            base += 4
            for j in range(3):
                value = flat[h, pl.ds(base + j, width, stride=3), :]
                place = slice(width * j + 128 * h, width * j + 128 * (h + 1))
                wqkv[layer, :, place] = value.astype(BF16)
                wqkv_t[layer, place] = jnp.transpose(value).astype(BF16)
            base += 3 * width
            value = flat[h, pl.ds(base, width), :]
            wo[layer, :, lanes] = value.astype(BF16)
            wo_t[layer, lanes] = jnp.transpose(value).astype(BF16)

    parts = hidden // width

    def hidden_weights(layer):
        for h in range(2):
            lanes = slice(128 * h, 128 * (h + 1))
            base = plan.base(layer) + plan.mixer
            for j in range(parts):
                value = flat[h, pl.ds(base + j, width, stride=parts), :]
                place = slice(width * j + 128 * h, width * j + 128 * (h + 1))
                wup[layer, :, place] = value.astype(BF16)
                wup_t[layer, place] = jnp.transpose(value).astype(BF16)
            base += hidden
            turned = jnp.transpose(flat[h, pl.ds(base, 128), :])
            for j in range(parts):
                place = slice(width * j + 128 * h, width * j + 128 * (h + 1))
                bup[layer, place] = column_of(turned, j)
            base += parts
            value = flat[h, pl.ds(base, hidden), :]
            wd[layer, :, lanes] = value.astype(BF16)
            wd_t[layer, lanes] = jnp.transpose(value).astype(BF16)

    reach_a, reach_b = plan.reach[0, "mixer"], plan.reach[0, "hidden"]
    reach_c, reach_d = plan.reach[1, "mixer"], plan.reach[1, "hidden"]

    def first_groups(group):
        @pl.when(group != my_z)
        def _():
            forward_group(group)

    send_near()
    send_up()
    each(0, reach_a, first_groups)

    each_other_z(reach_a, reach_b, forward_group)
    qmask[...] = jnp.zeros_like(qmask)
    domask[...] = jnp.zeros_like(domask)
    gnorm[...] = jnp.zeros_like(gnorm)
    gemb[...] = jnp.zeros_like(gemb)
    ones = jnp.ones((16, rows), BF16)
    gbuf[...] = jnp.transpose(cot[...].astype(F32))
    each(0, reach_a, pass_group)

    each(0, reach_a, take_group)
    unpack(0, reach_a)

    depth_row = lax.broadcasted_iota(jnp.int32, (128, 128), 0)
    for h in range(2):
        lanes = slice(128 * h, 128 * (h + 1))
        block = flat[h, :128]
        turned = jnp.transpose(block)
        rbias[lanes] = jnp.broadcast_to(turned[:, plan.depth : plan.depth + 1], (128, 128))
        block = jnp.where(depth_row < plan.depth, block, 0.0)
        rin[:, lanes] = block.astype(BF16)
        rit[lanes] = jnp.transpose(block).astype(BF16)
    mixer_weights(0)

    embedded = mm(rit[...], masked_all[me]) + twice(rbias[...])
    emb[...] = embedded
    hid[0] = embedded

    def normed_copy(app, block, target, slot):
        return remote(
            nrm.at[app, block], nrm.at[app, block], send_n.at[app, slot], recv_n.at[app, block],
            {"seq": target},
        )

    def grad_copy(app, block, target, slot):
        return remote(
            nrm.at[app, block], nrm.at[app, me], send_g.at[app, slot], recv_g.at[app, me],
            {"seq": target},
        )

    def near_copy(app, target):
        return remote(
            merge.at[app], nrm.at[app, me], send_g.at[app, 0], recv_g.at[app, me], {"seq": target}
        )

    def grad_arrival(app, source):
        return remote(
            nrm.at[app, source], nrm.at[app, source], send_g.at[app, 0], recv_g.at[app, source],
            {"seq": source},
        )

    def turn_of(app):
        return pl.ds(pl.multiple_of(app * rows, rows), rows)

    def merge_copy(app):
        return remote(
            vt.at[:, turn_of(app)], merge.at[app], send_g.at[app, 1], recv_m.at[app], sibling
        )

    causal = lax.broadcasted_iota(jnp.int32, (rows, rows), 0) <= lax.broadcasted_iota(
        jnp.int32, (rows, rows), 1
    )

    def mask_last(values, fill):
        before = values.shape[0] - rows
        last_block = jnp.where(causal, values[before:], fill)
        return jnp.concatenate([values[:before], last_block], axis=0) if before else last_block

    def project_block(app, layer, block):
        block_t = nrm[app, block]
        places = slice(block * rows, (block + 1) * rows)
        both = mm(wqkv_t[layer, width:], block_t).astype(BF16)
        kt[app, :, places] = both[:width]
        vt[:, places] = both[width:]
        kv[app, places] = mm(
            jnp.transpose(block_t.astype(F32)).astype(BF16), wqkv[layer, :, width:]
        ).astype(BF16)

    far_peak, far_total = ref.far_peak, ref.far_total

    def soften(app, keys, tops, sums, diagonal):
        for head in range(HEADS):
            scores = mm(kv[app, keys, :width], qmask[head]) * exp_scale
            if diagonal:
                scores = mask_last(scores, -jnp.inf)
            top = jnp.max(scores, axis=0, keepdims=True)
            weight = jnp.exp2(scores - top)
            tops[head : head + 1] = top
            sums[head : head + 1] = jnp.sum(weight, axis=0, keepdims=True)
            ps[head, keys] = weight.astype(BF16)

    def mix(head, keys):
        lanes = slice(head * head_width, (head + 1) * head_width)
        return lanes, mm(vt[lanes, keys], ps[head, keys])

    def finish_heads(app, keys, far):
        for head in range(HEADS):
            lanes, out = mix(head, keys)
            row = slice(head, head + 1)
            if far:
                top = jnp.maximum(peak[row], far_peak[row])
                fade, far_fade = jnp.exp2(peak[row] - top), jnp.exp2(far_peak[row] - top)
                out = hid[app + 1, lanes] * fade + out * far_fade
                peak[row] = top
                total[row] = total[row] * fade + far_total[row] * far_fade
            out = out * (1.0 / total[row])
            osave[app, lanes] = out
            att[app, lanes] = out.astype(BF16)
        lse[app] = peak[...] + jnp.log2(total[...])

    def first_normed(block):
        points_copy(block, me).wait_recv()
        unit, _ = normalise(mm(rit[...], masked_all[block]) + twice(rbias[...]))
        nrm[0, block] = (unit * twice(norms[0, 0]) + twice(norms[0, 1])).astype(BF16)

    def gather_blocks(app, layer, place):
        project_block(app, layer, place)
        near, far = place - 2, 1 - (place - 2)

        @pl.when(app == 0)
        def _():
            each(0, place, first_normed)

        if place % 2 == 1:

            @pl.when(app > 0)
            def _():
                normed_copy(app, place - 1, me, 0).wait_recv()

            project_block(app, layer, place - 1)

        def pass_near():
            normed_copy(app, near, me, 0).wait_recv()
            normed_copy(app, near, place + 1 - 2 * (place % 2), 2).start()

        keys = slice(place // 2 * 2 * rows, (place + 1) * rows)
        if place < 2:
            soften(app, keys, peak, total, True)
            finish_heads(app, keys, False)
        else:
            pl.when(app > 1)(pass_near)
            soften(app, keys, peak, total, True)
            for head in range(HEADS):
                lanes, out = mix(head, keys)
                hid[app + 1, lanes] = out
            pl.when(app == 1)(pass_near)
            project_block(app, layer, near)

            @pl.when(app > 0)
            def _():
                normed_copy(app, far, me, 0).wait_recv()

            project_block(app, layer, far)
            far_keys = slice(0, 2 * rows)
            soften(app, far_keys, far_peak, far_total, False)
            finish_heads(app, far_keys, True)

    def forward(app, carry):
        layer = lax.rem(app, LAYERS)

        @pl.when(app == 1)
        def _():
            each(reach_c, reach_d, pass_group)
            each(reach_b, reach_c, take_group)
            unpack(reach_b, reach_c)
            mixer_weights(1)

        unit, _ = normalise(hid[app])
        normed = (unit * twice(norms[layer, 0]) + twice(norms[layer, 1])).astype(BF16)
        nrm[app, me] = normed

        @pl.when((my_y == 0) & (app > 0))
        def _():
            normed_copy(app, me, me + 2, 1).start()

        @pl.when((my_c == 0) & (app > 0))
        def _():
            normed_copy(app, me, me + 1, 0).start()

        queries = mm(wqkv_t[layer, :width], normed).astype(BF16)
        qsave[app] = queries
        for head in range(HEADS):
            lanes = slice(head * head_width, (head + 1) * head_width)
            qmask[head, lanes] = queries[lanes]

        for place in range(SEQ):

            @pl.when(me == place)
            def _(place=place):
                gather_blocks(app, layer, place)

        updated = hid[app] + mm(wo_t[layer], att[app])
        upd[app] = updated
        unit, _ = normalise(updated)
        second = (unit * twice(norms[layer, 2]) + twice(norms[layer, 3])).astype(BF16)
        nrm2[app] = second

        @pl.when(app == 0)
        def _():
            each(reach_a, reach_c, pass_group)
            each_other_z(reach_b, reach_d, forward_group)
            each(reach_a, reach_b, take_group)
            unpack(reach_a, reach_b)
            hidden_weights(0)

        @pl.when(app == 1)
        def _():
            each(reach_c, reach_d, take_group)
            unpack(reach_c, reach_d)
            hidden_weights(1)

        before = mm(wup_t[layer], nrm2[app]) + twice(bup[layer])
        squared = before * before
        turned = jnp.tanh(before * (GELU_A + (GELU_A * GELU_B) * squared))
        risen = 0.5 * (1.0 + turned)
        act[app] = (before * risen).astype(BF16)
        gp[app] = risen + before * (1.0 - turned * turned) * (
            0.5 * GELU_A + (1.5 * GELU_A * GELU_B) * squared
        )
        result = upd[app] + mm(wd_t[layer], act[app])
        again = jnp.where((layer == LAYERS - 1) & (app < APPS - 1), 1.0, 0.0)
        hid[app + 1] = result + again * emb[...]
        return carry

    lax.fori_loop(0, APPS, forward, 0)
    states[...] = jnp.transpose(hid[APPS]).astype(BF16)

    for w in waves:
        each_other_z(0, zs, lambda z, w=w: weights_z(my_z, z, w).wait_send())
        each_other_z(0, zs, lambda z, w=w: weights_plane_out(z, 1, w).wait_send())
        for step in (2, 3):
            each(0, zs, lambda z, step=step, w=w: weights_plane_out(z, step, w).wait_send())
        each_other_z(0, zs, lambda z, w=w: weights_core(2 * z + my_x, my_c, w).wait_send())
        each(0, zs, lambda z, w=w: weights_core(2 * z + 1 - my_x, my_c, w).wait_send())
    for step in range(1, SEQ):

        @pl.when(me + step < SEQ)
        def _(step=step):
            points_copy(me, me + step).wait_send()


    def normed_sent(app):
        @pl.when(my_c == 0)
        def _():
            normed_copy(app, me, me + 1, 0).wait_send()

        @pl.when(my_y == 0)
        def _():
            normed_copy(app, me, me + 2, 1).wait_send()

        @pl.when(my_y == 1)
        def _():
            normed_copy(app, my_c, my_y * 2 + 1 - my_c, 2).wait_send()

    each(1, APPS, normed_sent)
    flat[:, pl.ds(plan.used, plan.total - plan.used), :] = jnp.zeros(
        (2, plan.total - plan.used, 128), F32
    )

    from_core, from_plane, from_z = ref.from_core, ref.from_plane, ref.from_z
    last, summed = ref.last, ref.summed

    def grads_core(group, w):
        pair = pl.ds(2 * group, 2)
        return remote(
            gathered.at[pair, 1 - my_c, :, w], from_core.at[pair, :, w],
            ref.send_gc.at[group, w], ref.recv_gc.at[group, w], sibling,
        )

    def grads_plane(group, step, w):
        x, y, device = in_plane(step)
        return remote(
            gathered.at[2 * group + x, my_c, y, w], from_plane.at[group, here, w],
            ref.send_gp.at[group, step, w], ref.recv_gp.at[group, here, w], device,
        )

    def grads_plane_in(group, step, w):
        x, y, device = in_plane(step)
        place = x * 2 + y
        return place, remote(
            gathered.at[2 * group + my_x, my_c, my_y, w], from_plane.at[group, place, w],
            ref.send_gp.at[group, step, w], ref.recv_gp.at[group, place, w], device,
        )

    def grads_z(source_z, target_z, w):
        return remote(
            gathered.at[2 * target_z + my_x, my_c, my_y, w], from_z.at[source_z, w],
            ref.send_gz.at[target_z, w], ref.recv_gz.at[source_z, w],
            {"dp": 2 * target_z + my_x},
        )

    def round_group(low, high):
        def body(group):
            for w in waves:
                for h in range(2):
                    for x in range(2):
                        for r in range(2):
                            start = (2 * group + x) * plan.flat + (2 * r + w) * quarter
                            gathered[2 * group + x, h, r, w] = flat[
                                h, pl.ds(start, quarter), :
                            ].astype(BF16)
                grads_core(group, w).start()

        each(low, high, body)

    def plane_group(low, high):
        def body(group):
            for w in waves:
                grads_core(group, w).wait()
                for step in (3, 2, 1, 0):
                    x, y, _ = in_plane(step)
                    share = 2 * group + x
                    gathered[share, my_c, y, w] = (
                        gathered[share, my_c, y, w].astype(F32) + from_core[share, y, w].astype(F32)
                    ).astype(BF16)
                    if step:
                        grads_plane(group, step, w).start()

        each(low, high, body)

    def rise_group(low, high):
        def body(group):
            for w in waves:
                value = gathered[2 * group + my_x, my_c, my_y, w].astype(F32)
                for step in (1, 2, 3):
                    place, arrival = grads_plane_in(group, step, w)
                    arrival.wait_recv()
                    value = value + from_plane[group, place, w].astype(F32)
                gathered[2 * group + my_x, my_c, my_y, w] = value.astype(BF16)

                @pl.when(group != my_z)
                def _(w=w):
                    grads_z(my_z, group, w).start()

                @pl.when(group == my_z)
                def _(w=w, value=value):
                    last[w] = value

        each(low, high, body)

    first_low, first_from, first_places, first_rise, first_levels, first_sum = (
        ref.first_low, ref.first_from, ref.first_places, ref.first_rise, ref.first_levels, ref.first_sum,
    )

    def first_core():
        return remote(
            first_low.at[1 - my_c], first_from, ref.send_f.at[0], ref.recv_fc.at[0], sibling
        )

    def first_plane(step):
        _, _, device = in_plane(step)
        return remote(
            first_low.at[my_c], first_places.at[here],
            ref.send_f.at[step], ref.recv_fp.at[here], device,
        )

    def first_plane_in(step):
        x, y, device = in_plane(step)
        place = x * 2 + y
        return place, remote(
            first_low.at[my_c], first_places.at[place],
            ref.send_f.at[step], ref.recv_fp.at[place], device,
        )

    def first_z(b, source):
        return remote(
            first_rise.at[b], first_levels.at[source], ref.send_f.at[5 + b],
            ref.recv_fz.at[source], {"dp": 2 * plan.late[b][0] + my_x},
        )

    def first_share(column):
        piece = first_sum.at[column]
        return remote(piece, piece, ref.send_f.at[4], ref.recv_fs.at[0], sibling)

    def to_first_x(body):
        @pl.when(my_x == 0)
        def _():
            body(1)

        @pl.when(my_x == 1)
        def _():
            body(2)
            body(3)

    def share_sum(kind, w, column, half, device):
        piece = summed.at[column, half, w]
        return remote(
            piece, piece, ref.send_gs.at[kind, w], ref.recv_gs.at[kind, w], device
        )

    def collect(low, high):
        def when_mine(group):
            @pl.when(group == my_z)
            def _():
                for w in waves:

                    def body(z, w=w):
                        grads_z(z, my_z, w).wait_recv()
                        last[w] += from_z[z, w].astype(F32)

                    each_other_z(0, zs, body)
                    summed[my_c, my_y, w] = last[w].astype(BF16)
                    share_sum(1, w, my_c, my_y, across).start()
                    share_sum(0, w, my_c, my_y, sibling).start()

        each(low, high, when_mine)

    def first_group(row):
        return min(zs, -(-row // (2 * plan.flat)))

    group_a = first_group(plan.base(1) + plan.mixer)
    group_b = first_group(plan.base(0) + plan.mixer)
    group_e = plan.settled

    def accumulate(app, layer, offset, stride, value, again=False):
        start = plan.base(0) + layer * plan.block + offset
        count = value.shape[0]
        for h in range(2):
            place = (h, pl.ds(start, count, stride=stride), slice(None))
            part = value[:, 128 * h : 128 * (h + 1)]
            kept = flat[place]
            flat[place] = part + (kept if again else jnp.where(app < LAYERS, kept, 0.0))

    part_q, held = emb, hid.at[APPS]

    def soften_back(app, keys, diagonal):
        for head in range(HEADS):
            scores = mm(kv[app, keys, :width], qmask[head]) * exp_scale
            weight = jnp.exp2(scores - lse[app, head : head + 1])
            if diagonal:
                weight = mask_last(weight, 0.0)
            ps[head, keys] = weight.astype(BF16)
            grad = mm(kv[app, keys, width:], domask[head])
            ds[head, keys] = (weight * (grad - total[head : head + 1])).astype(BF16)

    def heads_back(app, keys, own, added):
        for head in range(HEADS):
            lanes = slice(head * head_width, (head + 1) * head_width)
            key_lanes = slice(width + head * head_width, width + (head + 1) * head_width)
            value_lanes = slice(2 * width + head * head_width, 2 * width + (head + 1) * head_width)
            dqkv[key_lanes, keys] = (
                mm_nt(qsave[app, lanes], ds[head, keys]) * score_scale
            ).astype(BF16)
            dqkv[value_lanes, keys] = mm_nt(grad_low[lanes], ps[head, keys]).astype(BF16)
            part = mm(kt[app, lanes, keys], ds[head, keys])
            if own is None:
                part_q[lanes] = part
            else:
                part = part + part_q[lanes] if added else part
                dqkv[lanes, own] = (part * score_scale).astype(BF16)

    def span_of(low, high):
        return slice(low * rows, high * rows)

    def normed_back(layer, first, block):
        return mm(wqkv[layer, :, first:], dqkv[first:, span_of(block, block + 1)])

    def weights_back(app, layer, first, block, again):
        grads = mm_nt(nrm[app, block], dqkv[first:, span_of(block, block + 1)])
        for j in range(first // width, 3):
            accumulate(
                app, layer, 4 + j, 3, grads[:, width * j - first : width * (j + 1) - first],
                again=j > 0 and again,
            )

    def attend_back(app, layer, place):
        start = place // 2 * 2
        if start:
            kept, passed = place % 2, 1 - place % 2
            soften_back(app, span_of(0, start), False)
            heads_back(app, span_of(0, start), None, False)
            vt[:, turn_of(app)] = normed_back(layer, width, passed).astype(BF16)
            merge_copy(app).start()
            held[...] = normed_back(layer, width, kept)
            weights_back(app, layer, width, passed, False)
            weights_back(app, layer, width, kept, True)
        soften_back(app, span_of(start, place + 1), True)
        if start:
            merge_copy(app).wait_recv()
            nrm[app, kept] = (held[...] + merge[app].astype(F32)).astype(BF16)
            grad_copy(app, kept, kept, 2).start()
        heads_back(app, span_of(start, place + 1), span_of(place, place + 1), bool(start))
        if place % 2:
            merge[app] = normed_back(layer, width, place - 1).astype(BF16)
            near_copy(app, place - 1).start()
            weights_back(app, layer, width, place - 1, bool(start))
        gin[...] = normed_back(layer, 0, place)
        weights_back(app, layer, 0, place, bool(start) or place % 2 == 1)

    def flush_norms(layer):
        start = plan.base(0) + layer * plan.block
        for h in range(2):
            for j in range(4):
                flat[h, pl.ds(start + j, 1), :] = jnp.sum(
                    jnp.transpose(gnorm[layer, j, 128 * h : 128 * (h + 1)]), axis=0, keepdims=True
                )

    def backward(order, carry):
        app = APPS - 1 - order
        layer = lax.rem(app, LAYERS)

        @pl.when(app == 0)
        def _():
            plane_group(group_e, group_a)

        out_low = gbuf[...].astype(BF16)
        accumulate(app, layer, plan.mixer + hidden + parts, 1, mm_nt(act[app], out_low))
        pre_low = (mm(wd[layer], out_low) * gp[app]).astype(BF16)
        act[app] = pre_low
        for j in range(parts):
            part = act[app, width * j : width * (j + 1)]
            accumulate(app, layer, plan.mixer + j, parts, mm_nt(nrm2[app], part))
            accumulate(app, layer, plan.mixer + hidden + j, 1, mm_nt(ones, part)[:1])

        @pl.when(app == 1)
        def _():
            round_group(group_a, zs)

        @pl.when(app == 0)
        def _():
            round_group(group_b, group_e)

        grad_second = mm(wup[layer], act[app])
        unit, scale = normalise(upd[app])
        gnorm[layer, 2] += halves(grad_second * unit)
        gnorm[layer, 3] += halves(grad_second)
        grad_updated = gbuf[...] + normalise_back(grad_second, unit, scale, twice(norms[layer, 2]))
        gbuf[...] = grad_updated
        branch_low = grad_updated.astype(BF16)
        accumulate(app, layer, 4 + 3 * width, 1, mm_nt(att[app], branch_low))
        grad_att = mm(wo[layer], branch_low).astype(BF16)
        grad_low[...] = grad_att
        for head in range(HEADS):
            lanes = slice(head * head_width, (head + 1) * head_width)
            domask[head, lanes] = grad_att[lanes]
            qmask[head, lanes] = qsave[app, lanes]
            total[head : head + 1] = jnp.sum(
                osave[app, lanes] * grad_att[lanes].astype(F32), axis=0, keepdims=True
            )

        @pl.when(app == 1)
        def _():
            plane_group(group_a, zs)

        @pl.when(app == 0)
        def _():
            plane_group(group_b, group_e)

        for place in range(SEQ):

            @pl.when(me == place)
            def _(place=place):
                attend_back(app, layer, place)

        @pl.when(app == 0)
        def _():
            round_group(0, group_b)
            rise_group(group_e, group_a)
            plane_group(0, group_b)
            rise_group(group_b, group_e)

        def arrive(source):
            grad_arrival(app, source).wait_recv()
            gin[...] += nrm[app, source].astype(F32)

        @pl.when(my_c == 0)
        def _():
            arrive(me + 1)

        @pl.when(my_y == 0)
        def _():
            arrive(me + 2)

        grad_normed = gin[...]
        unit, scale = normalise(hid[app])
        gnorm[layer, 0] += halves(grad_normed * unit)
        gnorm[layer, 1] += halves(grad_normed)
        grad_in = gbuf[...] + normalise_back(grad_normed, unit, scale, twice(norms[layer, 0]))
        gbuf[...] = grad_in
        first = jnp.where(layer == 0, 1.0, 0.0)
        gemb[...] += first * grad_in

        @pl.when(app < LAYERS)
        def _():
            flush_norms(layer)

        @pl.when(app == 1)
        def _():
            round_group(group_e, group_a)
            rise_group(group_a, zs)

        return carry

    lax.fori_loop(0, APPS, backward, 0)
    embed_low = gemb[...].astype(BF16)
    grad_in_rows = mm_nt(masked_all[me], embed_low)
    grad_bias_rows = mm_nt(ones, embed_low)
    for h in range(2):
        lanes = slice(128 * h, 128 * (h + 1))
        flat[h, : plan.depth] = grad_in_rows[: plan.depth, lanes]
        flat[h, plan.depth : plan.depth + 1] = grad_bias_rows[:1, lanes]
    for b, (group, _) in enumerate(plan.late):
        for h in range(2):
            first_low[h, b] = flat[h, pl.ds(2 * group * plan.flat, FIRST), :].astype(BF16)
    first_core().start()
    point_grad[...] = jnp.where(depth_mask, mm(rin[...], embed_low)[: plan.depth], 0.0)
    first_core().wait()
    first_low[my_c] = (first_low[my_c].astype(F32) + first_from[...].astype(F32)).astype(BF16)
    to_first_x(lambda step: first_plane(step).start())
    rise_group(0, group_b)

    @pl.when(my_x == 0)
    def _():
        first_places[here] = first_low[my_c]
        for step in (1, 2, 3):
            place, arrival = first_plane_in(step)
            arrival.wait_recv()
        first_rise[...] = sum(first_places[place].astype(F32) for place in range(4)).astype(BF16)

        for b, (group, _) in enumerate(plan.late):

            @pl.when(my_z != group)
            def _(b=b):
                first_z(b, my_z).start()

    collect(0, zs)
    for b, (group, _) in enumerate(plan.late):

        @pl.when(owner == 2 * group)
        def _(b=b):
            first_levels[my_z] = first_rise[b]
            each_other_z(0, zs, lambda z: first_z(b, z).wait_recv())
            first_sum[my_c] = sum(first_levels[z].astype(F32) for z in range(zs)).astype(BF16)
            first_share(my_c).start()

    for w in waves:
        share_sum(1, w, my_c, 1 - my_y, across).wait_recv()
        share_sum(2, w, my_c, 1 - my_y, sibling).start()
    for w in waves:
        share_sum(0, w, 1 - my_c, my_y, sibling).wait_recv()
    for w in waves:
        share_sum(2, w, 1 - my_c, 1 - my_y, sibling).wait_recv()
    for h in range(2):
        for r, w, start in quarters:
            count = min(quarter, plan.flat - start)
            if count > 0:
                flat[0, pl.ds(2 * start + h, count, stride=2), :] = summed[h, r, w].astype(F32)[
                    :count
                ]
    for group, count in plan.late:

        @pl.when(owner == 2 * group)
        def _(count=count):
            first_share(1 - my_c).wait_recv()
            for h in range(2):
                flat[0, pl.ds(h, count, stride=2), :] = first_sum[h].astype(F32)[:count]

    gradients[...] = flat[0, : gradients.shape[0]].astype(BF16)

    to_first_x(lambda step: first_plane(step).wait_send())

    for b, (group, _) in enumerate(plan.late):

        @pl.when((my_x == 0) & (my_z != group))
        def _(b=b):
            first_z(b, my_z).wait_send()

        @pl.when(owner == 2 * group)
        def _():
            first_share(my_c).wait_send()

    for w in waves:
        for step in (1, 2, 3):
            each(0, zs, lambda z, step=step, w=w: grads_plane(z, step, w).wait_send())
        each_other_z(0, zs, lambda z, w=w: grads_z(my_z, z, w).wait_send())
        share_sum(0, w, my_c, my_y, sibling).wait_send()
        share_sum(1, w, my_c, my_y, across).wait_send()
        share_sum(2, w, my_c, 1 - my_y, sibling).wait_send()

    def finish(app):
        @pl.when(my_c == 1)
        def _():
            near_copy(app, me - 1).wait_send()

        @pl.when(my_y == 1)
        def _():
            merge_copy(app).wait_send()
            grad_copy(app, my_c, my_c, 2).wait_send()

    each(0, APPS, finish)


def update_kernel(
    summed, weights, momenta, averages, states, point_grad,
    grad_out, fresh_out, momentum_out, mean_out, states_out, point_out,
):
    grad = summed[...].astype(F32)
    momentum = MOMENTUM * momenta[...] + grad
    fresh = weights[...] - RATE * (grad + MOMENTUM * momentum)
    grad_out[...] = grad
    momentum_out[...] = momentum
    fresh_out[...] = fresh
    mean_out[...] = AVERAGE_DECAY * averages[...] + (1.0 - AVERAGE_DECAY) * fresh

    @pl.when(pl.program_id(0) == 0)
    def _():
        states_out[...] = states[...]
        for row in range(point_grad.shape[0]):
            point_out[row] = point_grad[row : row + 1]


def shards(points, counts, cotangent, weights, momenta, averages):
    rows, depth = points.shape[1:]
    width = cotangent.shape[2]
    share = weights.shape[0]
    plan = Plan(rows, depth, width, share, lax.axis_size("dp"), lax.axis_size("seq"))
    hidden, dp_count, zs, quarter = plan.hidden, plan.dp, plan.zs, plan.quarter
    vmem = pl.BlockSpec(memory_space=pltpu.VMEM)
    smem = pl.BlockSpec(memory_space=pltpu.SMEM)
    shape = jax.ShapeDtypeStruct
    lines = (share // 128, 128)
    outs = (shape((rows, width), BF16), shape((depth, rows), F32), shape(lines, BF16))
    low = lambda *dims: pltpu.VMEM(dims, BF16)
    full = lambda *dims: pltpu.VMEM(dims, F32)
    flags = lambda *dims: pltpu.SemaphoreType.DMA(dims)
    scratch = dict(
        gathered=low(dp_count, 2, 2, 2, quarter, 128),
        flat=full(2, plan.space, 128),
        rin=low(128, width),
        rit=low(width, 128),
        rbias=full(width, 128),
        norms=low(LAYERS, 4, width, 128),
        bup=low(LAYERS, hidden, 128),
        wqkv=low(LAYERS, width, 3 * width),
        wqkv_t=low(LAYERS, 3 * width, width),
        wo=low(LAYERS, width, width),
        wo_t=low(LAYERS, width, width),
        wup=low(LAYERS, width, hidden),
        wup_t=low(LAYERS, hidden, width),
        wd=low(LAYERS, hidden, width),
        wd_t=low(LAYERS, width, hidden),
        masked_all=low(SEQ, 128, rows),
        gnorm=full(LAYERS, 4, width, 128),
        from_core=low(dp_count, 2, 2, quarter, 128),
        from_plane=low(zs, 4, 2, quarter, 128),
        from_z=low(zs, 2, quarter, 128),
        last=full(2, quarter, 128),
        first_low=low(2, len(plan.late), FIRST, 128),
        first_from=low(len(plan.late), FIRST, 128),
        first_places=low(4, len(plan.late), FIRST, 128),
        first_rise=low(len(plan.late), FIRST, 128),
        first_levels=low(zs, FIRST, 128),
        first_sum=low(2, FIRST, 128),
        send_f=flags(5 + len(plan.late)),
        recv_fc=flags(1),
        recv_fp=flags(4),
        recv_fz=flags(zs),
        recv_fs=flags(1),
        summed=low(2, 2, 2, quarter, 128),
        hid=full(APPS + 1, width, rows),
        nrm=low(APPS, SEQ, width, rows),
        qsave=low(APPS, width, rows),
        kv=low(APPS, SEQ * rows, 2 * width),
        kt=low(APPS, width, SEQ * rows),
        vt=low(width, SEQ * rows),
        att=low(APPS, width, rows),
        osave=full(APPS, width, rows),
        lse=full(APPS, HEADS, rows),
        upd=full(APPS, width, rows),
        nrm2=low(APPS, width, rows),
        gp=full(APPS, hidden, rows),
        act=low(APPS, hidden, rows),
        emb=full(width, rows),
        qmask=low(HEADS, width, rows),
        domask=low(HEADS, width, rows),
        ps=low(HEADS, SEQ * rows, rows),
        ds=low(HEADS, SEQ * rows, rows),
        dqkv=low(3 * width, SEQ * rows),
        grad_low=low(width, rows),
        peak=full(HEADS, rows),
        total=full(HEADS, rows),
        far_peak=full(HEADS, rows),
        far_total=full(HEADS, rows),
        gbuf=full(width, rows),
        gemb=full(width, rows),
        gin=full(width, rows),
        merge=low(APPS, width, rows),
        send_n=flags(APPS, 3),
        recv_n=flags(APPS, SEQ),
        send_g=flags(APPS, 3),
        recv_g=flags(APPS, SEQ),
        recv_m=flags(APPS),
        send_p=flags(SEQ),
        recv_p=flags(SEQ),
        send_wz=flags(zs, 2),
        recv_wz=flags(zs, 2),
        send_wp=flags(zs, 4, 2),
        recv_wp=flags(zs, 4, 2),
        send_wc=flags(dp_count, 2),
        recv_wc=flags(dp_count, 2),
        send_gc=flags(zs, 2),
        recv_gc=flags(zs, 2),
        send_gp=flags(zs, 4, 2),
        recv_gp=flags(zs, 4, 2),
        send_gz=flags(zs, 2),
        recv_gz=flags(zs, 2),
        send_gs=flags(3, 2),
        recv_gs=flags(3, 2),
    )
    mine = weights.reshape(lines)
    states, point_grad, summed = pl.pallas_call(
        functools.partial(whole_kernel, plan, tuple(scratch)),
        out_shape=outs,
        in_specs=[vmem, smem, vmem, vmem],
        out_specs=(vmem,) * len(outs),
        scratch_shapes=list(scratch.values()),
        compiler_params=pltpu.CompilerParams(
            collective_id=0, has_side_effects=True, vmem_limit_bytes=63 * 1024 * 1024
        ),
    )(points[0].T, counts, cotangent[0], mine)
    vector = shape(lines, F32)
    step_rows = min(776, lines[0])
    line_block = pl.BlockSpec((step_rows, 128), lambda i: (i, 0))
    states_block = pl.BlockSpec((rows, width), lambda i: (0, 0))
    point_block = pl.BlockSpec((depth, rows), lambda i: (0, 0))
    grad, fresh, momentum, mean, states, point_grad = pl.pallas_call(
        update_kernel,
        grid=(-(-lines[0] // step_rows),),
        out_shape=(
            vector, vector, vector, vector, shape((rows, width), BF16), shape((depth, 1, rows), F32),
        ),
        in_specs=[line_block] * 4 + [states_block, point_block],
        out_specs=(
            line_block, line_block, line_block, line_block, states_block,
            pl.BlockSpec((depth, 1, rows), lambda i: (0, 0, 0)),
        ),
        compiler_params=pltpu.CompilerParams(vmem_limit_bytes=63 * 1024 * 1024),
    )(summed, mine, momenta.reshape(lines), averages.reshape(lines), states, point_grad)
    return (
        states[None], jnp.transpose(point_grad, (1, 2, 0)),
        *(v.reshape(-1) for v in (grad, fresh, momentum, mean)),
    )


def solution(mesh):
    placed = (P("dp", "seq", None), P("dp"), P("dp", "seq", None), P("dp"), P("dp"), P("dp"))
    return jax.shard_map(
        shards,
        mesh=mesh,
        in_specs=placed,
        out_specs=(P("dp", "seq", None), P("dp", "seq", None), P("dp"), P("dp"), P("dp"), P("dp")),
        check_vma=False,
    )
```

```python
import functools
import math
import types

import jax
import jax.numpy as jnp
from jax import lax
from jax.experimental import pallas as pl
from jax.experimental.pallas import tpu as pltpu
from jax.sharding import PartitionSpec as P

MESH = pl.DeviceIdType.MESH
HEADS = 8
FF = 1024
LAYERS = 2
LOOPS = 2
APPS = LAYERS * LOOPS

EPSILON = 1e-05
RATE = 0.0003
MOMENTUM = 0.5
AVERAGE_DECAY = 0.9

F32 = jnp.float32
BF16 = jnp.bfloat16
GELU_A = math.sqrt(2.0 / math.pi)
GELU_B = 0.044715
SEQ = 4
FIRST = 32


def mm(left, right):
    return jnp.dot(left, right, preferred_element_type=F32)


def mm_nt(left, right):
    return lax.dot_general(left, right, (((1,), (1,)), ((), ())), preferred_element_type=F32)


def twice(column):
    column = column.astype(F32)
    return jnp.concatenate([column, column], axis=1)


def halves(values):
    return values[:, :128] + values[:, 128:]


def normalise(values):
    centred = values - jnp.mean(values, axis=0, keepdims=True)
    variance = jnp.mean(centred * centred, axis=0, keepdims=True)
    scale = lax.rsqrt(variance + EPSILON)
    return centred * scale, scale


def normalise_back(grad, unit, scale, gain):
    scaled = grad * gain
    first = jnp.mean(scaled, axis=0, keepdims=True)
    second = jnp.mean(scaled * unit, axis=0, keepdims=True)
    return (scaled - first - unit * second) * scale


class Plan:
    def __init__(self, rows, depth, width, share, dp_count, seq_count):
        self.rows = rows
        self.depth = depth
        self.width = width
        self.hidden = FF
        self.dp = dp_count
        self.zs = dp_count // 2
        self.seq = seq_count
        self.flat = share // width
        self.quarter = -(-self.flat // 64) * 16
        self.mixer = 4 + 3 * width + width
        self.block = self.mixer + FF + FF // width + FF
        self.total = self.flat * dp_count
        self.space = self.total + 64 + width
        self.used = self.base(LAYERS)
        self.reach = {
            (layer, part): min(self.zs, -(-(self.base(layer) + rows_here) // (2 * self.flat)))
            for layer in range(LAYERS)
            for part, rows_here in (("mixer", self.mixer), ("hidden", self.block))
        }
        self.reach[LAYERS - 1, "hidden"] = self.zs
        self.late = [(0, self.base(0) + 4)]
        group, spill = divmod(self.base(1), 2 * self.flat)
        if group and 0 < spill <= FIRST - 4:
            self.late.append((group, spill + 4))
            self.settled = group
        else:
            self.settled = min(self.zs, -(-self.base(1) // (2 * self.flat)))

    def base(self, layer):
        return self.depth + 1 + layer * self.block


def whole_kernel(plan, names, *refs):
    points, counts, cot, weights, states, point_grad, gradients, *scratch = refs
    ref = types.SimpleNamespace(**dict(zip(names, scratch, strict=True)))
    rows, width, hidden = plan.rows, plan.width, plan.hidden
    dp_count, zs, quarter = plan.dp, plan.zs, plan.quarter
    head_width = width // HEADS
    exp_scale = math.log2(math.e) / math.sqrt(head_width)
    score_scale = 1.0 / math.sqrt(head_width)
    quarters = [(r, w, (2 * r + w) * quarter) for r in range(2) for w in range(2)]
    waves = range(2)
    gnorm, hid, nrm, qsave, kv, kt, vt, att = (
        ref.gnorm, ref.hid, ref.nrm, ref.qsave, ref.kv, ref.kt, ref.vt, ref.att,
    )
    osave, lse, upd, nrm2, gp, act, emb, qmask = (
        ref.osave, ref.lse, ref.upd, ref.nrm2, ref.gp, ref.act, ref.emb, ref.qmask,
    )
    domask, ps, ds, dqkv, grad_low, peak, total, gbuf = (
        ref.domask, ref.ps, ref.ds, ref.dqkv, ref.grad_low, ref.peak, ref.total, ref.gbuf,
    )
    gemb, gin, merge, send_n, recv_n, send_g, recv_g, recv_m = (
        ref.gemb, ref.gin, ref.merge, ref.send_n, ref.recv_n, ref.send_g, ref.recv_g, ref.recv_m,
    )
    gathered, flat = (
        ref.gathered, ref.flat,
    )
    rin, rit, rbias, norms, bup = ref.rin, ref.rit, ref.rbias, ref.norms, ref.bup
    wqkv, wqkv_t, wo, wo_t = ref.wqkv, ref.wqkv_t, ref.wo, ref.wo_t
    wup, wup_t, wd, wd_t = ref.wup, ref.wup_t, ref.wd, ref.wd_t

    me = lax.axis_index("seq")
    owner = lax.axis_index("dp")
    my_z, my_x = owner // 2, lax.rem(owner, 2)
    my_y, my_c = me // 2, lax.rem(me, 2)
    sibling = {"seq": my_y * 2 + (1 - my_c)}
    across = {"seq": (1 - my_y) * 2 + my_c}
    here = my_x * 2 + my_y

    def in_plane(step):
        x = lax.rem(my_x + step // 2, 2)
        y = lax.rem(my_y + step % 2, 2)
        return x, y, {"dp": my_z * 2 + x, "seq": y * 2 + my_c}

    barrier = pltpu.get_barrier_semaphore()

    def greet(device):
        pl.semaphore_signal(barrier, inc=1, device_id=device, device_id_type=MESH)

    def greet_z(step, carry):
        greet({"dp": lax.rem(my_z + step, zs) * 2 + my_x})
        return carry

    for step in range(1, plan.seq):
        greet({"seq": lax.rem(me + step, plan.seq)})
    for step in (2, 3):
        greet(in_plane(step)[2])
    lax.fori_loop(1, zs, greet_z, 0)

    def remote(source, target, send, receive, device):
        return pltpu.make_async_remote_copy(
            src_ref=source, dst_ref=target, send_sem=send, recv_sem=receive,
            device_id=device, device_id_type=MESH,
        )

    def each(low, high, body):
        def step(z, carry):
            body(z)
            return carry

        lax.fori_loop(low, high, step, 0)

    def each_other_z(low, high, body):
        def step(z):
            @pl.when(z != my_z)
            def _():
                body(z)

        each(low, high, step)

    for h in range(2):
        for r, w, start in quarters:
            count = min(quarter, plan.flat - start)
            whole_rows = count // 16 * 16
            if whole_rows:
                gathered[owner, h, r, w, :whole_rows] = weights[
                    pl.ds(2 * start + h, whole_rows, stride=2), :
                ].astype(BF16)
            if whole_rows < quarter:
                rest = [jnp.zeros((quarter - count, 128), F32)]
                if whole_rows < count:
                    begin = 2 * (start + whole_rows) + h
                    rest = [weights[pl.ds(begin, count - whole_rows, stride=2), :], *rest]
                gathered[owner, h, r, w, whole_rows:] = jnp.concatenate(rest, axis=0).astype(BF16)

    depth_mask = lax.broadcasted_iota(jnp.int32, (plan.depth, rows), 0) < counts[0]
    gin[...] = jnp.zeros_like(gin)
    gin[: plan.depth] = jnp.where(depth_mask, points[...].astype(F32), 0.0)
    masked_all = ref.masked_all
    masked_all[me] = gin[:128].astype(BF16)

    pl.semaphore_wait(barrier, plan.seq + zs)

    def points_copy(source, target):
        piece = masked_all.at[source]
        return remote(
            piece, piece, ref.send_p.at[target], ref.recv_p.at[source], {"seq": target}
        )

    for step in range(1, SEQ):

        @pl.when(me + step < SEQ)
        def _(step=step):
            points_copy(me, me + step).start()

    def weights_z(source_z, target_z, w):
        piece = gathered.at[2 * source_z + my_x, my_c, my_y, w]
        return remote(
            piece, piece, ref.send_wz.at[target_z, w], ref.recv_wz.at[source_z, w],
            {"dp": 2 * target_z + my_x},
        )

    def weights_plane_out(group, step, w):
        piece = gathered.at[2 * group + my_x, my_c, my_y, w]
        _, _, device = in_plane(step)
        return remote(
            piece, piece, ref.send_wp.at[group, step, w], ref.recv_wp.at[group, here, w],
            device,
        )

    def weights_plane_in(group, step, w):
        x, y, device = in_plane(step)
        piece = gathered.at[2 * group + x, my_c, y, w]
        return remote(
            piece, piece, ref.send_wp.at[group, step, w],
            ref.recv_wp.at[group, x * 2 + y, w], device,
        )

    def weights_core(share, column, w):
        piece = gathered.at[share, column, :, w]
        return remote(
            piece, piece, ref.send_wc.at[share, w], ref.recv_wc.at[share, w], sibling
        )

    def send_near():
        for w in waves:
            for step in (2, 3):
                weights_plane_out(my_z, step, w).start()
        for w in waves:
            each(0, my_z, lambda z, w=w: weights_z(my_z, z, w).start())

    def send_up():
        for w in waves:
            each(0, zs - 1 - my_z, lambda i, w=w: weights_z(my_z, zs - 1 - i, w).start())

    def forward_group(group):
        for w in waves:
            weights_z(group, my_z, w).wait_recv()
            for step in (1, 2, 3):
                weights_plane_out(group, step, w).start()

    def pass_group(group):
        for w in waves:

            @pl.when(group != my_z)
            def _(w=w):
                weights_plane_in(group, 1, w).wait_recv()
                weights_core(2 * group + my_x, my_c, w).start()

            for step in (2, 3):
                weights_plane_in(group, step, w).wait_recv()
            weights_core(2 * group + 1 - my_x, my_c, w).start()

    def take_group(group):
        for w in waves:

            @pl.when(group != my_z)
            def _(w=w):
                weights_core(2 * group + my_x, 1 - my_c, w).wait_recv()

            weights_core(2 * group + 1 - my_x, 1 - my_c, w).wait_recv()

    def unpack(low, high):
        for share in range(2 * low, 2 * high):
            for h in range(2):
                for r, w, start in quarters:
                    flat[h, pl.ds(share * plan.flat + start, quarter), :] = gathered[
                        share, h, r, w
                    ].astype(F32)

    def column_of(turned, j):
        return jnp.broadcast_to(turned[:, j : j + 1], (128, 128)).astype(BF16)

    def mixer_weights(layer):
        for h in range(2):
            lanes = slice(128 * h, 128 * (h + 1))
            base = plan.base(layer)
            turned = jnp.transpose(flat[h, pl.ds(base, 128), :])
            for j in range(4):
                norms[layer, j, lanes] = column_of(turned, j)
            base += 4
            for j in range(3):
                value = flat[h, pl.ds(base + j, width, stride=3), :]
                place = slice(width * j + 128 * h, width * j + 128 * (h + 1))
                wqkv[layer, :, place] = value.astype(BF16)
                wqkv_t[layer, place] = jnp.transpose(value).astype(BF16)
            base += 3 * width
            value = flat[h, pl.ds(base, width), :]
            wo[layer, :, lanes] = value.astype(BF16)
            wo_t[layer, lanes] = jnp.transpose(value).astype(BF16)

    parts = hidden // width

    def hidden_weights(layer):
        for h in range(2):
            lanes = slice(128 * h, 128 * (h + 1))
            base = plan.base(layer) + plan.mixer
            for j in range(parts):
                value = flat[h, pl.ds(base + j, width, stride=parts), :]
                place = slice(width * j + 128 * h, width * j + 128 * (h + 1))
                wup[layer, :, place] = value.astype(BF16)
                wup_t[layer, place] = jnp.transpose(value).astype(BF16)
            base += hidden
            turned = jnp.transpose(flat[h, pl.ds(base, 128), :])
            for j in range(parts):
                place = slice(width * j + 128 * h, width * j + 128 * (h + 1))
                bup[layer, place] = column_of(turned, j)
            base += parts
            value = flat[h, pl.ds(base, hidden), :]
            wd[layer, :, lanes] = value.astype(BF16)
            wd_t[layer, lanes] = jnp.transpose(value).astype(BF16)

    reach_a, reach_b = plan.reach[0, "mixer"], plan.reach[0, "hidden"]
    reach_c, reach_d = plan.reach[1, "mixer"], plan.reach[1, "hidden"]

    def first_groups(group):
        @pl.when(group != my_z)
        def _():
            forward_group(group)

    send_near()
    send_up()
    each(0, reach_a, first_groups)

    each_other_z(reach_a, reach_b, forward_group)
    qmask[...] = jnp.zeros_like(qmask)
    domask[...] = jnp.zeros_like(domask)
    gnorm[...] = jnp.zeros_like(gnorm)
    gemb[...] = jnp.zeros_like(gemb)
    ones = jnp.ones((16, rows), BF16)
    gbuf[...] = jnp.transpose(cot[...].astype(F32))
    each(0, reach_a, pass_group)

    each(0, reach_a, take_group)
    unpack(0, reach_a)

    depth_row = lax.broadcasted_iota(jnp.int32, (128, 128), 0)
    for h in range(2):
        lanes = slice(128 * h, 128 * (h + 1))
        block = flat[h, :128]
        turned = jnp.transpose(block)
        rbias[lanes] = jnp.broadcast_to(turned[:, plan.depth : plan.depth + 1], (128, 128))
        block = jnp.where(depth_row < plan.depth, block, 0.0)
        rin[:, lanes] = block.astype(BF16)
        rit[lanes] = jnp.transpose(block).astype(BF16)
    mixer_weights(0)

    embedded = mm(rit[...], masked_all[me]) + twice(rbias[...])
    emb[...] = embedded
    hid[0] = embedded

    def normed_copy(app, block, target, slot):
        return remote(
            nrm.at[app, block], nrm.at[app, block], send_n.at[app, slot], recv_n.at[app, block],
            {"seq": target},
        )

    def grad_copy(app, block, target, slot):
        return remote(
            nrm.at[app, block], nrm.at[app, me], send_g.at[app, slot], recv_g.at[app, me],
            {"seq": target},
        )

    def near_copy(app, target):
        return remote(
            merge.at[app], nrm.at[app, me], send_g.at[app, 0], recv_g.at[app, me], {"seq": target}
        )

    def grad_arrival(app, source):
        return remote(
            nrm.at[app, source], nrm.at[app, source], send_g.at[app, 0], recv_g.at[app, source],
            {"seq": source},
        )

    def turn_of(app):
        return pl.ds(pl.multiple_of(app * rows, rows), rows)

    def merge_copy(app):
        return remote(
            vt.at[:, turn_of(app)], merge.at[app], send_g.at[app, 1], recv_m.at[app], sibling
        )

    causal = lax.broadcasted_iota(jnp.int32, (rows, rows), 0) <= lax.broadcasted_iota(
        jnp.int32, (rows, rows), 1
    )

    def mask_last(values, fill):
        before = values.shape[0] - rows
        last_block = jnp.where(causal, values[before:], fill)
        return jnp.concatenate([values[:before], last_block], axis=0) if before else last_block

    def project_block(app, layer, block):
        block_t = nrm[app, block]
        places = slice(block * rows, (block + 1) * rows)
        both = mm(wqkv_t[layer, width:], block_t).astype(BF16)
        kt[app, :, places] = both[:width]
        vt[:, places] = both[width:]
        kv[app, places] = mm(
            jnp.transpose(block_t.astype(F32)).astype(BF16), wqkv[layer, :, width:]
        ).astype(BF16)

    far_peak, far_total = ref.far_peak, ref.far_total

    def soften(app, keys, tops, sums, diagonal):
        for head in range(HEADS):
            scores = mm(kv[app, keys, :width], qmask[head]) * exp_scale
            if diagonal:
                scores = mask_last(scores, -jnp.inf)
            top = jnp.max(scores, axis=0, keepdims=True)
            weight = jnp.exp2(scores - top)
            tops[head : head + 1] = top
            sums[head : head + 1] = jnp.sum(weight, axis=0, keepdims=True)
            ps[head, keys] = weight.astype(BF16)

    def mix(head, keys):
        lanes = slice(head * head_width, (head + 1) * head_width)
        return lanes, mm(vt[lanes, keys], ps[head, keys])

    def finish_heads(app, keys, far):
        for head in range(HEADS):
            lanes, out = mix(head, keys)
            row = slice(head, head + 1)
            if far:
                top = jnp.maximum(peak[row], far_peak[row])
                fade, far_fade = jnp.exp2(peak[row] - top), jnp.exp2(far_peak[row] - top)
                out = hid[app + 1, lanes] * fade + out * far_fade
                peak[row] = top
                total[row] = total[row] * fade + far_total[row] * far_fade
            out = out * (1.0 / total[row])
            osave[app, lanes] = out
            att[app, lanes] = out.astype(BF16)
        lse[app] = peak[...] + jnp.log2(total[...])

    def first_normed(block):
        points_copy(block, me).wait_recv()
        unit, _ = normalise(mm(rit[...], masked_all[block]) + twice(rbias[...]))
        nrm[0, block] = (unit * twice(norms[0, 0]) + twice(norms[0, 1])).astype(BF16)

    def gather_blocks(app, layer, place):
        project_block(app, layer, place)
        near, far = place - 2, 1 - (place - 2)

        @pl.when(app == 0)
        def _():
            each(0, place, first_normed)

        if place % 2 == 1:

            @pl.when(app > 0)
            def _():
                normed_copy(app, place - 1, me, 0).wait_recv()

            project_block(app, layer, place - 1)

        def pass_near():
            normed_copy(app, near, me, 0).wait_recv()
            normed_copy(app, near, place + 1 - 2 * (place % 2), 2).start()

        keys = slice(place // 2 * 2 * rows, (place + 1) * rows)
        if place < 2:
            soften(app, keys, peak, total, True)
            finish_heads(app, keys, False)
        else:
            pl.when(app > 1)(pass_near)
            soften(app, keys, peak, total, True)
            for head in range(HEADS):
                lanes, out = mix(head, keys)
                hid[app + 1, lanes] = out
            pl.when(app == 1)(pass_near)
            project_block(app, layer, near)

            @pl.when(app > 0)
            def _():
                normed_copy(app, far, me, 0).wait_recv()

            project_block(app, layer, far)
            far_keys = slice(0, 2 * rows)
            soften(app, far_keys, far_peak, far_total, False)
            finish_heads(app, far_keys, True)

    def forward(app, carry):
        layer = lax.rem(app, LAYERS)

        @pl.when(app == 1)
        def _():
            each(reach_c, reach_d, pass_group)
            each(reach_b, reach_c, take_group)
            unpack(reach_b, reach_c)
            mixer_weights(1)

        unit, _ = normalise(hid[app])
        normed = (unit * twice(norms[layer, 0]) + twice(norms[layer, 1])).astype(BF16)
        nrm[app, me] = normed

        @pl.when((my_y == 0) & (app > 0))
        def _():
            normed_copy(app, me, me + 2, 1).start()

        @pl.when((my_c == 0) & (app > 0))
        def _():
            normed_copy(app, me, me + 1, 0).start()

        queries = mm(wqkv_t[layer, :width], normed).astype(BF16)
        qsave[app] = queries
        for head in range(HEADS):
            lanes = slice(head * head_width, (head + 1) * head_width)
            qmask[head, lanes] = queries[lanes]

        for place in range(SEQ):

            @pl.when(me == place)
            def _(place=place):
                gather_blocks(app, layer, place)

        updated = hid[app] + mm(wo_t[layer], att[app])
        upd[app] = updated
        unit, _ = normalise(updated)
        second = (unit * twice(norms[layer, 2]) + twice(norms[layer, 3])).astype(BF16)
        nrm2[app] = second

        @pl.when(app == 0)
        def _():
            each(reach_a, reach_c, pass_group)
            each_other_z(reach_b, reach_d, forward_group)
            each(reach_a, reach_b, take_group)
            unpack(reach_a, reach_b)
            hidden_weights(0)

        @pl.when(app == 1)
        def _():
            each(reach_c, reach_d, take_group)
            unpack(reach_c, reach_d)
            hidden_weights(1)

        before = mm(wup_t[layer], nrm2[app]) + twice(bup[layer])
        squared = before * before
        turned = jnp.tanh(before * (GELU_A + (GELU_A * GELU_B) * squared))
        risen = 0.5 * (1.0 + turned)
        act[app] = (before * risen).astype(BF16)
        gp[app] = risen + before * (1.0 - turned * turned) * (
            0.5 * GELU_A + (1.5 * GELU_A * GELU_B) * squared
        )
        result = upd[app] + mm(wd_t[layer], act[app])
        again = jnp.where((layer == LAYERS - 1) & (app < APPS - 1), 1.0, 0.0)
        hid[app + 1] = result + again * emb[...]
        return carry

    lax.fori_loop(0, APPS, forward, 0)
    states[...] = jnp.transpose(hid[APPS]).astype(BF16)

    for w in waves:
        each_other_z(0, zs, lambda z, w=w: weights_z(my_z, z, w).wait_send())
        each_other_z(0, zs, lambda z, w=w: weights_plane_out(z, 1, w).wait_send())
        for step in (2, 3):
            each(0, zs, lambda z, step=step, w=w: weights_plane_out(z, step, w).wait_send())
        each_other_z(0, zs, lambda z, w=w: weights_core(2 * z + my_x, my_c, w).wait_send())
        each(0, zs, lambda z, w=w: weights_core(2 * z + 1 - my_x, my_c, w).wait_send())
    for step in range(1, SEQ):

        @pl.when(me + step < SEQ)
        def _(step=step):
            points_copy(me, me + step).wait_send()


    def normed_sent(app):
        @pl.when(my_c == 0)
        def _():
            normed_copy(app, me, me + 1, 0).wait_send()

        @pl.when(my_y == 0)
        def _():
            normed_copy(app, me, me + 2, 1).wait_send()

        @pl.when(my_y == 1)
        def _():
            normed_copy(app, my_c, my_y * 2 + 1 - my_c, 2).wait_send()

    each(1, APPS, normed_sent)
    flat[:, pl.ds(plan.used, plan.total - plan.used), :] = jnp.zeros(
        (2, plan.total - plan.used, 128), F32
    )

    from_core, from_plane, from_z = ref.from_core, ref.from_plane, ref.from_z
    last, summed = ref.last, ref.summed

    def grads_core(group, w):
        pair = pl.ds(2 * group, 2)
        return remote(
            gathered.at[pair, 1 - my_c, :, w], from_core.at[pair, :, w],
            ref.send_gc.at[group, w], ref.recv_gc.at[group, w], sibling,
        )

    def grads_plane(group, step, w):
        x, y, device = in_plane(step)
        return remote(
            gathered.at[2 * group + x, my_c, y, w], from_plane.at[group, here, w],
            ref.send_gp.at[group, step, w], ref.recv_gp.at[group, here, w], device,
        )

    def grads_plane_in(group, step, w):
        x, y, device = in_plane(step)
        place = x * 2 + y
        return place, remote(
            gathered.at[2 * group + my_x, my_c, my_y, w], from_plane.at[group, place, w],
            ref.send_gp.at[group, step, w], ref.recv_gp.at[group, place, w], device,
        )

    def grads_z(source_z, target_z, w):
        return remote(
            gathered.at[2 * target_z + my_x, my_c, my_y, w], from_z.at[source_z, w],
            ref.send_gz.at[target_z, w], ref.recv_gz.at[source_z, w],
            {"dp": 2 * target_z + my_x},
        )

    def round_group(low, high):
        def body(group):
            for w in waves:
                for h in range(2):
                    for x in range(2):
                        for r in range(2):
                            start = (2 * group + x) * plan.flat + (2 * r + w) * quarter
                            gathered[2 * group + x, h, r, w] = flat[
                                h, pl.ds(start, quarter), :
                            ].astype(BF16)
                grads_core(group, w).start()

        each(low, high, body)

    def plane_group(low, high):
        def body(group):
            for w in waves:
                grads_core(group, w).wait()
                for step in (3, 2, 1, 0):
                    x, y, _ = in_plane(step)
                    share = 2 * group + x
                    gathered[share, my_c, y, w] = (
                        gathered[share, my_c, y, w].astype(F32) + from_core[share, y, w].astype(F32)
                    ).astype(BF16)
                    if step:
                        grads_plane(group, step, w).start()

        each(low, high, body)

    def rise_group(low, high):
        def body(group):
            for w in waves:
                value = gathered[2 * group + my_x, my_c, my_y, w].astype(F32)
                for step in (1, 2, 3):
                    place, arrival = grads_plane_in(group, step, w)
                    arrival.wait_recv()
                    value = value + from_plane[group, place, w].astype(F32)
                gathered[2 * group + my_x, my_c, my_y, w] = value.astype(BF16)

                @pl.when(group != my_z)
                def _(w=w):
                    grads_z(my_z, group, w).start()

                @pl.when(group == my_z)
                def _(w=w, value=value):
                    last[w] = value

        each(low, high, body)

    first_low, first_from, first_places, first_rise, first_levels, first_sum = (
        ref.first_low, ref.first_from, ref.first_places, ref.first_rise, ref.first_levels, ref.first_sum,
    )

    def first_core():
        return remote(
            first_low.at[1 - my_c], first_from, ref.send_f.at[0], ref.recv_fc.at[0], sibling
        )

    def first_plane(step):
        _, _, device = in_plane(step)
        return remote(
            first_low.at[my_c], first_places.at[here],
            ref.send_f.at[step], ref.recv_fp.at[here], device,
        )

    def first_plane_in(step):
        x, y, device = in_plane(step)
        place = x * 2 + y
        return place, remote(
            first_low.at[my_c], first_places.at[place],
            ref.send_f.at[step], ref.recv_fp.at[place], device,
        )

    def first_z(b, source):
        return remote(
            first_rise.at[b], first_levels.at[source], ref.send_f.at[5 + b],
            ref.recv_fz.at[source], {"dp": 2 * plan.late[b][0] + my_x},
        )

    def first_share(column):
        piece = first_sum.at[column]
        return remote(piece, piece, ref.send_f.at[4], ref.recv_fs.at[0], sibling)

    def to_first_x(body):
        @pl.when(my_x == 0)
        def _():
            body(1)

        @pl.when(my_x == 1)
        def _():
            body(2)
            body(3)

    def share_sum(kind, w, column, half, device):
        piece = summed.at[column, half, w]
        return remote(
            piece, piece, ref.send_gs.at[kind, w], ref.recv_gs.at[kind, w], device
        )

    def collect(low, high):
        def when_mine(group):
            @pl.when(group == my_z)
            def _():
                for w in waves:

                    def body(z, w=w):
                        grads_z(z, my_z, w).wait_recv()
                        last[w] += from_z[z, w].astype(F32)

                    each_other_z(0, zs, body)
                    summed[my_c, my_y, w] = last[w].astype(BF16)
                    share_sum(1, w, my_c, my_y, across).start()
                    share_sum(0, w, my_c, my_y, sibling).start()

        each(low, high, when_mine)

    def first_group(row):
        return min(zs, -(-row // (2 * plan.flat)))

    group_a = first_group(plan.base(1) + plan.mixer)
    group_b = first_group(plan.base(0) + plan.mixer)
    group_e = plan.settled

    def accumulate(app, layer, offset, stride, value, again=False):
        start = plan.base(0) + layer * plan.block + offset
        count = value.shape[0]
        for h in range(2):
            place = (h, pl.ds(start, count, stride=stride), slice(None))
            part = value[:, 128 * h : 128 * (h + 1)]
            kept = flat[place]
            flat[place] = part + (kept if again else jnp.where(app < LAYERS, kept, 0.0))

    part_q, held = emb, hid.at[APPS]

    def soften_back(app, keys, diagonal):
        for head in range(HEADS):
            scores = mm(kv[app, keys, :width], qmask[head]) * exp_scale
            weight = jnp.exp2(scores - lse[app, head : head + 1])
            if diagonal:
                weight = mask_last(weight, 0.0)
            ps[head, keys] = weight.astype(BF16)
            grad = mm(kv[app, keys, width:], domask[head])
            ds[head, keys] = (weight * (grad - total[head : head + 1])).astype(BF16)

    def heads_back(app, keys, own, added):
        for head in range(HEADS):
            lanes = slice(head * head_width, (head + 1) * head_width)
            key_lanes = slice(width + head * head_width, width + (head + 1) * head_width)
            value_lanes = slice(2 * width + head * head_width, 2 * width + (head + 1) * head_width)
            dqkv[key_lanes, keys] = (
                mm_nt(qsave[app, lanes], ds[head, keys]) * score_scale
            ).astype(BF16)
            dqkv[value_lanes, keys] = mm_nt(grad_low[lanes], ps[head, keys]).astype(BF16)
            part = mm(kt[app, lanes, keys], ds[head, keys])
            if own is None:
                part_q[lanes] = part
            else:
                part = part + part_q[lanes] if added else part
                dqkv[lanes, own] = (part * score_scale).astype(BF16)

    def span_of(low, high):
        return slice(low * rows, high * rows)

    def normed_back(layer, first, block):
        return mm(wqkv[layer, :, first:], dqkv[first:, span_of(block, block + 1)])

    def weights_back(app, layer, first, block, again):
        grads = mm_nt(nrm[app, block], dqkv[first:, span_of(block, block + 1)])
        for j in range(first // width, 3):
            accumulate(
                app, layer, 4 + j, 3, grads[:, width * j - first : width * (j + 1) - first],
                again=j > 0 and again,
            )

    def attend_back(app, layer, place):
        start = place // 2 * 2
        if start:
            kept, passed = place % 2, 1 - place % 2
            soften_back(app, span_of(0, start), False)
            heads_back(app, span_of(0, start), None, False)
            vt[:, turn_of(app)] = normed_back(layer, width, passed).astype(BF16)
            merge_copy(app).start()
            held[...] = normed_back(layer, width, kept)
            weights_back(app, layer, width, passed, False)
            weights_back(app, layer, width, kept, True)
        soften_back(app, span_of(start, place + 1), True)
        if start:
            merge_copy(app).wait_recv()
            nrm[app, kept] = (held[...] + merge[app].astype(F32)).astype(BF16)
            grad_copy(app, kept, kept, 2).start()
        heads_back(app, span_of(start, place + 1), span_of(place, place + 1), bool(start))
        if place % 2:
            merge[app] = normed_back(layer, width, place - 1).astype(BF16)
            near_copy(app, place - 1).start()
            weights_back(app, layer, width, place - 1, bool(start))
        gin[...] = normed_back(layer, 0, place)
        weights_back(app, layer, 0, place, bool(start) or place % 2 == 1)

    def flush_norms(layer):
        start = plan.base(0) + layer * plan.block
        for h in range(2):
            for j in range(4):
                flat[h, pl.ds(start + j, 1), :] = jnp.sum(
                    jnp.transpose(gnorm[layer, j, 128 * h : 128 * (h + 1)]), axis=0, keepdims=True
                )

    def backward(order, carry):
        app = APPS - 1 - order
        layer = lax.rem(app, LAYERS)

        @pl.when((app == 0) & (my_y == 1))
        def _():
            plane_group(group_e, group_a)

        out_low = gbuf[...].astype(BF16)
        accumulate(app, layer, plan.mixer + hidden + parts, 1, mm_nt(act[app], out_low))
        pre_low = (mm(wd[layer], out_low) * gp[app]).astype(BF16)
        act[app] = pre_low
        for j in range(parts):
            part = act[app, width * j : width * (j + 1)]
            accumulate(app, layer, plan.mixer + j, parts, mm_nt(nrm2[app], part))
            accumulate(app, layer, plan.mixer + hidden + j, 1, mm_nt(ones, part)[:1])

        @pl.when(app == 1)
        def _():
            round_group(group_a, zs)

        @pl.when(app == 0)
        def _():
            round_group(group_b, group_e)

        grad_second = mm(wup[layer], act[app])
        unit, scale = normalise(upd[app])
        gnorm[layer, 2] += halves(grad_second * unit)
        gnorm[layer, 3] += halves(grad_second)
        grad_updated = gbuf[...] + normalise_back(grad_second, unit, scale, twice(norms[layer, 2]))
        gbuf[...] = grad_updated
        branch_low = grad_updated.astype(BF16)
        accumulate(app, layer, 4 + 3 * width, 1, mm_nt(att[app], branch_low))
        grad_att = mm(wo[layer], branch_low).astype(BF16)
        grad_low[...] = grad_att
        for head in range(HEADS):
            lanes = slice(head * head_width, (head + 1) * head_width)
            domask[head, lanes] = grad_att[lanes]
            qmask[head, lanes] = qsave[app, lanes]
            total[head : head + 1] = jnp.sum(
                osave[app, lanes] * grad_att[lanes].astype(F32), axis=0, keepdims=True
            )

        @pl.when(app == 1)
        def _():
            plane_group(group_a, zs)

        @pl.when(app == 0)
        def _():
            rise_group(group_a, zs)
            plane_group(group_b, group_e)

        for place in range(SEQ):

            @pl.when(me == place)
            def _(place=place):
                attend_back(app, layer, place)

        @pl.when(app == 0)
        def _():
            round_group(0, group_b)
            rise_group(group_e, group_a)
            plane_group(0, group_b)
            rise_group(group_b, group_e)

        @pl.when(app == 1)
        def _():
            round_group(group_e, group_a)

        @pl.when((app == 1) & (my_y == 0))
        def _():
            plane_group(group_e, group_a)

        def arrive(source):
            grad_arrival(app, source).wait_recv()
            gin[...] += nrm[app, source].astype(F32)

        @pl.when(my_c == 0)
        def _():
            arrive(me + 1)

        @pl.when(my_y == 0)
        def _():
            arrive(me + 2)

        grad_normed = gin[...]
        unit, scale = normalise(hid[app])
        gnorm[layer, 0] += halves(grad_normed * unit)
        gnorm[layer, 1] += halves(grad_normed)
        grad_in = gbuf[...] + normalise_back(grad_normed, unit, scale, twice(norms[layer, 0]))
        gbuf[...] = grad_in
        first = jnp.where(layer == 0, 1.0, 0.0)
        gemb[...] += first * grad_in

        @pl.when(app < LAYERS)
        def _():
            flush_norms(layer)

        return carry

    lax.fori_loop(0, APPS, backward, 0)
    embed_low = gemb[...].astype(BF16)
    grad_in_rows = mm_nt(masked_all[me], embed_low)
    grad_bias_rows = mm_nt(ones, embed_low)
    for h in range(2):
        lanes = slice(128 * h, 128 * (h + 1))
        flat[h, : plan.depth] = grad_in_rows[: plan.depth, lanes]
        flat[h, plan.depth : plan.depth + 1] = grad_bias_rows[:1, lanes]
    for b, (group, _) in enumerate(plan.late):
        for h in range(2):
            first_low[h, b] = flat[h, pl.ds(2 * group * plan.flat, FIRST), :].astype(BF16)
    first_core().start()
    point_grad[...] = jnp.where(depth_mask, mm(rin[...], embed_low)[: plan.depth], 0.0)
    first_core().wait()
    first_low[my_c] = (first_low[my_c].astype(F32) + first_from[...].astype(F32)).astype(BF16)
    to_first_x(lambda step: first_plane(step).start())
    rise_group(0, group_b)

    @pl.when(my_x == 0)
    def _():
        first_places[here] = first_low[my_c]
        for step in (1, 2, 3):
            place, arrival = first_plane_in(step)
            arrival.wait_recv()
        first_rise[...] = sum(first_places[place].astype(F32) for place in range(4)).astype(BF16)

        for b, (group, _) in enumerate(plan.late):

            @pl.when(my_z != group)
            def _(b=b):
                first_z(b, my_z).start()

    collect(0, zs)
    for b, (group, _) in enumerate(plan.late):

        @pl.when(owner == 2 * group)
        def _(b=b):
            first_levels[my_z] = first_rise[b]
            each_other_z(0, zs, lambda z: first_z(b, z).wait_recv())
            first_sum[my_c] = sum(first_levels[z].astype(F32) for z in range(zs)).astype(BF16)
            first_share(my_c).start()

    for w in waves:
        share_sum(1, w, my_c, 1 - my_y, across).wait_recv()
        share_sum(2, w, my_c, 1 - my_y, sibling).start()
    for w in waves:
        share_sum(0, w, 1 - my_c, my_y, sibling).wait_recv()
    for w in waves:
        share_sum(2, w, 1 - my_c, 1 - my_y, sibling).wait_recv()
    for h in range(2):
        for r, w, start in quarters:
            count = min(quarter, plan.flat - start)
            if count > 0:
                flat[0, pl.ds(2 * start + h, count, stride=2), :] = summed[h, r, w].astype(F32)[
                    :count
                ]
    for group, count in plan.late:

        @pl.when(owner == 2 * group)
        def _(count=count):
            first_share(1 - my_c).wait_recv()
            for h in range(2):
                flat[0, pl.ds(h, count, stride=2), :] = first_sum[h].astype(F32)[:count]

    gradients[...] = flat[0, : gradients.shape[0]].astype(BF16)

    to_first_x(lambda step: first_plane(step).wait_send())

    for b, (group, _) in enumerate(plan.late):

        @pl.when((my_x == 0) & (my_z != group))
        def _(b=b):
            first_z(b, my_z).wait_send()

        @pl.when(owner == 2 * group)
        def _():
            first_share(my_c).wait_send()

    for w in waves:
        for step in (1, 2, 3):
            each(0, zs, lambda z, step=step, w=w: grads_plane(z, step, w).wait_send())
        each_other_z(0, zs, lambda z, w=w: grads_z(my_z, z, w).wait_send())
        share_sum(0, w, my_c, my_y, sibling).wait_send()
        share_sum(1, w, my_c, my_y, across).wait_send()
        share_sum(2, w, my_c, 1 - my_y, sibling).wait_send()

    def finish(app):
        @pl.when(my_c == 1)
        def _():
            near_copy(app, me - 1).wait_send()

        @pl.when(my_y == 1)
        def _():
            merge_copy(app).wait_send()
            grad_copy(app, my_c, my_c, 2).wait_send()

    each(0, APPS, finish)


def update_kernel(
    summed, weights, momenta, averages, states, point_grad,
    grad_out, fresh_out, momentum_out, mean_out, states_out, point_out,
):
    grad = summed[...].astype(F32)
    momentum = MOMENTUM * momenta[...] + grad
    fresh = weights[...] - RATE * (grad + MOMENTUM * momentum)
    grad_out[...] = grad
    momentum_out[...] = momentum
    fresh_out[...] = fresh
    mean_out[...] = AVERAGE_DECAY * averages[...] + (1.0 - AVERAGE_DECAY) * fresh

    @pl.when(pl.program_id(0) == 0)
    def _():
        states_out[...] = states[...]
        for row in range(point_grad.shape[0]):
            point_out[row] = point_grad[row : row + 1]


def shards(points, counts, cotangent, weights, momenta, averages):
    rows, depth = points.shape[1:]
    width = cotangent.shape[2]
    share = weights.shape[0]
    plan = Plan(rows, depth, width, share, lax.axis_size("dp"), lax.axis_size("seq"))
    hidden, dp_count, zs, quarter = plan.hidden, plan.dp, plan.zs, plan.quarter
    vmem = pl.BlockSpec(memory_space=pltpu.VMEM)
    smem = pl.BlockSpec(memory_space=pltpu.SMEM)
    shape = jax.ShapeDtypeStruct
    lines = (share // 128, 128)
    outs = (shape((rows, width), BF16), shape((depth, rows), F32), shape(lines, BF16))
    low = lambda *dims: pltpu.VMEM(dims, BF16)
    full = lambda *dims: pltpu.VMEM(dims, F32)
    flags = lambda *dims: pltpu.SemaphoreType.DMA(dims)
    scratch = dict(
        gathered=low(dp_count, 2, 2, 2, quarter, 128),
        flat=full(2, plan.space, 128),
        rin=low(128, width),
        rit=low(width, 128),
        rbias=full(width, 128),
        norms=low(LAYERS, 4, width, 128),
        bup=low(LAYERS, hidden, 128),
        wqkv=low(LAYERS, width, 3 * width),
        wqkv_t=low(LAYERS, 3 * width, width),
        wo=low(LAYERS, width, width),
        wo_t=low(LAYERS, width, width),
        wup=low(LAYERS, width, hidden),
        wup_t=low(LAYERS, hidden, width),
        wd=low(LAYERS, hidden, width),
        wd_t=low(LAYERS, width, hidden),
        masked_all=low(SEQ, 128, rows),
        gnorm=full(LAYERS, 4, width, 128),
        from_core=low(dp_count, 2, 2, quarter, 128),
        from_plane=low(zs, 4, 2, quarter, 128),
        from_z=low(zs, 2, quarter, 128),
        last=full(2, quarter, 128),
        first_low=low(2, len(plan.late), FIRST, 128),
        first_from=low(len(plan.late), FIRST, 128),
        first_places=low(4, len(plan.late), FIRST, 128),
        first_rise=low(len(plan.late), FIRST, 128),
        first_levels=low(zs, FIRST, 128),
        first_sum=low(2, FIRST, 128),
        send_f=flags(5 + len(plan.late)),
        recv_fc=flags(1),
        recv_fp=flags(4),
        recv_fz=flags(zs),
        recv_fs=flags(1),
        summed=low(2, 2, 2, quarter, 128),
        hid=full(APPS + 1, width, rows),
        nrm=low(APPS, SEQ, width, rows),
        qsave=low(APPS, width, rows),
        kv=low(APPS, SEQ * rows, 2 * width),
        kt=low(APPS, width, SEQ * rows),
        vt=low(width, SEQ * rows),
        att=low(APPS, width, rows),
        osave=full(APPS, width, rows),
        lse=full(APPS, HEADS, rows),
        upd=full(APPS, width, rows),
        nrm2=low(APPS, width, rows),
        gp=full(APPS, hidden, rows),
        act=low(APPS, hidden, rows),
        emb=full(width, rows),
        qmask=low(HEADS, width, rows),
        domask=low(HEADS, width, rows),
        ps=low(HEADS, SEQ * rows, rows),
        ds=low(HEADS, SEQ * rows, rows),
        dqkv=low(3 * width, SEQ * rows),
        grad_low=low(width, rows),
        peak=full(HEADS, rows),
        total=full(HEADS, rows),
        far_peak=full(HEADS, rows),
        far_total=full(HEADS, rows),
        gbuf=full(width, rows),
        gemb=full(width, rows),
        gin=full(width, rows),
        merge=low(APPS, width, rows),
        send_n=flags(APPS, 3),
        recv_n=flags(APPS, SEQ),
        send_g=flags(APPS, 3),
        recv_g=flags(APPS, SEQ),
        recv_m=flags(APPS),
        send_p=flags(SEQ),
        recv_p=flags(SEQ),
        send_wz=flags(zs, 2),
        recv_wz=flags(zs, 2),
        send_wp=flags(zs, 4, 2),
        recv_wp=flags(zs, 4, 2),
        send_wc=flags(dp_count, 2),
        recv_wc=flags(dp_count, 2),
        send_gc=flags(zs, 2),
        recv_gc=flags(zs, 2),
        send_gp=flags(zs, 4, 2),
        recv_gp=flags(zs, 4, 2),
        send_gz=flags(zs, 2),
        recv_gz=flags(zs, 2),
        send_gs=flags(3, 2),
        recv_gs=flags(3, 2),
    )
    mine = weights.reshape(lines)
    states, point_grad, summed = pl.pallas_call(
        functools.partial(whole_kernel, plan, tuple(scratch)),
        out_shape=outs,
        in_specs=[vmem, smem, vmem, vmem],
        out_specs=(vmem,) * len(outs),
        scratch_shapes=list(scratch.values()),
        compiler_params=pltpu.CompilerParams(
            collective_id=0, has_side_effects=True, vmem_limit_bytes=63 * 1024 * 1024
        ),
    )(points[0].T, counts, cotangent[0], mine)
    vector = shape(lines, F32)
    step_rows = min(776, lines[0])
    line_block = pl.BlockSpec((step_rows, 128), lambda i: (i, 0))
    states_block = pl.BlockSpec((rows, width), lambda i: (0, 0))
    point_block = pl.BlockSpec((depth, rows), lambda i: (0, 0))
    grad, fresh, momentum, mean, states, point_grad = pl.pallas_call(
        update_kernel,
        grid=(-(-lines[0] // step_rows),),
        out_shape=(
            vector, vector, vector, vector, shape((rows, width), BF16), shape((depth, 1, rows), F32),
        ),
        in_specs=[line_block] * 4 + [states_block, point_block],
        out_specs=(
            line_block, line_block, line_block, line_block, states_block,
            pl.BlockSpec((depth, 1, rows), lambda i: (0, 0, 0)),
        ),
        compiler_params=pltpu.CompilerParams(vmem_limit_bytes=63 * 1024 * 1024),
    )(summed, mine, momenta.reshape(lines), averages.reshape(lines), states, point_grad)
    return (
        states[None], jnp.transpose(point_grad, (1, 2, 0)),
        *(v.reshape(-1) for v in (grad, fresh, momentum, mean)),
    )


def solution(mesh):
    placed = (P("dp", "seq", None), P("dp"), P("dp", "seq", None), P("dp"), P("dp"), P("dp"))
    return jax.shard_map(
        shards,
        mesh=mesh,
        in_specs=placed,
        out_specs=(P("dp", "seq", None), P("dp", "seq", None), P("dp"), P("dp"), P("dp"), P("dp")),
        check_vma=False,
    )
```

```python
import functools
import math
import types

import jax
import jax.numpy as jnp
from jax import lax
from jax.experimental import pallas as pl
from jax.experimental.pallas import tpu as pltpu
from jax.sharding import PartitionSpec as P

MESH = pl.DeviceIdType.MESH
HEADS = 8
FF = 1024
LAYERS = 2
LOOPS = 2
APPS = LAYERS * LOOPS

EPSILON = 1e-05
RATE = 0.0003
MOMENTUM = 0.5
AVERAGE_DECAY = 0.9

F32 = jnp.float32
BF16 = jnp.bfloat16
GELU_A = math.sqrt(2.0 / math.pi)
GELU_B = 0.044715
SEQ = 4
FIRST = 32


def mm(left, right):
    return jnp.dot(left, right, preferred_element_type=F32)


def mm_nt(left, right):
    return lax.dot_general(left, right, (((1,), (1,)), ((), ())), preferred_element_type=F32)


def twice(column):
    column = column.astype(F32)
    return jnp.concatenate([column, column], axis=1)


def halves(values):
    return values[:, :128] + values[:, 128:]


def normalise(values):
    centred = values - jnp.mean(values, axis=0, keepdims=True)
    variance = jnp.mean(centred * centred, axis=0, keepdims=True)
    scale = lax.rsqrt(variance + EPSILON)
    return centred * scale, scale


def normalise_back(grad, unit, scale, gain):
    scaled = grad * gain
    first = jnp.mean(scaled, axis=0, keepdims=True)
    second = jnp.mean(scaled * unit, axis=0, keepdims=True)
    return (scaled - first - unit * second) * scale


class Plan:
    def __init__(self, rows, depth, width, share, dp_count, seq_count):
        self.rows = rows
        self.depth = depth
        self.width = width
        self.hidden = FF
        self.dp = dp_count
        self.zs = dp_count // 2
        self.seq = seq_count
        self.flat = share // width
        self.quarter = -(-self.flat // 64) * 16
        self.mixer = 4 + 3 * width + width
        self.block = self.mixer + FF + FF // width + FF
        self.total = self.flat * dp_count
        self.space = self.total + 64 + width
        self.used = self.base(LAYERS)
        self.reach = {
            (layer, part): min(self.zs, -(-(self.base(layer) + rows_here) // (2 * self.flat)))
            for layer in range(LAYERS)
            for part, rows_here in (("mixer", self.mixer), ("hidden", self.block))
        }
        self.reach[LAYERS - 1, "hidden"] = self.zs
        self.late = [(0, self.base(0) + 4)]
        group, spill = divmod(self.base(1), 2 * self.flat)
        if group and 0 < spill <= FIRST - 4:
            self.late.append((group, spill + 4))
            self.settled = group
        else:
            self.settled = min(self.zs, -(-self.base(1) // (2 * self.flat)))

    def base(self, layer):
        return self.depth + 1 + layer * self.block


def whole_kernel(plan, names, *refs):
    points, counts, cot, weights, states, point_grad, gradients, *scratch = refs
    ref = types.SimpleNamespace(**dict(zip(names, scratch, strict=True)))
    rows, width, hidden = plan.rows, plan.width, plan.hidden
    dp_count, zs, quarter = plan.dp, plan.zs, plan.quarter
    head_width = width // HEADS
    exp_scale = math.log2(math.e) / math.sqrt(head_width)
    score_scale = 1.0 / math.sqrt(head_width)
    quarters = [(r, w, (2 * r + w) * quarter) for r in range(2) for w in range(2)]
    waves = range(2)
    gnorm, hid, nrm, qsave, kv, kt, vt, att = (
        ref.gnorm, ref.hid, ref.nrm, ref.qsave, ref.kv, ref.kt, ref.vt, ref.att,
    )
    osave, lse, upd, nrm2, gp, act, emb, qmask = (
        ref.osave, ref.lse, ref.upd, ref.nrm2, ref.gp, ref.act, ref.emb, ref.qmask,
    )
    domask, ps, ds, dqkv, grad_low, peak, total, gbuf = (
        ref.domask, ref.ps, ref.ds, ref.dqkv, ref.grad_low, ref.peak, ref.total, ref.gbuf,
    )
    gemb, gin, merge, send_n, recv_n, send_g, recv_g, recv_m = (
        ref.gemb, ref.gin, ref.merge, ref.send_n, ref.recv_n, ref.send_g, ref.recv_g, ref.recv_m,
    )
    gathered, flat = (
        ref.gathered, ref.flat,
    )
    rin, rit, rbias, norms, bup = ref.rin, ref.rit, ref.rbias, ref.norms, ref.bup
    wqkv, wqkv_t, wo, wo_t = ref.wqkv, ref.wqkv_t, ref.wo, ref.wo_t
    wup, wup_t, wd, wd_t = ref.wup, ref.wup_t, ref.wd, ref.wd_t

    me = lax.axis_index("seq")
    owner = lax.axis_index("dp")
    my_z, my_x = owner // 2, lax.rem(owner, 2)
    my_y, my_c = me // 2, lax.rem(me, 2)
    sibling = {"seq": my_y * 2 + (1 - my_c)}
    across = {"seq": (1 - my_y) * 2 + my_c}
    here = my_x * 2 + my_y

    def in_plane(step):
        x = lax.rem(my_x + step // 2, 2)
        y = lax.rem(my_y + step % 2, 2)
        return x, y, {"dp": my_z * 2 + x, "seq": y * 2 + my_c}

    barrier = pltpu.get_barrier_semaphore()

    def greet(device):
        pl.semaphore_signal(barrier, inc=1, device_id=device, device_id_type=MESH)

    def greet_z(step, carry):
        greet({"dp": lax.rem(my_z + step, zs) * 2 + my_x})
        return carry

    for step in range(1, plan.seq):
        greet({"seq": lax.rem(me + step, plan.seq)})
    for step in (2, 3):
        greet(in_plane(step)[2])
    lax.fori_loop(1, zs, greet_z, 0)

    def remote(source, target, send, receive, device):
        return pltpu.make_async_remote_copy(
            src_ref=source, dst_ref=target, send_sem=send, recv_sem=receive,
            device_id=device, device_id_type=MESH,
        )

    def each(low, high, body):
        def step(z, carry):
            body(z)
            return carry

        lax.fori_loop(low, high, step, 0)

    def each_other_z(low, high, body):
        def step(z):
            @pl.when(z != my_z)
            def _():
                body(z)

        each(low, high, step)

    for h in range(2):
        for r, w, start in quarters:
            count = min(quarter, plan.flat - start)
            whole_rows = count // 16 * 16
            if whole_rows:
                gathered[owner, h, r, w, :whole_rows] = weights[
                    pl.ds(2 * start + h, whole_rows, stride=2), :
                ].astype(BF16)
            if whole_rows < quarter:
                rest = [jnp.zeros((quarter - count, 128), F32)]
                if whole_rows < count:
                    begin = 2 * (start + whole_rows) + h
                    rest = [weights[pl.ds(begin, count - whole_rows, stride=2), :], *rest]
                gathered[owner, h, r, w, whole_rows:] = jnp.concatenate(rest, axis=0).astype(BF16)

    depth_mask = lax.broadcasted_iota(jnp.int32, (plan.depth, rows), 0) < counts[0]
    gin[...] = jnp.zeros_like(gin)
    gin[: plan.depth] = jnp.where(depth_mask, points[...].astype(F32), 0.0)
    masked_all = ref.masked_all
    masked_all[me] = gin[:128].astype(BF16)

    pl.semaphore_wait(barrier, plan.seq + zs)

    def points_copy(source, target):
        piece = masked_all.at[source]
        return remote(
            piece, piece, ref.send_p.at[target], ref.recv_p.at[source], {"seq": target}
        )

    for step in range(1, SEQ):

        @pl.when(me + step < SEQ)
        def _(step=step):
            points_copy(me, me + step).start()

    def weights_z(source_z, target_z, w):
        piece = gathered.at[2 * source_z + my_x, my_c, my_y, w]
        return remote(
            piece, piece, ref.send_wz.at[target_z, w], ref.recv_wz.at[source_z, w],
            {"dp": 2 * target_z + my_x},
        )

    def weights_plane_out(group, step, w):
        piece = gathered.at[2 * group + my_x, my_c, my_y, w]
        _, _, device = in_plane(step)
        return remote(
            piece, piece, ref.send_wp.at[group, step, w], ref.recv_wp.at[group, here, w],
            device,
        )

    def weights_plane_in(group, step, w):
        x, y, device = in_plane(step)
        piece = gathered.at[2 * group + x, my_c, y, w]
        return remote(
            piece, piece, ref.send_wp.at[group, step, w],
            ref.recv_wp.at[group, x * 2 + y, w], device,
        )

    def weights_core(share, column, w):
        piece = gathered.at[share, column, :, w]
        return remote(
            piece, piece, ref.send_wc.at[share, w], ref.recv_wc.at[share, w], sibling
        )

    def send_near():
        for w in waves:
            for step in (2, 3):
                weights_plane_out(my_z, step, w).start()
        for w in waves:
            each(0, my_z, lambda z, w=w: weights_z(my_z, z, w).start())

    def send_up():
        for w in waves:
            each(0, zs - 1 - my_z, lambda i, w=w: weights_z(my_z, zs - 1 - i, w).start())

    def forward_group(group):
        for w in waves:
            weights_z(group, my_z, w).wait_recv()
            for step in (1, 2, 3):
                weights_plane_out(group, step, w).start()

    def pass_group(group):
        for w in waves:

            @pl.when(group != my_z)
            def _(w=w):
                weights_plane_in(group, 1, w).wait_recv()
                weights_core(2 * group + my_x, my_c, w).start()

            for step in (2, 3):
                weights_plane_in(group, step, w).wait_recv()
            weights_core(2 * group + 1 - my_x, my_c, w).start()

    def take_group(group):
        for w in waves:

            @pl.when(group != my_z)
            def _(w=w):
                weights_core(2 * group + my_x, 1 - my_c, w).wait_recv()

            weights_core(2 * group + 1 - my_x, 1 - my_c, w).wait_recv()

    def unpack(low, high):
        for share in range(2 * low, 2 * high):
            for h in range(2):
                for r, w, start in quarters:
                    flat[h, pl.ds(share * plan.flat + start, quarter), :] = gathered[
                        share, h, r, w
                    ].astype(F32)

    def column_of(turned, j):
        return jnp.broadcast_to(turned[:, j : j + 1], (128, 128)).astype(BF16)

    def mixer_weights(layer):
        for h in range(2):
            lanes = slice(128 * h, 128 * (h + 1))
            base = plan.base(layer)
            turned = jnp.transpose(flat[h, pl.ds(base, 128), :])
            for j in range(4):
                norms[layer, j, lanes] = column_of(turned, j)
            base += 4
            for j in range(3):
                value = flat[h, pl.ds(base + j, width, stride=3), :]
                place = slice(width * j + 128 * h, width * j + 128 * (h + 1))
                wqkv[layer, :, place] = value.astype(BF16)
                wqkv_t[layer, place] = jnp.transpose(value).astype(BF16)
            base += 3 * width
            value = flat[h, pl.ds(base, width), :]
            wo[layer, :, lanes] = value.astype(BF16)
            wo_t[layer, lanes] = jnp.transpose(value).astype(BF16)

    parts = hidden // width

    def hidden_weights(layer):
        for h in range(2):
            lanes = slice(128 * h, 128 * (h + 1))
            base = plan.base(layer) + plan.mixer
            for j in range(parts):
                value = flat[h, pl.ds(base + j, width, stride=parts), :]
                place = slice(width * j + 128 * h, width * j + 128 * (h + 1))
                wup[layer, :, place] = value.astype(BF16)
                wup_t[layer, place] = jnp.transpose(value).astype(BF16)
            base += hidden
            turned = jnp.transpose(flat[h, pl.ds(base, 128), :])
            for j in range(parts):
                place = slice(width * j + 128 * h, width * j + 128 * (h + 1))
                bup[layer, place] = column_of(turned, j)
            base += parts
            value = flat[h, pl.ds(base, hidden), :]
            wd[layer, :, lanes] = value.astype(BF16)
            wd_t[layer, lanes] = jnp.transpose(value).astype(BF16)

    reach_a, reach_b = plan.reach[0, "mixer"], plan.reach[0, "hidden"]
    reach_c, reach_d = plan.reach[1, "mixer"], plan.reach[1, "hidden"]

    def first_groups(group):
        @pl.when(group != my_z)
        def _():
            forward_group(group)

    send_near()
    send_up()
    each(0, reach_a, first_groups)

    each_other_z(reach_a, reach_b, forward_group)
    qmask[...] = jnp.zeros_like(qmask)
    domask[...] = jnp.zeros_like(domask)
    gnorm[...] = jnp.zeros_like(gnorm)
    gemb[...] = jnp.zeros_like(gemb)
    ones = jnp.ones((16, rows), BF16)
    gbuf[...] = jnp.transpose(cot[...].astype(F32))
    each(0, reach_a, pass_group)

    each(0, reach_a, take_group)
    unpack(0, reach_a)

    depth_row = lax.broadcasted_iota(jnp.int32, (128, 128), 0)
    for h in range(2):
        lanes = slice(128 * h, 128 * (h + 1))
        block = flat[h, :128]
        turned = jnp.transpose(block)
        rbias[lanes] = jnp.broadcast_to(turned[:, plan.depth : plan.depth + 1], (128, 128))
        block = jnp.where(depth_row < plan.depth, block, 0.0)
        rin[:, lanes] = block.astype(BF16)
        rit[lanes] = jnp.transpose(block).astype(BF16)
    mixer_weights(0)

    embedded = mm(rit[...], masked_all[me]) + twice(rbias[...])
    emb[...] = embedded
    hid[0] = embedded

    def normed_copy(app, block, target, slot):
        return remote(
            nrm.at[app, block], nrm.at[app, block], send_n.at[app, slot], recv_n.at[app, block],
            {"seq": target},
        )

    def grad_copy(app, block, target, slot):
        return remote(
            nrm.at[app, block], nrm.at[app, me], send_g.at[app, slot], recv_g.at[app, me],
            {"seq": target},
        )

    def near_copy(app, target):
        return remote(
            merge.at[app], nrm.at[app, me], send_g.at[app, 0], recv_g.at[app, me], {"seq": target}
        )

    def grad_arrival(app, source):
        return remote(
            nrm.at[app, source], nrm.at[app, source], send_g.at[app, 0], recv_g.at[app, source],
            {"seq": source},
        )

    def turn_of(app):
        return pl.ds(pl.multiple_of(app * rows, rows), rows)

    def merge_copy(app):
        return remote(
            vt.at[:, turn_of(app)], merge.at[app], send_g.at[app, 1], recv_m.at[app], sibling
        )

    causal = lax.broadcasted_iota(jnp.int32, (rows, rows), 0) <= lax.broadcasted_iota(
        jnp.int32, (rows, rows), 1
    )

    def mask_last(values, fill):
        before = values.shape[0] - rows
        last_block = jnp.where(causal, values[before:], fill)
        return jnp.concatenate([values[:before], last_block], axis=0) if before else last_block

    def project_block(app, layer, block):
        block_t = nrm[app, block]
        places = slice(block * rows, (block + 1) * rows)
        both = mm(wqkv_t[layer, width:], block_t).astype(BF16)
        kt[app, :, places] = both[:width]
        vt[:, places] = both[width:]
        kv[app, places] = mm(
            jnp.transpose(block_t.astype(F32)).astype(BF16), wqkv[layer, :, width:]
        ).astype(BF16)

    far_peak, far_total = ref.far_peak, ref.far_total

    def soften(app, keys, tops, sums, diagonal):
        for head in range(HEADS):
            scores = mm(kv[app, keys, :width], qmask[head]) * exp_scale
            if diagonal:
                scores = mask_last(scores, -jnp.inf)
            top = jnp.max(scores, axis=0, keepdims=True)
            weight = jnp.exp2(scores - top)
            tops[head : head + 1] = top
            sums[head : head + 1] = jnp.sum(weight, axis=0, keepdims=True)
            ps[head, keys] = weight.astype(BF16)

    def mix(head, keys):
        lanes = slice(head * head_width, (head + 1) * head_width)
        return lanes, mm(vt[lanes, keys], ps[head, keys])

    def finish_heads(app, keys, far):
        for head in range(HEADS):
            lanes, out = mix(head, keys)
            row = slice(head, head + 1)
            if far:
                top = jnp.maximum(peak[row], far_peak[row])
                fade, far_fade = jnp.exp2(peak[row] - top), jnp.exp2(far_peak[row] - top)
                out = hid[app + 1, lanes] * fade + out * far_fade
                peak[row] = top
                total[row] = total[row] * fade + far_total[row] * far_fade
            out = out * (1.0 / total[row])
            osave[app, lanes] = out
            att[app, lanes] = out.astype(BF16)
        lse[app] = peak[...] + jnp.log2(total[...])

    def first_normed(block):
        points_copy(block, me).wait_recv()
        unit, _ = normalise(mm(rit[...], masked_all[block]) + twice(rbias[...]))
        nrm[0, block] = (unit * twice(norms[0, 0]) + twice(norms[0, 1])).astype(BF16)

    def gather_blocks(app, layer, place):
        project_block(app, layer, place)
        near, far = place - 2, 1 - (place - 2)

        @pl.when(app == 0)
        def _():
            each(0, place, first_normed)

        if place % 2 == 1:

            @pl.when(app > 0)
            def _():
                normed_copy(app, place - 1, me, 0).wait_recv()

            project_block(app, layer, place - 1)

        def pass_near():
            normed_copy(app, near, me, 0).wait_recv()
            normed_copy(app, near, place + 1 - 2 * (place % 2), 2).start()

        keys = slice(place // 2 * 2 * rows, (place + 1) * rows)
        if place < 2:
            soften(app, keys, peak, total, True)
            finish_heads(app, keys, False)
        else:
            pl.when(app > 1)(pass_near)
            soften(app, keys, peak, total, True)
            for head in range(HEADS):
                lanes, out = mix(head, keys)
                hid[app + 1, lanes] = out
            pl.when(app == 1)(pass_near)
            project_block(app, layer, near)

            @pl.when(app > 0)
            def _():
                normed_copy(app, far, me, 0).wait_recv()

            project_block(app, layer, far)
            far_keys = slice(0, 2 * rows)
            soften(app, far_keys, far_peak, far_total, False)
            finish_heads(app, far_keys, True)

    def forward(app, carry):
        layer = lax.rem(app, LAYERS)

        @pl.when(app == 1)
        def _():
            each(reach_c, reach_d, pass_group)
            each(reach_b, reach_c, take_group)
            unpack(reach_b, reach_c)
            mixer_weights(1)

        unit, _ = normalise(hid[app])
        normed = (unit * twice(norms[layer, 0]) + twice(norms[layer, 1])).astype(BF16)
        nrm[app, me] = normed

        @pl.when((my_y == 0) & (app > 0))
        def _():
            normed_copy(app, me, me + 2, 1).start()

        @pl.when((my_c == 0) & (app > 0))
        def _():
            normed_copy(app, me, me + 1, 0).start()

        queries = mm(wqkv_t[layer, :width], normed).astype(BF16)
        qsave[app] = queries
        for head in range(HEADS):
            lanes = slice(head * head_width, (head + 1) * head_width)
            qmask[head, lanes] = queries[lanes]

        for place in range(SEQ):

            @pl.when(me == place)
            def _(place=place):
                gather_blocks(app, layer, place)

        updated = hid[app] + mm(wo_t[layer], att[app])
        upd[app] = updated
        unit, _ = normalise(updated)
        second = (unit * twice(norms[layer, 2]) + twice(norms[layer, 3])).astype(BF16)
        nrm2[app] = second

        @pl.when(app == 0)
        def _():
            each(reach_a, reach_c, pass_group)
            each_other_z(reach_b, reach_d, forward_group)
            each(reach_a, reach_b, take_group)
            unpack(reach_a, reach_b)
            hidden_weights(0)

        @pl.when(app == 1)
        def _():
            each(reach_c, reach_d, take_group)
            unpack(reach_c, reach_d)
            hidden_weights(1)

        before = mm(wup_t[layer], nrm2[app]) + twice(bup[layer])
        squared = before * before
        turned = jnp.tanh(before * (GELU_A + (GELU_A * GELU_B) * squared))
        risen = 0.5 * (1.0 + turned)
        act[app] = (before * risen).astype(BF16)
        gp[app] = risen + before * (1.0 - turned * turned) * (
            0.5 * GELU_A + (1.5 * GELU_A * GELU_B) * squared
        )
        result = upd[app] + mm(wd_t[layer], act[app])
        again = jnp.where((layer == LAYERS - 1) & (app < APPS - 1), 1.0, 0.0)
        hid[app + 1] = result + again * emb[...]
        return carry

    lax.fori_loop(0, APPS, forward, 0)
    states[...] = jnp.transpose(hid[APPS]).astype(BF16)

    for w in waves:
        each_other_z(0, zs, lambda z, w=w: weights_z(my_z, z, w).wait_send())
        each_other_z(0, zs, lambda z, w=w: weights_plane_out(z, 1, w).wait_send())
        for step in (2, 3):
            each(0, zs, lambda z, step=step, w=w: weights_plane_out(z, step, w).wait_send())
        each_other_z(0, zs, lambda z, w=w: weights_core(2 * z + my_x, my_c, w).wait_send())
        each(0, zs, lambda z, w=w: weights_core(2 * z + 1 - my_x, my_c, w).wait_send())
    for step in range(1, SEQ):

        @pl.when(me + step < SEQ)
        def _(step=step):
            points_copy(me, me + step).wait_send()


    def normed_sent(app):
        @pl.when(my_c == 0)
        def _():
            normed_copy(app, me, me + 1, 0).wait_send()

        @pl.when(my_y == 0)
        def _():
            normed_copy(app, me, me + 2, 1).wait_send()

        @pl.when(my_y == 1)
        def _():
            normed_copy(app, my_c, my_y * 2 + 1 - my_c, 2).wait_send()

    each(1, APPS, normed_sent)
    flat[:, pl.ds(plan.used, plan.total - plan.used), :] = jnp.zeros(
        (2, plan.total - plan.used, 128), F32
    )

    from_core, from_plane, from_z = ref.from_core, ref.from_plane, ref.from_z
    last, summed = ref.last, ref.summed

    def grads_core(group, w):
        pair = pl.ds(2 * group, 2)
        return remote(
            gathered.at[pair, 1 - my_c, :, w], from_core.at[pair, :, w],
            ref.send_gc.at[group, w], ref.recv_gc.at[group, w], sibling,
        )

    def grads_plane(group, step, w):
        x, y, device = in_plane(step)
        return remote(
            gathered.at[2 * group + x, my_c, y, w], from_plane.at[group, here, w],
            ref.send_gp.at[group, step, w], ref.recv_gp.at[group, here, w], device,
        )

    def grads_plane_in(group, step, w):
        x, y, device = in_plane(step)
        place = x * 2 + y
        return place, remote(
            gathered.at[2 * group + my_x, my_c, my_y, w], from_plane.at[group, place, w],
            ref.send_gp.at[group, step, w], ref.recv_gp.at[group, place, w], device,
        )

    def grads_z(source_z, target_z, w):
        return remote(
            gathered.at[2 * target_z + my_x, my_c, my_y, w], from_z.at[source_z, w],
            ref.send_gz.at[target_z, w], ref.recv_gz.at[source_z, w],
            {"dp": 2 * target_z + my_x},
        )

    def round_group(low, high):
        def body(group):
            for w in waves:
                for h in range(2):
                    for x in range(2):
                        for r in range(2):
                            start = (2 * group + x) * plan.flat + (2 * r + w) * quarter
                            gathered[2 * group + x, h, r, w] = flat[
                                h, pl.ds(start, quarter), :
                            ].astype(BF16)
                grads_core(group, w).start()

        each(low, high, body)

    def plane_group(low, high):
        def body(group):
            for w in waves:
                grads_core(group, w).wait()
                for step in (3, 2, 1, 0):
                    x, y, _ = in_plane(step)
                    share = 2 * group + x
                    gathered[share, my_c, y, w] = (
                        gathered[share, my_c, y, w].astype(F32) + from_core[share, y, w].astype(F32)
                    ).astype(BF16)
                    if step:
                        grads_plane(group, step, w).start()

        each(low, high, body)

    def rise_group(low, high):
        def body(group):
            for w in waves:
                value = gathered[2 * group + my_x, my_c, my_y, w].astype(F32)
                for step in (1, 2, 3):
                    place, arrival = grads_plane_in(group, step, w)
                    arrival.wait_recv()
                    value = value + from_plane[group, place, w].astype(F32)
                gathered[2 * group + my_x, my_c, my_y, w] = value.astype(BF16)

                @pl.when(group != my_z)
                def _(w=w):
                    grads_z(my_z, group, w).start()

                @pl.when(group == my_z)
                def _(w=w, value=value):
                    last[w] = value

        each(low, high, body)

    first_low, first_from, first_places, first_rise, first_levels, first_sum = (
        ref.first_low, ref.first_from, ref.first_places, ref.first_rise, ref.first_levels, ref.first_sum,
    )

    def first_core():
        return remote(
            first_low.at[1 - my_c], first_from, ref.send_f.at[0], ref.recv_fc.at[0], sibling
        )

    def first_plane(step):
        _, _, device = in_plane(step)
        return remote(
            first_low.at[my_c], first_places.at[here],
            ref.send_f.at[step], ref.recv_fp.at[here], device,
        )

    def first_plane_in(step):
        x, y, device = in_plane(step)
        place = x * 2 + y
        return place, remote(
            first_low.at[my_c], first_places.at[place],
            ref.send_f.at[step], ref.recv_fp.at[place], device,
        )

    def first_z(b, source):
        return remote(
            first_rise.at[b], first_levels.at[source], ref.send_f.at[5 + b],
            ref.recv_fz.at[source], {"dp": 2 * plan.late[b][0] + my_x},
        )

    def first_share(column):
        piece = first_sum.at[column]
        return remote(piece, piece, ref.send_f.at[4], ref.recv_fs.at[0], sibling)

    def to_first_x(body):
        @pl.when(my_x == 0)
        def _():
            body(1)

        @pl.when(my_x == 1)
        def _():
            body(2)
            body(3)

    def share_sum(kind, w, column, half, device):
        piece = summed.at[column, half, w]
        return remote(
            piece, piece, ref.send_gs.at[kind, w], ref.recv_gs.at[kind, w], device
        )

    def collect(low, high):
        def when_mine(group):
            @pl.when(group == my_z)
            def _():
                for w in waves:

                    def body(z, w=w):
                        grads_z(z, my_z, w).wait_recv()
                        last[w] += from_z[z, w].astype(F32)

                    each_other_z(0, zs, body)
                    summed[my_c, my_y, w] = last[w].astype(BF16)
                    share_sum(1, w, my_c, my_y, across).start()
                    share_sum(0, w, my_c, my_y, sibling).start()

        each(low, high, when_mine)

    def first_group(row):
        return min(zs, -(-row // (2 * plan.flat)))

    group_a = first_group(plan.base(1) + plan.mixer)
    group_b = first_group(plan.base(0) + plan.mixer)
    group_e = plan.settled

    def accumulate(app, layer, offset, stride, value, again=False):
        start = plan.base(0) + layer * plan.block + offset
        count = value.shape[0]
        for h in range(2):
            place = (h, pl.ds(start, count, stride=stride), slice(None))
            part = value[:, 128 * h : 128 * (h + 1)]
            kept = flat[place]
            flat[place] = part + (kept if again else jnp.where(app < LAYERS, kept, 0.0))

    part_q, held = emb, hid.at[APPS]

    def soften_back(app, keys, diagonal):
        for head in range(HEADS):
            scores = mm(kv[app, keys, :width], qmask[head]) * exp_scale
            weight = jnp.exp2(scores - lse[app, head : head + 1])
            if diagonal:
                weight = mask_last(weight, 0.0)
            ps[head, keys] = weight.astype(BF16)
            grad = mm(kv[app, keys, width:], domask[head])
            ds[head, keys] = (weight * (grad - total[head : head + 1])).astype(BF16)

    def heads_back(app, keys, own, added):
        for head in range(HEADS):
            lanes = slice(head * head_width, (head + 1) * head_width)
            key_lanes = slice(width + head * head_width, width + (head + 1) * head_width)
            value_lanes = slice(2 * width + head * head_width, 2 * width + (head + 1) * head_width)
            dqkv[key_lanes, keys] = (
                mm_nt(qsave[app, lanes], ds[head, keys]) * score_scale
            ).astype(BF16)
            dqkv[value_lanes, keys] = mm_nt(grad_low[lanes], ps[head, keys]).astype(BF16)
            part = mm(kt[app, lanes, keys], ds[head, keys])
            if own is None:
                part_q[lanes] = part
            else:
                part = part + part_q[lanes] if added else part
                dqkv[lanes, own] = (part * score_scale).astype(BF16)

    def span_of(low, high):
        return slice(low * rows, high * rows)

    def normed_back(layer, first, block):
        return mm(wqkv[layer, :, first:], dqkv[first:, span_of(block, block + 1)])

    def weights_back(app, layer, first, block, again):
        grads = mm_nt(nrm[app, block], dqkv[first:, span_of(block, block + 1)])
        for j in range(first // width, 3):
            accumulate(
                app, layer, 4 + j, 3, grads[:, width * j - first : width * (j + 1) - first],
                again=j > 0 and again,
            )

    def attend_back(app, layer, place):
        start = place // 2 * 2
        if start:
            kept, passed = place % 2, 1 - place % 2
            soften_back(app, span_of(0, start), False)
            heads_back(app, span_of(0, start), None, False)
            vt[:, turn_of(app)] = normed_back(layer, width, passed).astype(BF16)
            merge_copy(app).start()
            held[...] = normed_back(layer, width, kept)
            weights_back(app, layer, width, passed, False)
            weights_back(app, layer, width, kept, True)
        soften_back(app, span_of(start, place + 1), True)
        if start:
            merge_copy(app).wait_recv()
            nrm[app, kept] = (held[...] + merge[app].astype(F32)).astype(BF16)
            grad_copy(app, kept, kept, 2).start()
        heads_back(app, span_of(start, place + 1), span_of(place, place + 1), bool(start))
        if place % 2:
            merge[app] = normed_back(layer, width, place - 1).astype(BF16)
            near_copy(app, place - 1).start()
            weights_back(app, layer, width, place - 1, bool(start))
        gin[...] = normed_back(layer, 0, place)
        weights_back(app, layer, 0, place, bool(start) or place % 2 == 1)

    def flush_norms(layer):
        start = plan.base(0) + layer * plan.block
        for h in range(2):
            for j in range(4):
                flat[h, pl.ds(start + j, 1), :] = jnp.sum(
                    jnp.transpose(gnorm[layer, j, 128 * h : 128 * (h + 1)]), axis=0, keepdims=True
                )

    def backward(order, carry):
        app = APPS - 1 - order
        layer = lax.rem(app, LAYERS)

        @pl.when((app == 0) & (my_y == 1))
        def _():
            plane_group(group_e, group_a)

        out_low = gbuf[...].astype(BF16)
        accumulate(app, layer, plan.mixer + hidden + parts, 1, mm_nt(act[app], out_low))
        pre_low = (mm(wd[layer], out_low) * gp[app]).astype(BF16)
        act[app] = pre_low
        for j in range(parts):
            part = act[app, width * j : width * (j + 1)]
            accumulate(app, layer, plan.mixer + j, parts, mm_nt(nrm2[app], part))
            accumulate(app, layer, plan.mixer + hidden + j, 1, mm_nt(ones, part)[:1])

        @pl.when(app == 1)
        def _():
            round_group(group_a, zs)

        @pl.when(app == 0)
        def _():
            round_group(group_b, group_e)

        grad_second = mm(wup[layer], act[app])
        unit, scale = normalise(upd[app])
        gnorm[layer, 2] += halves(grad_second * unit)
        gnorm[layer, 3] += halves(grad_second)
        grad_updated = gbuf[...] + normalise_back(grad_second, unit, scale, twice(norms[layer, 2]))
        gbuf[...] = grad_updated
        branch_low = grad_updated.astype(BF16)
        accumulate(app, layer, 4 + 3 * width, 1, mm_nt(att[app], branch_low))
        grad_att = mm(wo[layer], branch_low).astype(BF16)
        grad_low[...] = grad_att
        for head in range(HEADS):
            lanes = slice(head * head_width, (head + 1) * head_width)
            domask[head, lanes] = grad_att[lanes]
            qmask[head, lanes] = qsave[app, lanes]
            total[head : head + 1] = jnp.sum(
                osave[app, lanes] * grad_att[lanes].astype(F32), axis=0, keepdims=True
            )

        @pl.when(app == 1)
        def _():
            plane_group(group_a, zs)

        @pl.when(app == 0)
        def _():
            rise_group(group_a, zs)
            plane_group(group_b, group_e)

        for place in range(SEQ):

            @pl.when(me == place)
            def _(place=place):
                attend_back(app, layer, place)

        @pl.when(app == 0)
        def _():
            round_group(0, group_b)
            plane_group(0, group_b)
            rise_group(group_e, group_a)
            rise_group(group_b, group_e)

        @pl.when(app == 1)
        def _():
            round_group(group_e, group_a)

        @pl.when((app == 1) & (my_y == 0))
        def _():
            plane_group(group_e, group_a)

        def arrive(source):
            grad_arrival(app, source).wait_recv()
            gin[...] += nrm[app, source].astype(F32)

        @pl.when(my_c == 0)
        def _():
            arrive(me + 1)

        @pl.when(my_y == 0)
        def _():
            arrive(me + 2)

        grad_normed = gin[...]
        unit, scale = normalise(hid[app])
        gnorm[layer, 0] += halves(grad_normed * unit)
        gnorm[layer, 1] += halves(grad_normed)
        grad_in = gbuf[...] + normalise_back(grad_normed, unit, scale, twice(norms[layer, 0]))
        gbuf[...] = grad_in
        first = jnp.where(layer == 0, 1.0, 0.0)
        gemb[...] += first * grad_in

        @pl.when(app < LAYERS)
        def _():
            flush_norms(layer)

        return carry

    lax.fori_loop(0, APPS, backward, 0)
    embed_low = gemb[...].astype(BF16)
    grad_in_rows = mm_nt(masked_all[me], embed_low)
    grad_bias_rows = mm_nt(ones, embed_low)
    for h in range(2):
        lanes = slice(128 * h, 128 * (h + 1))
        flat[h, : plan.depth] = grad_in_rows[: plan.depth, lanes]
        flat[h, plan.depth : plan.depth + 1] = grad_bias_rows[:1, lanes]
    for b, (group, _) in enumerate(plan.late):
        for h in range(2):
            first_low[h, b] = flat[h, pl.ds(2 * group * plan.flat, FIRST), :].astype(BF16)
    first_core().start()
    point_grad[...] = jnp.where(depth_mask, mm(rin[...], embed_low)[: plan.depth], 0.0)
    first_core().wait()
    first_low[my_c] = (first_low[my_c].astype(F32) + first_from[...].astype(F32)).astype(BF16)
    to_first_x(lambda step: first_plane(step).start())
    rise_group(0, group_b)

    @pl.when(my_x == 0)
    def _():
        first_places[here] = first_low[my_c]
        for step in (1, 2, 3):
            place, arrival = first_plane_in(step)
            arrival.wait_recv()
        first_rise[...] = sum(first_places[place].astype(F32) for place in range(4)).astype(BF16)

        for b, (group, _) in enumerate(plan.late):

            @pl.when(my_z != group)
            def _(b=b):
                first_z(b, my_z).start()

    collect(0, zs)
    for b, (group, _) in enumerate(plan.late):

        @pl.when(owner == 2 * group)
        def _(b=b):
            first_levels[my_z] = first_rise[b]
            each_other_z(0, zs, lambda z: first_z(b, z).wait_recv())
            first_sum[my_c] = sum(first_levels[z].astype(F32) for z in range(zs)).astype(BF16)
            first_share(my_c).start()

    for w in waves:
        share_sum(1, w, my_c, 1 - my_y, across).wait_recv()
        share_sum(2, w, my_c, 1 - my_y, sibling).start()
    for w in waves:
        share_sum(0, w, 1 - my_c, my_y, sibling).wait_recv()
    for w in waves:
        share_sum(2, w, 1 - my_c, 1 - my_y, sibling).wait_recv()
    for h in range(2):
        for r, w, start in quarters:
            count = min(quarter, plan.flat - start)
            if count > 0:
                flat[0, pl.ds(2 * start + h, count, stride=2), :] = summed[h, r, w].astype(F32)[
                    :count
                ]
    for group, count in plan.late:

        @pl.when(owner == 2 * group)
        def _(count=count):
            first_share(1 - my_c).wait_recv()
            for h in range(2):
                flat[0, pl.ds(h, count, stride=2), :] = first_sum[h].astype(F32)[:count]

    gradients[...] = flat[0, : gradients.shape[0]].astype(BF16)

    to_first_x(lambda step: first_plane(step).wait_send())

    for b, (group, _) in enumerate(plan.late):

        @pl.when((my_x == 0) & (my_z != group))
        def _(b=b):
            first_z(b, my_z).wait_send()

        @pl.when(owner == 2 * group)
        def _():
            first_share(my_c).wait_send()

    for w in waves:
        for step in (1, 2, 3):
            each(0, zs, lambda z, step=step, w=w: grads_plane(z, step, w).wait_send())
        each_other_z(0, zs, lambda z, w=w: grads_z(my_z, z, w).wait_send())
        share_sum(0, w, my_c, my_y, sibling).wait_send()
        share_sum(1, w, my_c, my_y, across).wait_send()
        share_sum(2, w, my_c, 1 - my_y, sibling).wait_send()

    def finish(app):
        @pl.when(my_c == 1)
        def _():
            near_copy(app, me - 1).wait_send()

        @pl.when(my_y == 1)
        def _():
            merge_copy(app).wait_send()
            grad_copy(app, my_c, my_c, 2).wait_send()

    each(0, APPS, finish)


def update_kernel(
    summed, weights, momenta, averages, states, point_grad,
    grad_out, fresh_out, momentum_out, mean_out, states_out, point_out,
):
    grad = summed[...].astype(F32)
    momentum = MOMENTUM * momenta[...] + grad
    fresh = weights[...] - RATE * (grad + MOMENTUM * momentum)
    grad_out[...] = grad
    momentum_out[...] = momentum
    fresh_out[...] = fresh
    mean_out[...] = AVERAGE_DECAY * averages[...] + (1.0 - AVERAGE_DECAY) * fresh

    @pl.when(pl.program_id(0) == 0)
    def _():
        states_out[...] = states[...]
        for row in range(point_grad.shape[0]):
            point_out[row] = point_grad[row : row + 1]


def shards(points, counts, cotangent, weights, momenta, averages):
    rows, depth = points.shape[1:]
    width = cotangent.shape[2]
    share = weights.shape[0]
    plan = Plan(rows, depth, width, share, lax.axis_size("dp"), lax.axis_size("seq"))
    hidden, dp_count, zs, quarter = plan.hidden, plan.dp, plan.zs, plan.quarter
    vmem = pl.BlockSpec(memory_space=pltpu.VMEM)
    smem = pl.BlockSpec(memory_space=pltpu.SMEM)
    shape = jax.ShapeDtypeStruct
    lines = (share // 128, 128)
    outs = (shape((rows, width), BF16), shape((depth, rows), F32), shape(lines, BF16))
    low = lambda *dims: pltpu.VMEM(dims, BF16)
    full = lambda *dims: pltpu.VMEM(dims, F32)
    flags = lambda *dims: pltpu.SemaphoreType.DMA(dims)
    scratch = dict(
        gathered=low(dp_count, 2, 2, 2, quarter, 128),
        flat=full(2, plan.space, 128),
        rin=low(128, width),
        rit=low(width, 128),
        rbias=full(width, 128),
        norms=low(LAYERS, 4, width, 128),
        bup=low(LAYERS, hidden, 128),
        wqkv=low(LAYERS, width, 3 * width),
        wqkv_t=low(LAYERS, 3 * width, width),
        wo=low(LAYERS, width, width),
        wo_t=low(LAYERS, width, width),
        wup=low(LAYERS, width, hidden),
        wup_t=low(LAYERS, hidden, width),
        wd=low(LAYERS, hidden, width),
        wd_t=low(LAYERS, width, hidden),
        masked_all=low(SEQ, 128, rows),
        gnorm=full(LAYERS, 4, width, 128),
        from_core=low(dp_count, 2, 2, quarter, 128),
        from_plane=low(zs, 4, 2, quarter, 128),
        from_z=low(zs, 2, quarter, 128),
        last=full(2, quarter, 128),
        first_low=low(2, len(plan.late), FIRST, 128),
        first_from=low(len(plan.late), FIRST, 128),
        first_places=low(4, len(plan.late), FIRST, 128),
        first_rise=low(len(plan.late), FIRST, 128),
        first_levels=low(zs, FIRST, 128),
        first_sum=low(2, FIRST, 128),
        send_f=flags(5 + len(plan.late)),
        recv_fc=flags(1),
        recv_fp=flags(4),
        recv_fz=flags(zs),
        recv_fs=flags(1),
        summed=low(2, 2, 2, quarter, 128),
        hid=full(APPS + 1, width, rows),
        nrm=low(APPS, SEQ, width, rows),
        qsave=low(APPS, width, rows),
        kv=low(APPS, SEQ * rows, 2 * width),
        kt=low(APPS, width, SEQ * rows),
        vt=low(width, SEQ * rows),
        att=low(APPS, width, rows),
        osave=full(APPS, width, rows),
        lse=full(APPS, HEADS, rows),
        upd=full(APPS, width, rows),
        nrm2=low(APPS, width, rows),
        gp=full(APPS, hidden, rows),
        act=low(APPS, hidden, rows),
        emb=full(width, rows),
        qmask=low(HEADS, width, rows),
        domask=low(HEADS, width, rows),
        ps=low(HEADS, SEQ * rows, rows),
        ds=low(HEADS, SEQ * rows, rows),
        dqkv=low(3 * width, SEQ * rows),
        grad_low=low(width, rows),
        peak=full(HEADS, rows),
        total=full(HEADS, rows),
        far_peak=full(HEADS, rows),
        far_total=full(HEADS, rows),
        gbuf=full(width, rows),
        gemb=full(width, rows),
        gin=full(width, rows),
        merge=low(APPS, width, rows),
        send_n=flags(APPS, 3),
        recv_n=flags(APPS, SEQ),
        send_g=flags(APPS, 3),
        recv_g=flags(APPS, SEQ),
        recv_m=flags(APPS),
        send_p=flags(SEQ),
        recv_p=flags(SEQ),
        send_wz=flags(zs, 2),
        recv_wz=flags(zs, 2),
        send_wp=flags(zs, 4, 2),
        recv_wp=flags(zs, 4, 2),
        send_wc=flags(dp_count, 2),
        recv_wc=flags(dp_count, 2),
        send_gc=flags(zs, 2),
        recv_gc=flags(zs, 2),
        send_gp=flags(zs, 4, 2),
        recv_gp=flags(zs, 4, 2),
        send_gz=flags(zs, 2),
        recv_gz=flags(zs, 2),
        send_gs=flags(3, 2),
        recv_gs=flags(3, 2),
    )
    mine = weights.reshape(lines)
    states, point_grad, summed = pl.pallas_call(
        functools.partial(whole_kernel, plan, tuple(scratch)),
        out_shape=outs,
        in_specs=[vmem, smem, vmem, vmem],
        out_specs=(vmem,) * len(outs),
        scratch_shapes=list(scratch.values()),
        compiler_params=pltpu.CompilerParams(
            collective_id=0, has_side_effects=True, vmem_limit_bytes=63 * 1024 * 1024
        ),
    )(points[0].T, counts, cotangent[0], mine)
    vector = shape(lines, F32)
    step_rows = min(776, lines[0])
    line_block = pl.BlockSpec((step_rows, 128), lambda i: (i, 0))
    states_block = pl.BlockSpec((rows, width), lambda i: (0, 0))
    point_block = pl.BlockSpec((depth, rows), lambda i: (0, 0))
    grad, fresh, momentum, mean, states, point_grad = pl.pallas_call(
        update_kernel,
        grid=(-(-lines[0] // step_rows),),
        out_shape=(
            vector, vector, vector, vector, shape((rows, width), BF16), shape((depth, 1, rows), F32),
        ),
        in_specs=[line_block] * 4 + [states_block, point_block],
        out_specs=(
            line_block, line_block, line_block, line_block, states_block,
            pl.BlockSpec((depth, 1, rows), lambda i: (0, 0, 0)),
        ),
        compiler_params=pltpu.CompilerParams(vmem_limit_bytes=63 * 1024 * 1024),
    )(summed, mine, momenta.reshape(lines), averages.reshape(lines), states, point_grad)
    return (
        states[None], jnp.transpose(point_grad, (1, 2, 0)),
        *(v.reshape(-1) for v in (grad, fresh, momentum, mean)),
    )


def solution(mesh):
    placed = (P("dp", "seq", None), P("dp"), P("dp", "seq", None), P("dp"), P("dp"), P("dp"))
    return jax.shard_map(
        shards,
        mesh=mesh,
        in_specs=placed,
        out_specs=(P("dp", "seq", None), P("dp", "seq", None), P("dp"), P("dp"), P("dp"), P("dp")),
        check_vma=False,
    )
```
